128 devices in a mesh: down: 8 (over x_hi, z), cross: 16 (over y, x_lo, core).
Axes of the slice: x: 4 (x_hi: 2, x_lo: 2; x = x_hi * 2 + x_lo), y: 4, z: 4, core: 2. Of those that a mesh axis runs over, the one named last changes fastest.
Arguments:
- right_side: float32 [3, 35, 32, 8192], P(None, None, 'down', 'cross'), may hold values from -48 to 48
- stiffness: float32 [32, 8192], P('down', 'cross'), may hold values from 1 to 8
- coefficients: float32 [5, 32, 8192], P(None, 'down', 'cross'), may hold values from -0.73 to 3.001, as said below
- stencil_weights: float32 [13], replicated, may hold values from 0.05 to 0.3
Outputs:
- solution_field: float32 [3, 35, 32, 8192], P(None, None, 'down', 'cross')
- residual: float32 [3, 35, 32, 8192], P(None, None, 'down', 'cross')
The draws below stay inside these ranges and needn't reach their ends.
Inputs may be any that keep to these rules, and one draw needn't show every extreme that they name: `coefficients`: entry 0 at every cell lies between 0.5 and 3 and exceeds the sum of the magnitudes of entries 1 to 4 at that cell.
All inputs are finite; a program needn't handle non-finite values.
Results may differ from the reference program's by a relative error of at most 0.04.
Values sent between devices are 32-bit elements; how exact they have to be, the bound alone decides.
No kernel may reach another device: no remote copies, remote signals or barrier semaphores. Data moves between devices by JAX's collectives and lax.ppermute only.
A program may use at most 128 MiB of HBM per device.

```python
import math
import jax
import jax.numpy as jnp
from jax import lax

CZ = 32
COMPS = 3
VARS = 4
DEG = 3
MODES = 35
TERMS = 5
ITERS = 2
NX = 32
NY = 256


def draw_right_side(key, part):
    key = jax.random.fold_in(key, 11)
    shape = (COMPS, MODES, NX, NY * CZ)
    downslope = jnp.arange(NX, dtype=jnp.float32) / NX
    across = (jnp.arange(NY * CZ) // CZ).astype(jnp.float32) / NY
    scaling = 2.0 * (1.0 + 2.0 * downslope)[:, None] * (1.0 + across)[None, :]
    base_values = jnp.clip(jax.random.normal(key, shape, jnp.float32), -4.0, 4.0)
    return base_values * scaling


def draw_coefficients(key, part):
    key = jax.random.fold_in(key, 23)
    first_key, second_key = jax.random.split(key)
    mean_part = jnp.exp(jax.random.uniform(first_key, (1, NX, NY * CZ), jnp.float32, math.log(0.5), math.log(3.0)))
    ratios = jax.random.uniform(second_key, (VARS, NX, NY * CZ), jnp.float32, -0.24, 0.24)
    return jnp.concatenate([mean_part, mean_part * ratios], axis=0)


def level_of(stream_key, dims, shards, least, high):
    def one(axis_at, blocks):
        steps = jax.random.uniform(jax.random.fold_in(jax.random.fold_in(stream_key, 6), axis_at), (blocks,), jnp.float32, least / len(shards), high / len(shards))
        return jnp.repeat(jnp.exp(steps), dims[axis_at] // blocks).reshape((-1,) + (1,) * (len(dims) - axis_at - 1))

    factor_of = one(*shards[0])
    for cut in shards[1:]:
        factor_of = factor_of * one(*cut)
    return factor_of


def setup_inputs(seed: int = 0) -> dict:
    streams_of = jax.random.split(jax.random.key(seed), 5)
    return {
        "right_side": draw_right_side(jax.random.fold_in(streams_of[4], 71), 0),
        "stiffness": jnp.clip(jnp.exp(math.log(8.0) - 2.0794415 * jax.random.uniform(streams_of[1], (NX, NY * CZ), jnp.float32) ** level_of(streams_of[1], (NX, NY * CZ), ((0, 8), (1, 16)), -0.2, 0.2)), 1.0, 8.0),
        "coefficients": draw_coefficients(jax.random.fold_in(streams_of[4], 71), 0),
        "stencil_weights": jnp.clip(jnp.exp(jax.random.uniform(streams_of[3], (13,), jnp.float32, math.log(0.05), math.log(0.3))), 0.05, 0.3),
    }


def multi_indices(count_left, budget_left):
    if count_left == 0:
        return [()]
    return [(leading,) + remainder for leading in range(budget_left + 1) for remainder in multi_indices(count_left - 1, budget_left - leading)]

def chaos_matrices():
    picked = sorted(multi_indices(VARS, DEG), key=lambda multi_index: (sum(multi_index),) + tuple((-entry_value for entry_value in multi_index)))
    mode_count = len(picked)
    position = {multi_index: number for number, multi_index in enumerate(picked)}
    matrices = [[[0.0 for column_number in range(mode_count)] for row_number in range(mode_count)] for term_number in range(VARS + 1)]
    for row_number in range(mode_count):
        matrices[0][row_number][row_number] = 1.0
    for variable in range(VARS):
        for multi_index in picked:
            raised = list(multi_index)
            raised[variable] = raised[variable] + 1
            raised = tuple(raised)
            if raised in position:
                degree_here = multi_index[variable]
                entry_value = (degree_here + 1) / math.sqrt((2 * degree_here + 1) * (2 * degree_here + 3))
                matrices[variable + 1][position[multi_index]][position[raised]] = entry_value
                matrices[variable + 1][position[raised]][position[multi_index]] = entry_value
    return jnp.asarray(matrices, dtype=jnp.float32)

def offset_table():
    table = []
    for shift_x in (-1, 0, 1):
        for shift_y in (-1, 0, 1):
            for shift_z in (-1, 0, 1):
                linear = 9 * (shift_x + 1) + 3 * (shift_y + 1) + (shift_z + 1)
                if linear != 13:
                    table.append((shift_x, shift_y, shift_z, min(linear, 26 - linear)))
    return table

def operate_component(vector, stiffness, coefficients, stencil_weights, chaos_mats):
    widths = ((0, 0), (1, 1), (1, 1), (1, 1))
    padded_vec = jnp.pad(vector, widths)
    padded_coef = jnp.pad(coefficients, widths)
    result = stiffness * vector
    for term_index in range(TERMS):
        own_coef = coefficients[term_index]
        diagonal = jnp.zeros(own_coef.shape, own_coef.dtype)
        totals = jnp.zeros(vector.shape, vector.dtype)
        for shift_x, shift_y, shift_z, weight_slot in offset_table():
            near_coef = padded_coef[term_index, 1 + shift_x:1 + shift_x + NX, 1 + shift_y:1 + shift_y + NY, 1 + shift_z:1 + shift_z + CZ]
            near_vec = padded_vec[:, 1 + shift_x:1 + shift_x + NX, 1 + shift_y:1 + shift_y + NY, 1 + shift_z:1 + shift_z + CZ]
            edge_term = stencil_weights[weight_slot] * (own_coef + near_coef) * 0.5
            diagonal = diagonal + edge_term
            totals = totals + edge_term * near_vec
        term_field = diagonal * vector - totals
        if term_index == 0:
            result = result + term_field
        else:
            result = result + jnp.einsum('mn,nxyz->mxyz', chaos_mats[term_index], term_field, precision=lax.Precision.HIGHEST)
    return result

def reference(right_side, stiffness, coefficients, stencil_weights):
    chaos_mats = chaos_matrices().astype(right_side.dtype)
    grid_coef = coefficients.reshape(TERMS, NX, NY, CZ)
    grid_stiff = stiffness.reshape(NX, NY, CZ)

    def operate(vector):
        shaped = vector.reshape(COMPS, MODES, NX, NY, CZ)
        mapped = lax.map(lambda single: operate_component(single, grid_stiff, grid_coef, stencil_weights, chaos_mats), shaped)
        return mapped.reshape(vector.shape)
    solution_field = jnp.zeros_like(right_side)
    residual = right_side
    direction = right_side
    norm_now = jnp.sum(residual * residual)
    for iteration in range(ITERS):
        image_field = operate(direction)
        step_size = norm_now / jnp.sum(direction * image_field)
        solution_field = solution_field + step_size * direction
        residual = residual - step_size * image_field
        norm_next = jnp.sum(residual * residual)
        direction = residual + norm_next / norm_now * direction
        norm_now = norm_next
    return (solution_field, residual)
```

```python
import functools
import math

import jax
import jax.numpy as jnp
import numpy as np
from jax import lax
from jax.experimental import pallas as pl
from jax.experimental.pallas import tpu as pltpu
from jax.sharding import PartitionSpec as P

CZ = 32
VARS = 4
DEG = 3
TERMS = 5
COMPS = 3
MODES = 35
FIELDS = COMPS * MODES
STIFF = FIELDS + TERMS
ROWS = 4
LANES = 128
WIDE = 64


def multi_indices(count_left, budget_left):
    if count_left == 0:
        return [()]
    return [
        (leading,) + remainder
        for leading in range(budget_left + 1)
        for remainder in multi_indices(count_left - 1, budget_left - leading)
    ]


def chaos_terms():
    picked = sorted(
        multi_indices(VARS, DEG),
        key=lambda multi_index: (sum(multi_index),)
        + tuple((-entry_value for entry_value in multi_index)),
    )
    position = {multi_index: number for number, multi_index in enumerate(picked)}
    terms = [[] for mode in picked]
    for variable in range(VARS):
        for multi_index in picked:
            raised = list(multi_index)
            raised[variable] += 1
            raised = tuple(raised)
            if raised in position:
                degree = multi_index[variable]
                here, there = position[multi_index], position[raised]
                terms[here].append((variable, degree, there))
                terms[there].append((variable, degree, here))
    values = [(n + 1) / math.sqrt((2 * n + 1) * (2 * n + 3)) for n in range(DEG)]
    return terms, values


CHAOS, CHAOS_VALUES = chaos_terms()
TABLE = 1 + VARS * DEG


def tap_slots():
    own = np.arange(LANES)
    place = np.concatenate([own, own[:WIDE] + LANES, own[WIDE:] - LANES])
    y_in, z_in = place // CZ, place % CZ
    y_out, z_out = own // CZ, own % CZ
    dy = y_in[:, None] - y_out[None, :]
    dz = z_in[:, None] - z_out[None, :]
    near = (abs(dy) <= 1) & (abs(dz) <= 1)
    parts = []
    for dx in (0, 1, -1):
        linear = 9 * (dx + 1) + 3 * (dy + 1) + (dz + 1)
        slot = np.minimum(linear, 26 - linear)
        parts.append(np.where(near, slot, 13))
    return np.concatenate(parts, axis=1).astype(np.int32)


SLOTS = tap_slots()


def stencil_matrix(weights):
    slots = jnp.asarray(SLOTS)
    full = jnp.zeros(slots.shape, jnp.float32)
    for number in range(13):
        full = jnp.where(slots == number, 0.5 * weights[number], full)
    high = lax.reduce_precision(full, 8, 7)
    low = (full - high).astype(jnp.bfloat16)
    high = high.astype(jnp.bfloat16)
    return jnp.concatenate([high, high, low], axis=0)


def mix(table, load, mode, total):
    for variable, degree, other in CHAOS[mode]:
        total = total + table[1 + variable * DEG + degree] * load(other)
    return total


def window(high, low, now, chunks):
    after, before = (now + 1) % chunks, (now + chunks - 1) % chunks
    shape = high.shape[1:]
    left = lax.broadcasted_iota(jnp.int32, shape, 1) < WIDE
    own_high, own_low = high[now], low[now]
    mix_high = jnp.where(left, high[after], high[before])
    mix_low = jnp.where(left, low[after], low[before])
    return jnp.concatenate([own_high, mix_high, own_low, mix_low, own_high, mix_high], axis=1)


def stencil(high, low, now, chunks, matrix, out):
    parts = jnp.dot(
        window(high, low, now, chunks), matrix[...], preferred_element_type=jnp.float32
    )
    shape = out.shape
    centre = parts[:, :LANES].reshape(shape)
    ahead = parts[:, LANES : 2 * LANES].reshape(shape)
    behind = parts[:, 2 * LANES :].reshape(shape)
    out[...] = centre + pltpu.roll(ahead, 7, 1) + pltpu.roll(behind, 1, 1)


def split(value, high, low, now):
    value = value.reshape(high.shape[1:])
    top = value.astype(jnp.bfloat16)
    high[now] = top
    low[now] = (value - top.astype(jnp.float32)).astype(jnp.bfloat16)


def operator_kernel(
    chunks,
    own_ref, extra_ref, left_ref, right_ref, upper_ref, lower_ref, matrix_ref, sum_ref,
    image_ref, second_ref, sums_ref,
    field, field_high, field_low, grown, grown_high, grown_low,
    first_near, second_near, image, image_high, image_low, coef_table, diag_table,
):
    edge = chunks - 1
    for k in range(edge):
        lanes = pl.ds(k * LANES, LANES)
        field[k, :FIELDS, 0:ROWS, :] = own_ref[:, :, lanes]
        field[k, FIELDS : STIFF + 1, 0:ROWS, :] = extra_ref[:, :, lanes]
    field[edge, : STIFF + 1, 0:ROWS, :] = jnp.concatenate([right_ref[...], left_ref[...]], axis=2)
    for k in range(chunks):
        lanes = pl.ds(k * LANES, LANES)
        field[k, : STIFF + 1, ROWS : ROWS + 2, :] = upper_ref[:, :, lanes]
        field[k, : STIFF + 1, ROWS + 2 : ROWS + 4, :] = lower_ref[:, :, lanes]
        field[k, STIFF + 1] = jnp.zeros((8, LANES), jnp.float32)
        image[k, FIELDS] = jnp.zeros((8, LANES), jnp.float32)
    grown[FIELDS] = jnp.zeros((8, LANES), jnp.float32)

    def fill(table, k, values):
        table[k, 0] = values[0]
        for variable in range(VARS):
            for degree in range(DEG):
                table[k, 1 + variable * DEG + degree] = values[1 + variable] * CHAOS_VALUES[degree]

    def load_table(table, k):
        return [table[k, entry] for entry in range(TABLE)]

    @pl.loop(0, chunks)
    def grow(k):
        fill(coef_table, k, [field[k, FIELDS + term] for term in range(TERMS)])
        table = load_table(coef_table, k)

        @pl.loop(0, COMPS)
        def each(comp):
            base = comp * MODES
            for mode in range(MODES):
                load = lambda other: field[k, base + other]
                grown[base + mode] = mix(table, load, mode, table[0] * load(mode))

        split(grown[...], grown_high, grown_low, k)
        split(field[k], field_high, field_low, k)

    @pl.loop(0, chunks)
    def first(k):
        stencil(field_high, field_low, k, chunks, matrix_ref, first_near)
        stencil(grown_high, grown_low, k, chunks, matrix_ref, second_near)
        weight_sum = sum_ref[0]
        fill(
            diag_table,
            k,
            [
                field[k, FIELDS + term] * weight_sum + first_near[FIELDS + term]
                for term in range(TERMS)
            ],
        )
        coef = load_table(coef_table, k)
        diag = load_table(diag_table, k)
        stiff = field[k, STIFF]
        inside = stiff > 0.0

        @pl.loop(0, COMPS)
        def each(comp):
            base = comp * MODES
            for mode in range(MODES):
                load = lambda other: field[k, base + other]
                near = lambda other: first_near[base + other]
                value = mix(diag, load, mode, (stiff + diag[0]) * load(mode))
                value = value - mix(coef, near, mode, coef[0] * near(mode) + second_near[base + mode])
                image[k, base + mode] = jnp.where(inside, value, 0.0)

    @pl.loop(0, chunks)
    def regrow(k):
        table = load_table(coef_table, k)

        @pl.loop(0, COMPS)
        def each(comp):
            base = comp * MODES
            for mode in range(MODES):
                load = lambda other: image[k, base + other]
                grown[base + mode] = mix(table, load, mode, table[0] * load(mode))

        split(grown[...], grown_high, grown_low, k)
        split(image[k], image_high, image_low, k)

    third_near = first_near.at[pl.ds(0, FIELDS + 1)]
    zero = jnp.zeros((8, LANES), jnp.float32)

    def second(k, sums):
        stencil(image_high, image_low, k, chunks, matrix_ref, third_near)
        stencil(grown_high, grown_low, k, chunks, matrix_ref, second_near)
        coef = load_table(coef_table, k)
        diag = load_table(diag_table, k)
        stiff = field[k, STIFF]
        lanes = pl.ds(pl.multiple_of(k * LANES, LANES), LANES)

        def each(comp, sums):
            rr, rq, qq, qz = sums
            base = comp * MODES
            for mode in range(MODES):
                load = lambda other: image[k, base + other]
                near = lambda other: third_near[base + other]
                start, here = field[k, base + mode], load(mode)
                value = mix(diag, load, mode, (stiff + diag[0]) * here)
                value = value - mix(coef, near, mode, coef[0] * near(mode) + second_near[base + mode])
                image_ref[base + mode, :, lanes] = here[:ROWS]
                second_ref[base + mode, :, lanes] = value[:ROWS]
                rr, rq, qq, qz = rr + start * start, rq + start * here, qq + here * here, qz + here * value
            return rr, rq, qq, qz

        return lax.fori_loop(0, COMPS, each, sums)

    sums = lax.fori_loop(0, edge, second, (zero, zero, zero, zero))
    inner = lax.broadcasted_iota(jnp.int32, (8, LANES), 0) < ROWS
    lane = lax.broadcasted_iota(jnp.int32, sums_ref.shape, 1)
    row = jnp.zeros(sums_ref.shape, jnp.float32)
    for number, value in enumerate(sums):
        row = jnp.where(lane == number, jnp.sum(jnp.where(inner, value, 0.0)), row)
    sums_ref[...] = row


def finish_kernel(sums_ref, start_ref, image_ref, second_ref, field_ref, residual_ref):
    total = jnp.sum(sums_ref[...], axis=0, keepdims=True)
    lane = lax.broadcasted_iota(jnp.int32, total.shape, 1)
    rr, rq, qq, qz = [
        jnp.sum(jnp.where(lane == number, total, 0.0), axis=1, keepdims=True)[None]
        for number in range(4)
    ]
    step = rr / rq
    fresh = rr - 2.0 * step * rq + step * step * qq
    grow = 1.0 + fresh / rr
    curvature = grow * grow * rq - 2.0 * grow * step * qq + step * step * qz
    later = fresh / curvature
    both = step + later * grow
    cross = later * step
    start, image, second = start_ref[...], image_ref[...], second_ref[...]
    field_ref[...] = both * start - cross * image
    residual_ref[...] = start - both * image + cross * second


def shift(value, axis, by):
    size = lax.axis_size(axis)
    return lax.ppermute(value, axis, [(i, i + by) for i in range(size) if 0 <= i + by < size])


def per_device(right_side, stiffness, coefficients, stencil_weights):
    columns = right_side.shape[3]
    chunks = columns // LANES + 1
    devices = lax.axis_size("down") * lax.axis_size("cross")
    own = right_side.reshape(FIELDS, ROWS, columns)
    extra = jnp.concatenate([coefficients, stiffness[None]], axis=0)
    all_fields = jnp.concatenate([own, extra], axis=0)
    right = shift(all_fields[:, :, :WIDE], "cross", -1)
    left = shift(all_fields[:, :, columns - WIDE :], "cross", 1)
    wide = jnp.concatenate([all_fields, right, left], axis=2)
    upper = shift(wide[:, :2], "down", -1)
    lower = shift(wide[:, ROWS - 2 :], "down", 1)
    matrix = stencil_matrix(stencil_weights)
    weight_sum = jnp.sum(stencil_weights).reshape(1)
    vmem = pl.BlockSpec(memory_space=pltpu.VMEM)
    count = FIELDS + 1
    f32, bf16 = jnp.float32, jnp.bfloat16
    image, second, sums = pl.pallas_call(
        functools.partial(operator_kernel, chunks),
        out_shape=(
            jax.ShapeDtypeStruct(own.shape, f32),
            jax.ShapeDtypeStruct(own.shape, f32),
            jax.ShapeDtypeStruct((devices, LANES), f32),
        ),
        in_specs=[vmem] * 7 + [pl.BlockSpec(memory_space=pltpu.SMEM)],
        out_specs=(vmem, vmem, vmem),
        scratch_shapes=[
            pltpu.VMEM((chunks, STIFF + 2, 8, LANES), f32),
            pltpu.VMEM((chunks, (STIFF + 2) * 8, LANES), bf16),
            pltpu.VMEM((chunks, (STIFF + 2) * 8, LANES), bf16),
            pltpu.VMEM((count, 8, LANES), f32),
            pltpu.VMEM((chunks, count * 8, LANES), bf16),
            pltpu.VMEM((chunks, count * 8, LANES), bf16),
            pltpu.VMEM((STIFF + 2, 8, LANES), f32),
            pltpu.VMEM((count, 8, LANES), f32),
            pltpu.VMEM((chunks, count, 8, LANES), f32),
            pltpu.VMEM((chunks, count * 8, LANES), bf16),
            pltpu.VMEM((chunks, count * 8, LANES), bf16),
            pltpu.VMEM((chunks, TABLE, 8, LANES), f32),
            pltpu.VMEM((chunks, TABLE, 8, LANES), f32),
        ],
        compiler_params=pltpu.CompilerParams(vmem_limit_bytes=48 * 1024 * 1024),
        name="operator",
    )(own, extra, left, right, upper, lower, matrix, weight_sum)
    sums = lax.all_to_all(sums, ("down", "cross"), 0, 0, tiled=True)
    solution_field, residual = pl.pallas_call(
        finish_kernel,
        out_shape=(jax.ShapeDtypeStruct(own.shape, f32), jax.ShapeDtypeStruct(own.shape, f32)),
        in_specs=[vmem] * 4,
        out_specs=(vmem, vmem),
        compiler_params=pltpu.CompilerParams(vmem_limit_bytes=32 * 1024 * 1024),
        name="finish",
    )(sums, own, image, second)
    return solution_field.reshape(right_side.shape), residual.reshape(right_side.shape)


def solution(mesh):
    return jax.shard_map(
        per_device,
        mesh=mesh,
        in_specs=(
            P(None, None, "down", "cross"),
            P("down", "cross"),
            P(None, "down", "cross"),
            P(),
        ),
        out_specs=(P(None, None, "down", "cross"), P(None, None, "down", "cross")),
        check_vma=False,
    )
```

```python
import functools
import math

import jax
import jax.numpy as jnp
import numpy as np
from jax import lax
from jax.experimental import pallas as pl
from jax.experimental.pallas import tpu as pltpu
from jax.sharding import PartitionSpec as P

CZ = 32
VARS = 4
DEG = 3
TERMS = 5
COMPS = 3
MODES = 35
FIELDS = COMPS * MODES
STIFF = FIELDS + TERMS
ROWS = 4
LANES = 128
WIDE = 64


def multi_indices(count_left, budget_left):
    if count_left == 0:
        return [()]
    return [
        (leading,) + remainder
        for leading in range(budget_left + 1)
        for remainder in multi_indices(count_left - 1, budget_left - leading)
    ]


def chaos_terms():
    picked = sorted(
        multi_indices(VARS, DEG),
        key=lambda multi_index: (sum(multi_index),)
        + tuple((-entry_value for entry_value in multi_index)),
    )
    position = {multi_index: number for number, multi_index in enumerate(picked)}
    terms = [[] for mode in picked]
    for variable in range(VARS):
        for multi_index in picked:
            raised = list(multi_index)
            raised[variable] += 1
            raised = tuple(raised)
            if raised in position:
                degree = multi_index[variable]
                here, there = position[multi_index], position[raised]
                terms[here].append((variable, degree, there))
                terms[there].append((variable, degree, here))
    values = [(n + 1) / math.sqrt((2 * n + 1) * (2 * n + 3)) for n in range(DEG)]
    return terms, values


CHAOS, CHAOS_VALUES = chaos_terms()
TABLE = 1 + VARS * DEG


def tap_slots():
    own = np.arange(LANES)
    place = np.concatenate([own, own[:WIDE] + LANES, own[WIDE:] - LANES])
    y_in, z_in = place // CZ, place % CZ
    y_out, z_out = own // CZ, own % CZ
    dy = y_in[:, None] - y_out[None, :]
    dz = z_in[:, None] - z_out[None, :]
    near = (abs(dy) <= 1) & (abs(dz) <= 1)
    parts = []
    for dx in (0, 1, -1):
        linear = 9 * (dx + 1) + 3 * (dy + 1) + (dz + 1)
        slot = np.minimum(linear, 26 - linear)
        parts.append(np.where(near, slot, 13))
    return np.concatenate(parts, axis=1).astype(np.int32)


SLOTS = tap_slots()


def matrix_kernel(weights_ref, slots_ref, matrix_ref):
    slots = slots_ref[...]
    full = jnp.zeros(slots.shape, jnp.float32)
    for number in range(13):
        full = jnp.where(slots == number, 0.5 * weights_ref[number], full)
    high = full.astype(jnp.bfloat16)
    low = (full - high.astype(jnp.float32)).astype(jnp.bfloat16)
    rows = slots.shape[0]
    matrix_ref[:rows] = high
    matrix_ref[rows : 2 * rows] = high
    matrix_ref[2 * rows :] = low


def mix(table, load, mode, total):
    for variable, degree, other in CHAOS[mode]:
        total = total + table[1 + variable * DEG + degree] * load(other)
    return total


def window(high, low, now, chunks):
    after, before = (now + 1) % chunks, (now + chunks - 1) % chunks
    shape = high.shape[1:]
    left = lax.broadcasted_iota(jnp.int32, shape, 1) < WIDE
    own_high, own_low = high[now], low[now]
    mix_high = jnp.where(left, high[after], high[before])
    mix_low = jnp.where(left, low[after], low[before])
    return jnp.concatenate([own_high, mix_high, own_low, mix_low, own_high, mix_high], axis=1)


def stencil(high, low, now, chunks, matrix, out):
    parts = jnp.dot(
        window(high, low, now, chunks), matrix[...], preferred_element_type=jnp.float32
    )
    shape = out.shape
    centre = parts[:, :LANES].reshape(shape)
    ahead = parts[:, LANES : 2 * LANES].reshape(shape)
    behind = parts[:, 2 * LANES :].reshape(shape)
    out[...] = centre + pltpu.roll(ahead, 7, 1) + pltpu.roll(behind, 1, 1)


def split(value, high, low, now):
    value = value.reshape(high.shape[1:])
    top = value.astype(jnp.bfloat16)
    high[now] = top
    low[now] = (value - top.astype(jnp.float32)).astype(jnp.bfloat16)


def operator_kernel(
    chunks,
    own_ref, extra_ref, left_ref, right_ref, upper_ref, lower_ref, upper_corner_ref, lower_corner_ref,
    matrix_ref, weights_ref,
    image_ref, second_ref, sums_ref,
    field, field_high, field_low, grown, grown_high, grown_low,
    first_near, second_near, image, image_high, image_low, coef_table, diag_table,
):
    edge = chunks - 1
    for k in range(edge):
        lanes = pl.ds(k * LANES, LANES)
        field[k, :FIELDS, 0:ROWS, :] = own_ref[:, :, lanes]
        field[k, FIELDS : STIFF + 1, 0:ROWS, :] = extra_ref[:, :, lanes]
    field[edge, : STIFF + 1, 0:ROWS, :] = jnp.concatenate([right_ref[...], left_ref[...]], axis=2)
    for k in range(chunks):
        lanes = pl.ds(k * LANES if k < edge else 0, LANES)
        upper, lower = (upper_ref, lower_ref) if k < edge else (upper_corner_ref, lower_corner_ref)
        field[k, : STIFF + 1, ROWS : ROWS + 2, :] = upper[:, :, lanes]
        field[k, : STIFF + 1, ROWS + 2 : ROWS + 4, :] = lower[:, :, lanes]
        field[k, STIFF + 1] = jnp.zeros((8, LANES), jnp.float32)
        image[k, FIELDS] = jnp.zeros((8, LANES), jnp.float32)
    grown[FIELDS] = jnp.zeros((8, LANES), jnp.float32)

    def fill(table, k, values):
        table[k, 0] = values[0]
        for variable in range(VARS):
            for degree in range(DEG):
                table[k, 1 + variable * DEG + degree] = values[1 + variable] * CHAOS_VALUES[degree]

    def load_table(table, k):
        return [table[k, entry] for entry in range(TABLE)]

    @pl.loop(0, chunks)
    def grow(k):
        fill(coef_table, k, [field[k, FIELDS + term] for term in range(TERMS)])
        table = load_table(coef_table, k)

        @pl.loop(0, COMPS)
        def each(comp):
            base = comp * MODES
            for mode in range(MODES):
                load = lambda other: field[k, base + other]
                grown[base + mode] = mix(table, load, mode, table[0] * load(mode))

        split(grown[...], grown_high, grown_low, k)
        split(field[k], field_high, field_low, k)

    @pl.loop(0, chunks)
    def first(k):
        stencil(field_high, field_low, k, chunks, matrix_ref, first_near)
        stencil(grown_high, grown_low, k, chunks, matrix_ref, second_near)
        weight_sum = sum(weights_ref[number] for number in range(13))
        fill(
            diag_table,
            k,
            [
                field[k, FIELDS + term] * weight_sum + first_near[FIELDS + term]
                for term in range(TERMS)
            ],
        )
        coef = load_table(coef_table, k)
        diag = load_table(diag_table, k)
        stiff = field[k, STIFF]
        inside = stiff > 0.0

        @pl.loop(0, COMPS)
        def each(comp):
            base = comp * MODES
            for mode in range(MODES):
                load = lambda other: field[k, base + other]
                near = lambda other: first_near[base + other]
                value = mix(diag, load, mode, (stiff + diag[0]) * load(mode))
                value = value - mix(coef, near, mode, coef[0] * near(mode) + second_near[base + mode])
                image[k, base + mode] = jnp.where(inside, value, 0.0)

    @pl.loop(0, chunks)
    def regrow(k):
        table = load_table(coef_table, k)

        @pl.loop(0, COMPS)
        def each(comp):
            base = comp * MODES
            for mode in range(MODES):
                load = lambda other: image[k, base + other]
                grown[base + mode] = mix(table, load, mode, table[0] * load(mode))

        split(grown[...], grown_high, grown_low, k)
        split(image[k], image_high, image_low, k)

    third_near = first_near.at[pl.ds(0, FIELDS + 1)]
    zero = jnp.zeros((8, LANES), jnp.float32)

    def second(k, sums):
        stencil(image_high, image_low, k, chunks, matrix_ref, third_near)
        stencil(grown_high, grown_low, k, chunks, matrix_ref, second_near)
        coef = load_table(coef_table, k)
        diag = load_table(diag_table, k)
        stiff = field[k, STIFF]
        lanes = pl.ds(pl.multiple_of(k * LANES, LANES), LANES)

        def each(comp, sums):
            rr, rq, qq, qz = sums
            base = comp * MODES
            for mode in range(MODES):
                load = lambda other: image[k, base + other]
                near = lambda other: third_near[base + other]
                start, here = field[k, base + mode], load(mode)
                value = mix(diag, load, mode, (stiff + diag[0]) * here)
                value = value - mix(coef, near, mode, coef[0] * near(mode) + second_near[base + mode])
                image_ref[base + mode, :, lanes] = here[:ROWS]
                second_ref[base + mode, :, lanes] = value[:ROWS]
                rr, rq, qq, qz = rr + start * start, rq + start * here, qq + here * here, qz + here * value
            return rr, rq, qq, qz

        return lax.fori_loop(0, COMPS, each, sums)

    sums = lax.fori_loop(0, edge, second, (zero, zero, zero, zero))
    inner = lax.broadcasted_iota(jnp.int32, (8, LANES), 0) < ROWS
    lane = lax.broadcasted_iota(jnp.int32, sums_ref.shape, 1)
    row = jnp.zeros(sums_ref.shape, jnp.float32)
    for number, value in enumerate(sums):
        row = jnp.where(lane == number, jnp.sum(jnp.where(inner, value, 0.0)), row)
    sums_ref[...] = row


def finish_kernel(sums_ref, start_ref, image_ref, second_ref, field_ref, residual_ref):
    total = jnp.sum(sums_ref[...], axis=0, keepdims=True)
    lane = lax.broadcasted_iota(jnp.int32, total.shape, 1)
    rr, rq, qq, qz = [
        jnp.sum(jnp.where(lane == number, total, 0.0), axis=1, keepdims=True)[None]
        for number in range(4)
    ]
    step = rr / rq
    fresh = rr - 2.0 * step * rq + step * step * qq
    grow = 1.0 + fresh / rr
    curvature = grow * grow * rq - 2.0 * grow * step * qq + step * step * qz
    later = fresh / curvature
    both = step + later * grow
    cross = later * step
    start, image, second = start_ref[...], image_ref[...], second_ref[...]
    field_ref[...] = both * start - cross * image
    residual_ref[...] = start - both * image + cross * second


def shift(value, axis, by):
    size = lax.axis_size(axis)
    return lax.ppermute(value, axis, [(i, i + by) for i in range(size) if 0 <= i + by < size])


def per_device(right_side, stiffness, coefficients, stencil_weights):
    columns = right_side.shape[3]
    chunks = columns // LANES + 1
    devices = lax.axis_size("down") * lax.axis_size("cross")
    own = right_side.reshape(FIELDS, ROWS, columns)
    extra = jnp.concatenate([coefficients, stiffness[None]], axis=0)
    all_fields = jnp.concatenate([own, extra], axis=0)
    right = shift(all_fields[:, :, :WIDE], "cross", -1)
    left = shift(all_fields[:, :, columns - WIDE :], "cross", 1)
    upper = shift(all_fields[:, :2], "down", -1)
    lower = shift(all_fields[:, ROWS - 2 :], "down", 1)
    rims = jnp.concatenate([right, left], axis=2)
    upper_corner = shift(rims[:, :2], "down", -1)
    lower_corner = shift(rims[:, ROWS - 2 :], "down", 1)
    vmem = pl.BlockSpec(memory_space=pltpu.VMEM)
    count = FIELDS + 1
    f32, bf16 = jnp.float32, jnp.bfloat16
    smem = pl.BlockSpec(memory_space=pltpu.SMEM)
    matrix = pl.pallas_call(
        matrix_kernel,
        out_shape=jax.ShapeDtypeStruct((3 * SLOTS.shape[0], SLOTS.shape[1]), bf16),
        in_specs=[smem, vmem],
        out_specs=vmem,
        name="matrix",
    )(stencil_weights, jnp.asarray(SLOTS))
    image, second, sums = pl.pallas_call(
        functools.partial(operator_kernel, chunks),
        out_shape=(
            jax.ShapeDtypeStruct(own.shape, f32),
            jax.ShapeDtypeStruct(own.shape, f32),
            jax.ShapeDtypeStruct((devices, LANES), f32),
        ),
        in_specs=[vmem] * 9 + [smem],
        out_specs=(vmem, vmem, vmem),
        scratch_shapes=[
            pltpu.VMEM((chunks, STIFF + 2, 8, LANES), f32),
            pltpu.VMEM((chunks, (STIFF + 2) * 8, LANES), bf16),
            pltpu.VMEM((chunks, (STIFF + 2) * 8, LANES), bf16),
            pltpu.VMEM((count, 8, LANES), f32),
            pltpu.VMEM((chunks, count * 8, LANES), bf16),
            pltpu.VMEM((chunks, count * 8, LANES), bf16),
            pltpu.VMEM((STIFF + 2, 8, LANES), f32),
            pltpu.VMEM((count, 8, LANES), f32),
            pltpu.VMEM((chunks, count, 8, LANES), f32),
            pltpu.VMEM((chunks, count * 8, LANES), bf16),
            pltpu.VMEM((chunks, count * 8, LANES), bf16),
            pltpu.VMEM((chunks, TABLE, 8, LANES), f32),
            pltpu.VMEM((chunks, TABLE, 8, LANES), f32),
        ],
        compiler_params=pltpu.CompilerParams(vmem_limit_bytes=48 * 1024 * 1024),
        name="operator",
    )(own, extra, left, right, upper, lower, upper_corner, lower_corner, matrix, stencil_weights)
    sums = lax.all_to_all(sums, ("down", "cross"), 0, 0, tiled=True)
    solution_field, residual = pl.pallas_call(
        finish_kernel,
        out_shape=(jax.ShapeDtypeStruct(own.shape, f32), jax.ShapeDtypeStruct(own.shape, f32)),
        in_specs=[vmem] * 4,
        out_specs=(vmem, vmem),
        compiler_params=pltpu.CompilerParams(vmem_limit_bytes=32 * 1024 * 1024),
        name="finish",
    )(sums, own, image, second)
    return solution_field.reshape(right_side.shape), residual.reshape(right_side.shape)


def solution(mesh):
    return jax.shard_map(
        per_device,
        mesh=mesh,
        in_specs=(
            P(None, None, "down", "cross"),
            P("down", "cross"),
            P(None, "down", "cross"),
            P(),
        ),
        out_specs=(P(None, None, "down", "cross"), P(None, None, "down", "cross")),
        check_vma=False,
    )
```

```python
import functools
import math

import jax
import jax.numpy as jnp
import numpy as np
from jax import lax
from jax.experimental import pallas as pl
from jax.experimental.pallas import tpu as pltpu
from jax.sharding import PartitionSpec as P

CZ = 32
VARS = 4
DEG = 3
TERMS = 5
COMPS = 3
MODES = 35
FIELDS = COMPS * MODES
EXTRAS = TERMS + 1
GROUPS = (1, 2)
ROWS = 4
LANES = 128
WIDE = 64


def multi_indices(count_left, budget_left):
    if count_left == 0:
        return [()]
    return [
        (leading,) + remainder
        for leading in range(budget_left + 1)
        for remainder in multi_indices(count_left - 1, budget_left - leading)
    ]


def chaos_terms():
    picked = sorted(
        multi_indices(VARS, DEG),
        key=lambda multi_index: (sum(multi_index),)
        + tuple((-entry_value for entry_value in multi_index)),
    )
    position = {multi_index: number for number, multi_index in enumerate(picked)}
    terms = [[] for mode in picked]
    for variable in range(VARS):
        for multi_index in picked:
            raised = list(multi_index)
            raised[variable] += 1
            raised = tuple(raised)
            if raised in position:
                degree = multi_index[variable]
                here, there = position[multi_index], position[raised]
                terms[here].append((variable, degree, there))
                terms[there].append((variable, degree, here))
    values = [(n + 1) / math.sqrt((2 * n + 1) * (2 * n + 3)) for n in range(DEG)]
    return terms, values


CHAOS, CHAOS_VALUES = chaos_terms()
TABLE = 1 + VARS * DEG


def tap_slots():
    own = np.arange(LANES)
    place = np.concatenate([own, own[:WIDE] + LANES, own[WIDE:] - LANES])
    y_in, z_in = place // CZ, place % CZ
    y_out, z_out = own // CZ, own % CZ
    dy = y_in[:, None] - y_out[None, :]
    dz = z_in[:, None] - z_out[None, :]
    near = (abs(dy) <= 1) & (abs(dz) <= 1)
    parts = []
    for dx in (0, 1, -1):
        linear = 9 * (dx + 1) + 3 * (dy + 1) + (dz + 1)
        slot = np.minimum(linear, 26 - linear)
        parts.append(np.where(near, slot, 13))
    return np.concatenate(parts, axis=1).astype(np.int32)


SLOTS = tap_slots()


def matrix_kernel(weights_ref, slots_ref, matrix_ref):
    slots = slots_ref[...]
    full = jnp.zeros(slots.shape, jnp.float32)
    for number in range(13):
        full = jnp.where(slots == number, 0.5 * weights_ref[number], full)
    high = full.astype(jnp.bfloat16)
    low = (full - high.astype(jnp.float32)).astype(jnp.bfloat16)
    rows = slots.shape[0]
    matrix_ref[:rows] = high
    matrix_ref[rows : 2 * rows] = high
    matrix_ref[2 * rows :] = low


def mix(table, load, mode, total):
    for variable, degree, other in CHAOS[mode]:
        total = total + table[1 + variable * DEG + degree] * load(other)
    return total


def window(high, low, now, chunks):
    after, before = (now + 1) % chunks, (now + chunks - 1) % chunks
    shape = high.shape[1:]
    left = lax.broadcasted_iota(jnp.int32, shape, 1) < WIDE
    own_high, own_low = high[now], low[now]
    mix_high = jnp.where(left, high[after], high[before])
    mix_low = jnp.where(left, low[after], low[before])
    return jnp.concatenate([own_high, mix_high, own_low, mix_low, own_high, mix_high], axis=1)


def stencil(high, low, now, chunks, matrix, out):
    parts = jnp.dot(
        window(high, low, now, chunks), matrix[...], preferred_element_type=jnp.float32
    )
    shape = out.shape
    centre = parts[:, :LANES].reshape(shape)
    ahead = parts[:, LANES : 2 * LANES].reshape(shape)
    behind = parts[:, 2 * LANES :].reshape(shape)
    out[...] = centre + pltpu.roll(ahead, 7, 1) + pltpu.roll(behind, 1, 1)


def split(value, high, low, now):
    value = value.reshape(high.shape[1:])
    top = value.astype(jnp.bfloat16)
    high[now] = top
    low[now] = (value - top.astype(jnp.float32)).astype(jnp.bfloat16)


def operator_kernel(
    chunks, comps, cross_at, last,
    own_ref, extra_ref, left_ref, right_ref, upper_ref, lower_ref, upper_extra_ref, lower_extra_ref,
    matrix_ref, weights_ref, before_ref,
    image_ref, second_ref, sums_ref,
    field, field_high, field_low, grown, grown_high, grown_low,
    first_near, second_near, image, image_high, image_low, coef_table, diag_table,
):
    edge = chunks - 1
    fields = comps * MODES
    stiff_at = fields + TERMS
    own, extra = pl.ds(0, fields), pl.ds(fields, EXTRAS)
    cross_own, cross_extra = pl.ds(cross_at, fields), pl.ds(MODES, EXTRAS)
    for k in range(chunks):
        lanes = pl.ds(k * LANES, LANES)
        if k < edge:
            field[k, own, 0:ROWS, :] = own_ref[:, :, lanes]
            field[k, extra, 0:ROWS, :] = extra_ref[:, :, lanes]
        else:
            for to, here in ((own, cross_own), (extra, cross_extra)):
                field[k, to, 0:ROWS, :] = jnp.concatenate([right_ref[here], left_ref[here]], axis=2)
        for first_row, ref, extra_ref_here in (
            (ROWS, upper_ref, upper_extra_ref),
            (ROWS + 2, lower_ref, lower_extra_ref),
        ):
            rows = pl.ds(first_row, 2)
            field[k, own, rows, :] = ref[pl.ds(0, fields), :, lanes]
            field[k, extra, rows, :] = extra_ref_here[pl.ds(MODES, EXTRAS), :, lanes]
        for spare in range(fields + EXTRAS, field.shape[1]):
            field[k, spare] = jnp.zeros((8, LANES), jnp.float32)
        for spare in range(fields, image.shape[1]):
            image[k, spare] = jnp.zeros((8, LANES), jnp.float32)
    for spare in range(fields, grown.shape[0]):
        grown[spare] = jnp.zeros((8, LANES), jnp.float32)

    def fill(table, k, values):
        table[k, 0] = values[0]
        for variable in range(VARS):
            for degree in range(DEG):
                table[k, 1 + variable * DEG + degree] = values[1 + variable] * CHAOS_VALUES[degree]

    def load_table(table, k):
        return [table[k, entry] for entry in range(TABLE)]

    @pl.loop(0, chunks)
    def grow(k):
        fill(coef_table, k, [field[k, fields + term] for term in range(TERMS)])
        table = load_table(coef_table, k)

        @pl.loop(0, comps)
        def each(comp):
            base = comp * MODES
            for mode in range(MODES):
                load = lambda other: field[k, base + other]
                grown[base + mode] = mix(table, load, mode, table[0] * load(mode))

        split(grown[...], grown_high, grown_low, k)
        split(field[k], field_high, field_low, k)

    @pl.loop(0, chunks)
    def first(k):
        stencil(field_high, field_low, k, chunks, matrix_ref, first_near)
        stencil(grown_high, grown_low, k, chunks, matrix_ref, second_near)
        weight_sum = sum(weights_ref[number] for number in range(13))
        fill(
            diag_table,
            k,
            [
                field[k, fields + term] * weight_sum + first_near[fields + term]
                for term in range(TERMS)
            ],
        )
        coef = load_table(coef_table, k)
        diag = load_table(diag_table, k)
        stiff = field[k, stiff_at]
        inside = stiff > 0.0

        @pl.loop(0, comps)
        def each(comp):
            base = comp * MODES
            for mode in range(MODES):
                load = lambda other: field[k, base + other]
                near = lambda other: first_near[base + other]
                value = mix(diag, load, mode, (stiff + diag[0]) * load(mode))
                value = value - mix(coef, near, mode, coef[0] * near(mode) + second_near[base + mode])
                image[k, base + mode] = jnp.where(inside, value, 0.0)

    @pl.loop(0, chunks)
    def regrow(k):
        table = load_table(coef_table, k)

        @pl.loop(0, comps)
        def each(comp):
            base = comp * MODES
            for mode in range(MODES):
                load = lambda other: image[k, base + other]
                grown[base + mode] = mix(table, load, mode, table[0] * load(mode))

        split(grown[...], grown_high, grown_low, k)
        split(image[k], image_high, image_low, k)

    third_near = first_near.at[pl.ds(0, image.shape[1])]
    zero = jnp.zeros((8, LANES), jnp.float32)

    def second(k, sums):
        stencil(image_high, image_low, k, chunks, matrix_ref, third_near)
        stencil(grown_high, grown_low, k, chunks, matrix_ref, second_near)
        coef = load_table(coef_table, k)
        diag = load_table(diag_table, k)
        stiff = field[k, stiff_at]
        lanes = pl.ds(pl.multiple_of(k * LANES, LANES), LANES)

        def each(comp, sums):
            rr, rq, qq, qz = sums
            base = comp * MODES
            for mode in range(MODES):
                load = lambda other: image[k, base + other]
                near = lambda other: third_near[base + other]
                start, here = field[k, base + mode], load(mode)
                value = mix(diag, load, mode, (stiff + diag[0]) * here)
                value = value - mix(coef, near, mode, coef[0] * near(mode) + second_near[base + mode])
                image_ref[base + mode, :, lanes] = here[:ROWS]
                second_ref[base + mode, :, lanes] = value[:ROWS]
                rr, rq, qq, qz = rr + start * start, rq + start * here, qq + here * here, qz + here * value
            return rr, rq, qq, qz

        return lax.fori_loop(0, comps, each, sums)

    sums = lax.fori_loop(0, edge, second, (zero, zero, zero, zero))
    inner = lax.broadcasted_iota(jnp.int32, (8, LANES), 0) < ROWS
    sums = [jnp.where(inner, value, 0.0) + before_ref[n] for n, value in enumerate(sums)]
    if last:
        lane = lax.broadcasted_iota(jnp.int32, sums_ref.shape, 1)
        row = jnp.zeros(sums_ref.shape, jnp.float32)
        for number, value in enumerate(sums):
            row = jnp.where(lane == number, jnp.sum(value), row)
        sums_ref[...] = row
    else:
        for number, value in enumerate(sums):
            sums_ref[number] = value


def finish_kernel(sums_ref, start_ref, *refs):
    *parts, field_ref, residual_ref = refs
    total = jnp.sum(sums_ref[...], axis=0, keepdims=True)
    lane = lax.broadcasted_iota(jnp.int32, total.shape, 1)
    rr, rq, qq, qz = [
        jnp.sum(jnp.where(lane == number, total, 0.0), axis=1, keepdims=True)[None]
        for number in range(4)
    ]
    step = rr / rq
    fresh = rr - 2.0 * step * rq + step * step * qq
    grow = 1.0 + fresh / rr
    curvature = grow * grow * rq - 2.0 * grow * step * qq + step * step * qz
    later = fresh / curvature
    both = step + later * grow
    cross = later * step
    at = 0
    for image_ref, second_ref in zip(parts[::2], parts[1::2]):
        here = pl.ds(at, image_ref.shape[0])
        at += image_ref.shape[0]
        start, image, second = start_ref[here], image_ref[...], second_ref[...]
        field_ref[here] = both * start - cross * image
        residual_ref[here] = start - both * image + cross * second


def shift(value, axis, by):
    size = lax.axis_size(axis)
    return lax.ppermute(value, axis, [(i, i + by) for i in range(size) if 0 <= i + by < size])


def per_device(right_side, stiffness, coefficients, stencil_weights):
    columns = right_side.shape[3]
    chunks = columns // LANES + 1
    devices = lax.axis_size("down") * lax.axis_size("cross")
    own = right_side.reshape(FIELDS, ROWS, columns)
    extra = jnp.concatenate([coefficients, stiffness[None]], axis=0)
    all_fields = jnp.concatenate([own[:MODES], extra, own[MODES:]], axis=0)
    right = shift(all_fields[:, :, :WIDE], "cross", -1)
    left = shift(all_fields[:, :, columns - WIDE :], "cross", 1)
    wide = jnp.concatenate([all_fields, right, left], axis=2)
    vmem = pl.BlockSpec(memory_space=pltpu.VMEM)
    smem = pl.BlockSpec(memory_space=pltpu.SMEM)
    f32, bf16 = jnp.float32, jnp.bfloat16
    matrix = pl.pallas_call(
        matrix_kernel,
        out_shape=jax.ShapeDtypeStruct((3 * SLOTS.shape[0], SLOTS.shape[1]), bf16),
        in_specs=[smem, vmem],
        out_specs=vmem,
        name="matrix",
    )(stencil_weights, jnp.asarray(SLOTS))
    halos, begin = [], 0
    for comps in GROUPS:
        count = comps * MODES + (EXTRAS if begin == 0 else 0)
        part = wide[begin : begin + count]
        halos.append((begin, shift(part[:, :2], "down", -1), shift(part[:, ROWS - 2 :], "down", 1)))
        begin += count
    images, at = [], 0
    sums = jnp.zeros((4, 8, LANES), f32)
    for number, (comps, (cross_at, upper, lower)) in enumerate(zip(GROUPS, halos)):
        last = number == len(GROUPS) - 1
        fields = comps * MODES
        here = own[at : at + fields]
        at += fields
        count = fields + fields % 2
        wider = fields + EXTRAS + fields % 2
        image, second, sums = pl.pallas_call(
            functools.partial(operator_kernel, chunks, comps, cross_at, last),
            out_shape=(
                jax.ShapeDtypeStruct(here.shape, f32),
                jax.ShapeDtypeStruct(here.shape, f32),
                jax.ShapeDtypeStruct((devices, LANES) if last else sums.shape, f32),
            ),
            in_specs=[vmem] * 9 + [smem, vmem],
            out_specs=(vmem, vmem, vmem),
            scratch_shapes=[
                pltpu.VMEM((chunks, wider, 8, LANES), f32),
                pltpu.VMEM((chunks, wider * 8, LANES), bf16),
                pltpu.VMEM((chunks, wider * 8, LANES), bf16),
                pltpu.VMEM((count, 8, LANES), f32),
                pltpu.VMEM((chunks, count * 8, LANES), bf16),
                pltpu.VMEM((chunks, count * 8, LANES), bf16),
                pltpu.VMEM((wider, 8, LANES), f32),
                pltpu.VMEM((count, 8, LANES), f32),
                pltpu.VMEM((chunks, count, 8, LANES), f32),
                pltpu.VMEM((chunks, count * 8, LANES), bf16),
                pltpu.VMEM((chunks, count * 8, LANES), bf16),
                pltpu.VMEM((chunks, TABLE, 8, LANES), f32),
                pltpu.VMEM((chunks, TABLE, 8, LANES), f32),
            ],
            compiler_params=pltpu.CompilerParams(vmem_limit_bytes=40 * 1024 * 1024),
            cost_estimate=pl.CostEstimate(
                flops=18 * fields * 8 * 768 * 384 * 2, bytes_accessed=0, transcendentals=0
            ),
            name="operator",
        )(here, extra, left, right, upper, lower, halos[0][1], halos[0][2], matrix, stencil_weights, sums)
        images += [image, second]
    sums = lax.all_to_all(sums, ("down", "cross"), 0, 0, tiled=True)
    solution_field, residual = pl.pallas_call(
        finish_kernel,
        out_shape=(jax.ShapeDtypeStruct(own.shape, f32), jax.ShapeDtypeStruct(own.shape, f32)),
        in_specs=[vmem] * (2 + len(images)),
        out_specs=(vmem, vmem),
        compiler_params=pltpu.CompilerParams(vmem_limit_bytes=32 * 1024 * 1024),
        name="finish",
    )(sums, own, *images)
    return solution_field.reshape(right_side.shape), residual.reshape(right_side.shape)


def solution(mesh):
    return jax.shard_map(
        per_device,
        mesh=mesh,
        in_specs=(
            P(None, None, "down", "cross"),
            P("down", "cross"),
            P(None, "down", "cross"),
            P(),
        ),
        out_specs=(P(None, None, "down", "cross"), P(None, None, "down", "cross")),
        check_vma=False,
    )
```

```python
import functools
import math

import jax
import jax.numpy as jnp
import numpy as np
from jax import lax
from jax.experimental import pallas as pl
from jax.experimental.pallas import tpu as pltpu
from jax.sharding import PartitionSpec as P

CZ = 32
VARS = 4
DEG = 3
TERMS = 5
COMPS = 3
MODES = 35
FIELDS = COMPS * MODES
STIFF = FIELDS + TERMS
ROWS = 4
LANES = 128
WIDE = 64


def multi_indices(count_left, budget_left):
    if count_left == 0:
        return [()]
    return [
        (leading,) + remainder
        for leading in range(budget_left + 1)
        for remainder in multi_indices(count_left - 1, budget_left - leading)
    ]


def chaos_terms():
    picked = sorted(
        multi_indices(VARS, DEG),
        key=lambda multi_index: (sum(multi_index),)
        + tuple((-entry_value for entry_value in multi_index)),
    )
    position = {multi_index: number for number, multi_index in enumerate(picked)}
    terms = [[] for mode in picked]
    for variable in range(VARS):
        for multi_index in picked:
            raised = list(multi_index)
            raised[variable] += 1
            raised = tuple(raised)
            if raised in position:
                degree = multi_index[variable]
                here, there = position[multi_index], position[raised]
                terms[here].append((variable, degree, there))
                terms[there].append((variable, degree, here))
    values = [(n + 1) / math.sqrt((2 * n + 1) * (2 * n + 3)) for n in range(DEG)]
    return terms, values


CHAOS, CHAOS_VALUES = chaos_terms()
TABLE = 1 + VARS * DEG


def tap_slots(y_in, y_out, reach):
    z = np.arange(CZ)
    y_in, z_in = np.repeat(y_in, CZ), np.tile(z, len(y_in))
    y_out, z_out = np.repeat(y_out, CZ), np.tile(z, len(y_out))
    dy = y_in[:, None] - y_out[None, :]
    dz = z_in[:, None] - z_out[None, :]
    near = (abs(dy) <= 1) & (abs(dz) <= 1) & np.repeat(np.repeat(reach, CZ, 0), CZ, 1)
    parts = []
    for dx in (0, 1, -1):
        linear = 9 * (dx + 1) + 3 * (dy + 1) + (dz + 1)
        slot = np.minimum(linear, 26 - linear)
        parts.append(np.where(near & (linear != 13), slot, 13))
    return np.concatenate(parts, axis=1).astype(np.int32)


def chunk_slots():
    y_in = np.array([0, 1, 2, 3, 4, 5, -2, -1])
    return tap_slots(y_in, np.arange(4), np.ones((8, 4), bool))


def rim_slots():
    far = 100
    y_in = np.array([16, 17, -2 - far, -1 - far, -far, 1 - far, 14, 15])
    y_out = np.array([15, 16, -1 - far, -far])
    reach = np.ones((8, 4), bool)
    reach[4:, 0] = False
    reach[4:, 3] = False
    return tap_slots(y_in, y_out, reach)


SLOTS = np.stack([chunk_slots(), rim_slots()])


def matrix_kernel(weights_ref, slots_ref, matrix_ref):
    slots = slots_ref[0]
    full = jnp.zeros(slots.shape, jnp.float32)
    for number in range(13):
        full = jnp.where(slots == number, 0.5 * weights_ref[number], full)
    high = full.astype(jnp.bfloat16)
    low = (full - high.astype(jnp.float32)).astype(jnp.bfloat16)
    rows = slots.shape[0]
    matrix_ref[0, :rows] = high
    matrix_ref[0, rows : 2 * rows] = high
    matrix_ref[0, 2 * rows :] = low


def mix(table, load, mode, total):
    for variable, degree, other in CHAOS[mode]:
        total = total + table[1 + variable * DEG + degree] * load(other)
    return total


def window(own, after, before):
    left = lax.broadcasted_iota(jnp.int32, own[0].shape, 1) < WIDE
    high, low = [jnp.where(left, ahead, behind) for ahead, behind in zip(after, before)]
    return jnp.concatenate([own[0], high, own[1], low, own[0], high], axis=1)


def stencil(own, after, before, matrix, out):
    parts = jnp.dot(
        window(own, after, before), matrix[...], preferred_element_type=jnp.float32
    )
    shape = out.shape
    centre = parts[:, :LANES].reshape(shape)
    ahead = parts[:, LANES : 2 * LANES].reshape(shape)
    behind = parts[:, 2 * LANES :].reshape(shape)
    out[...] = centre + pltpu.roll(ahead, 7, 1) + pltpu.roll(behind, 1, 1)


def halves(value):
    value = value.reshape(value.shape[0] * 8, LANES)
    high = value.astype(jnp.bfloat16)
    return high, (value - high.astype(jnp.float32)).astype(jnp.bfloat16)


def fill(table, values):
    table[0] = values[0]
    for variable in range(VARS):
        for degree in range(DEG):
            table[1 + variable * DEG + degree] = values[1 + variable] * CHAOS_VALUES[degree]


def load_table(table):
    return [table[entry] for entry in range(TABLE)]


def grow(field, table, out):
    table = load_table(table)

    @pl.loop(0, COMPS)
    def each(comp):
        base = comp * MODES
        for mode in range(MODES):
            load = lambda other: field[base + other]
            out[base + mode] = mix(table, load, mode, table[0] * load(mode))


def apply(field, near, grown_near, coef, diag, stiff, store):
    coef, diag = load_table(coef), load_table(diag)

    def each(comp, carry):
        base = comp * MODES
        for mode in range(MODES):
            load = lambda other: field[base + other]
            close = lambda other: near[base + other]
            value = mix(diag, load, mode, (stiff + diag[0]) * load(mode))
            value = value - mix(
                coef, close, mode, coef[0] * close(mode) + grown_near[base + mode]
            )
            carry = store(base + mode, value, carry)
        return carry

    return each


def finish_chunk(start, image, near, grown_near, coef, diag, stiff, image_out, second_out, lanes, sums):
    def store(number, value, sums):
        rr, rq, qq, qz = sums
        first, here = start[number], image[number]
        image_out[number, :, lanes] = here[:ROWS]
        second_out[number, :, lanes] = value[:ROWS]
        return rr + first * first, rq + first * here, qq + here * here, qz + here * value

    return lax.fori_loop(0, COMPS, apply(image, near, grown_near, coef, diag, stiff, store), sums)


def fill_diag(table, field, near, weights_ref):
    weight_sum = sum(weights_ref[number] for number in range(13))
    fill(table, [field[FIELDS + t] * weight_sum + near[FIELDS + t] for t in range(TERMS)])


def inner_kernel(
    own_ref, extra_ref, upper_ref, lower_ref, matrix_ref, weights_ref,
    field, grown_high, grown_low, outer_near, outer_grown_near,
    image, image_high, image_low, image_grown_high, image_grown_low, coef_table, diag_table,
    image_ref, second_ref, sums_ref,
    field_high, field_low, grown, near, grown_near,
):
    chunks = field.shape[0]
    for k in range(chunks):
        lanes = pl.ds(k * LANES, LANES)
        field[k, :FIELDS, 0:ROWS, :] = own_ref[:, :, lanes]
        field[k, FIELDS : STIFF + 1, 0:ROWS, :] = extra_ref[:, :, lanes]
        field[k, : STIFF + 1, ROWS : ROWS + 2, :] = upper_ref[:, :, lanes]
        field[k, : STIFF + 1, ROWS + 2 : ROWS + 4, :] = lower_ref[:, :, lanes]
        field[k, STIFF + 1] = jnp.zeros((8, LANES), jnp.float32)
        image[k, FIELDS] = jnp.zeros((8, LANES), jnp.float32)
    grown[FIELDS] = jnp.zeros((8, LANES), jnp.float32)
    for ref in (field_high, field_low, grown_high, grown_low):
        ref[chunks] = jnp.zeros(ref.shape[1:], jnp.bfloat16)

    def step(k):
        return lax.rem(k + 1, chunks + 1), lax.rem(k + chunks, chunks + 1)

    @pl.loop(0, chunks)
    def grow_field(k):
        fill(coef_table.at[k], [field[k, FIELDS + term] for term in range(TERMS)])
        grow(field.at[k], coef_table.at[k], grown)
        grown_high[k], grown_low[k] = halves(grown[...])
        field_high[k], field_low[k] = halves(field[k])

    @pl.loop(0, chunks)
    def first(k):
        after, before = step(k)
        for high, low, out in ((field_high, field_low, near), (grown_high, grown_low, grown_near)):
            stencil(*[(high[at], low[at]) for at in (k, after, before)], matrix_ref, out)
        fill_diag(diag_table.at[k], field.at[k], near, weights_ref)
        stiff = field[k, STIFF]
        inside = stiff > 0.0

        def store(number, value, carry):
            image[k, number] = jnp.where(inside, value, 0.0)
            return carry

        lax.fori_loop(
            0,
            COMPS,
            apply(field.at[k], near, grown_near, coef_table.at[k], diag_table.at[k], stiff, store),
            0,
        )

        @pl.when(k == 0)
        def _():
            outer_near[0] = near[...]
            outer_grown_near[0] = grown_near[...]

        @pl.when(k == chunks - 1)
        def _():
            outer_near[1] = near[...]
            outer_grown_near[1] = grown_near[...]

    @pl.loop(0, chunks)
    def grow_image(k):
        grow(image.at[k], coef_table.at[k], grown)
        image_grown_high[k], image_grown_low[k] = halves(grown[...])
        image_high[k], image_low[k] = halves(image[k])

    image_near = near.at[pl.ds(0, FIELDS + 1)]
    zero = jnp.zeros((8, LANES), jnp.float32)

    def second(k, sums):
        for high, low, out in (
            (image_high, image_low, image_near),
            (image_grown_high, image_grown_low, grown_near),
        ):
            stencil(*[(high[at], low[at]) for at in (k, k + 1, k - 1)], matrix_ref, out)
        lanes = pl.ds(pl.multiple_of((k - 1) * LANES, LANES), LANES)
        return finish_chunk(
            field.at[k], image.at[k], image_near, grown_near, coef_table.at[k], diag_table.at[k],
            field[k, STIFF], image_ref, second_ref, lanes, sums,
        )

    sums = lax.fori_loop(1, chunks - 1, second, (zero, zero, zero, zero))
    for number, value in enumerate(sums):
        sums_ref[number] = value


def outer_kernel(
    right_ref, left_ref, matrix_ref, rim_matrix_ref, weights_ref,
    field, grown_high, grown_low, outer_near, outer_grown_near,
    image, image_high, image_low, image_grown_high, image_grown_low, coef_table, diag_table, before_ref,
    image_ref, second_ref, sums_ref,
    edge, rim, grown, near, grown_near, rim_image, edge_image, coef, diag, edge_coef, ends,
):
    final = field.shape[0] - 1
    lane = lax.broadcasted_iota(jnp.int32, (8, LANES), 1)
    zero = jnp.zeros((8, LANES), jnp.float32)
    edge[: STIFF + 1] = jnp.concatenate([right_ref[...], left_ref[...]], axis=2)
    edge[STIFF + 1] = zero
    grown[FIELDS] = zero
    rim_image[FIELDS] = zero
    for side in range(2):
        ends[side, FIELDS] = zero
    edge_image[FIELDS] = zero

    def to_rim(last, beyond, begin):
        right = pltpu.roll(jnp.where(lane >= 3 * CZ, last, beyond), CZ, last.ndim - 1)
        left = pltpu.roll(jnp.where(lane < CZ, begin, beyond), LANES - CZ, last.ndim - 1)
        return jnp.where(lane < WIDE, right, left)

    fill(edge_coef, [edge[FIELDS + term] for term in range(TERMS)])
    grow(edge, edge_coef, grown)
    edge_parts = halves(edge[...])
    begin, last = halves(field[0]), halves(field[final])
    stencil(edge_parts, begin, last, rim_matrix_ref, near)
    stencil(
        halves(grown[...]),
        (grown_high[0], grown_low[0]),
        (grown_high[final], grown_low[final]),
        rim_matrix_ref,
        grown_near,
    )
    left_rim, right_rim = lane >= 3 * CZ, lane < CZ

    def own_part(last, begin):
        moved = jnp.where(right_rim, pltpu.roll(last, CZ, last.ndim - 1), 0.0)
        return jnp.where(left_rim, pltpu.roll(begin, LANES - CZ, last.ndim - 1), moved)

    near[...] = near[...] + own_part(outer_near[1], outer_near[0])
    grown_near[...] = grown_near[...] + own_part(outer_grown_near[1], outer_grown_near[0])
    rim[...] = to_rim(field[final], edge[...], field[0])
    fill(coef, [rim[FIELDS + term] for term in range(TERMS)])
    fill_diag(diag, rim, near, weights_ref)
    stiff = rim[STIFF]
    inside = stiff > 0.0

    def store(number, value, carry):
        rim_image[number] = jnp.where(inside, value, 0.0)
        return carry

    lax.fori_loop(0, COMPS, apply(rim, near, grown_near, coef, diag, stiff, store), 0)
    grow(rim_image, coef, grown)

    def from_rim(value):
        return pltpu.roll(value, CZ, value.ndim - 1), pltpu.roll(value, LANES - CZ, value.ndim - 1)

    def placed(begin, last, value):
        to_left, to_right = from_rim(value)
        return (
            jnp.where(lane < CZ, to_left, begin),
            jnp.where(lane >= 3 * CZ, to_right, last),
            jnp.where(lane < WIDE, to_right, to_left),
        )

    ends[0], ends[1], edge_image[...] = placed(image[0], image[final], rim_image[...])
    image_parts = [halves(ends[0]), halves(ends[1]), halves(edge_image[...])]

    def joined(ref_high, ref_low, k):
        return (ref_high[k].astype(jnp.float32) + ref_low[k].astype(jnp.float32)).reshape(
            grown.shape
        )

    grown_parts = [
        halves(value)
        for value in placed(
            joined(image_grown_high, image_grown_low, 0),
            joined(image_grown_high, image_grown_low, final),
            grown[...],
        )
    ]
    for entry in range(TABLE):
        to_left, to_right = from_rim(diag[entry])
        edge_coef[entry] = jnp.where(lane < CZ, to_left, diag_table[0, entry])
        coef[entry] = jnp.where(lane >= 3 * CZ, to_right, diag_table[final, entry])
    image_near = near.at[pl.ds(0, FIELDS + 1)]
    sums = tuple(before_ref[number] for number in range(4))
    for side, k, table in ((0, 0, edge_coef), (1, final, coef)):
        for (begin, last, beyond), high, low, out in (
            (image_parts, image_high, image_low, image_near),
            (grown_parts, image_grown_high, image_grown_low, grown_near),
        ):
            if side == 0:
                chunk = (begin, (high[1], low[1]), beyond)
            else:
                chunk = (last, beyond, (high[final - 1], low[final - 1]))
            stencil(*chunk, matrix_ref, out)
        sums = finish_chunk(
            field.at[k], ends.at[side], image_near, grown_near, coef_table.at[k], table,
            field[k, STIFF], image_ref, second_ref, pl.ds(side * LANES, LANES), sums,
        )
    inner = lax.broadcasted_iota(jnp.int32, (8, LANES), 0) < ROWS
    column = lax.broadcasted_iota(jnp.int32, sums_ref.shape, 1)
    row = jnp.zeros(sums_ref.shape, jnp.float32)
    for number, value in enumerate(sums):
        row = jnp.where(column == number, jnp.sum(jnp.where(inner, value, 0.0)), row)
    sums_ref[...] = row


def finish_kernel(sums_ref, start_ref, *refs):
    *parts, field_ref, residual_ref = refs
    total = jnp.sum(sums_ref[...], axis=0, keepdims=True)
    lane = lax.broadcasted_iota(jnp.int32, total.shape, 1)
    rr, rq, qq, qz = [
        jnp.sum(jnp.where(lane == number, total, 0.0), axis=1, keepdims=True)[None]
        for number in range(4)
    ]
    step = rr / rq
    fresh = rr - 2.0 * step * rq + step * step * qq
    grow = 1.0 + fresh / rr
    curvature = grow * grow * rq - 2.0 * grow * step * qq + step * step * qz
    later = fresh / curvature
    both = step + later * grow
    cross = later * step
    inner, outer = parts[:2], parts[2:]
    columns = start_ref.shape[2]
    for (image_ref, second_ref), source, at, width in (
        (outer, 0, 0, LANES),
        (inner, 0, LANES, columns - 2 * LANES),
        (outer, LANES, columns - LANES, LANES),
    ):
        there, here = pl.ds(source, width), pl.ds(at, width)
        start, image, second = start_ref[:, :, here], image_ref[:, :, there], second_ref[:, :, there]
        field_ref[:, :, here] = both * start - cross * image
        residual_ref[:, :, here] = start - both * image + cross * second


def shift(value, axis, by):
    size = lax.axis_size(axis)
    return lax.ppermute(value, axis, [(i, i + by) for i in range(size) if 0 <= i + by < size])


def per_device(right_side, stiffness, coefficients, stencil_weights):
    columns = right_side.shape[3]
    chunks = columns // LANES
    devices = lax.axis_size("down") * lax.axis_size("cross")
    own = right_side.reshape(FIELDS, ROWS, columns)
    extra = jnp.concatenate([coefficients, stiffness[None]], axis=0)
    all_fields = jnp.concatenate([own, extra], axis=0)
    upper = shift(all_fields[:, :2], "down", -1)
    lower = shift(all_fields[:, ROWS - 2 :], "down", 1)
    tall = jnp.concatenate([all_fields, upper, lower], axis=1)
    right = shift(tall[:, :, :WIDE], "cross", -1)
    left = shift(tall[:, :, columns - WIDE :], "cross", 1)
    vmem = pl.BlockSpec(memory_space=pltpu.VMEM)
    smem = pl.BlockSpec(memory_space=pltpu.SMEM)
    f32, bf16 = jnp.float32, jnp.bfloat16
    params = pltpu.CompilerParams(vmem_limit_bytes=32 * 1024 * 1024)
    matrices = pl.pallas_call(
        matrix_kernel,
        grid=(2,),
        out_shape=jax.ShapeDtypeStruct((2, 3 * SLOTS.shape[1], SLOTS.shape[2]), bf16),
        in_specs=[smem, pl.BlockSpec((1,) + SLOTS.shape[1:], lambda i: (i, 0, 0))],
        out_specs=pl.BlockSpec((1, 3 * SLOTS.shape[1], SLOTS.shape[2]), lambda i: (i, 0, 0)),
        name="matrix",
    )(stencil_weights, jnp.asarray(SLOTS))
    matrix, rim_matrix = matrices[0], matrices[1]
    shape = jax.ShapeDtypeStruct
    count, wider = FIELDS + 1, STIFF + 2
    tiles = lambda number: (number, 8, LANES)
    rows = lambda number: (number * 8, LANES)
    half = (FIELDS, ROWS, columns // 2)
    *kept, image, second, sums = pl.pallas_call(
        inner_kernel,
        out_shape=(
            shape((chunks,) + tiles(wider), f32),
            shape((chunks + 1,) + rows(count), bf16),
            shape((chunks + 1,) + rows(count), bf16),
            shape((2,) + tiles(wider), f32),
            shape((2,) + tiles(count), f32),
            shape((chunks,) + tiles(count), f32),
            shape((chunks,) + rows(count), bf16),
            shape((chunks,) + rows(count), bf16),
            shape((chunks,) + rows(count), bf16),
            shape((chunks,) + rows(count), bf16),
            shape((chunks,) + tiles(TABLE), f32),
            shape((chunks,) + tiles(TABLE), f32),
            shape(half, f32),
            shape(half, f32),
            shape(tiles(4), f32),
        ),
        in_specs=[vmem] * 5 + [smem],
        out_specs=(vmem,) * 15,
        scratch_shapes=[
            pltpu.VMEM((chunks + 1,) + rows(wider), bf16),
            pltpu.VMEM((chunks + 1,) + rows(wider), bf16),
            pltpu.VMEM(tiles(count), f32),
            pltpu.VMEM(tiles(wider), f32),
            pltpu.VMEM(tiles(count), f32),
        ],
        compiler_params=params,
        cost_estimate=pl.CostEstimate(flops=10**10, bytes_accessed=0, transcendentals=0),
        name="inner",
    )(own, extra, upper, lower, matrix, stencil_weights)
    outer_image, outer_second, sums = pl.pallas_call(
        outer_kernel,
        out_shape=(shape(half, f32), shape(half, f32), shape((devices, LANES), f32)),
        in_specs=[vmem] * 4 + [smem] + [vmem] * 13,
        out_specs=(vmem,) * 3,
        scratch_shapes=[
            pltpu.VMEM(tiles(wider), f32),
            pltpu.VMEM(tiles(wider), f32),
            pltpu.VMEM(tiles(count), f32),
            pltpu.VMEM(tiles(wider), f32),
            pltpu.VMEM(tiles(count), f32),
            pltpu.VMEM(tiles(count), f32),
            pltpu.VMEM(tiles(count), f32),
            pltpu.VMEM(tiles(TABLE), f32),
            pltpu.VMEM(tiles(TABLE), f32),
            pltpu.VMEM(tiles(TABLE), f32),
            pltpu.VMEM((2,) + tiles(count), f32),
        ],
        compiler_params=params,
        name="outer",
    )(right, left, matrix, rim_matrix, stencil_weights, *kept, sums)
    sums = lax.all_to_all(sums, ("down", "cross"), 0, 0, tiled=True)
    solution_field, residual = pl.pallas_call(
        finish_kernel,
        out_shape=(shape(own.shape, f32), shape(own.shape, f32)),
        in_specs=[vmem] * 6,
        out_specs=(vmem, vmem),
        compiler_params=params,
        name="finish",
    )(sums, own, image, second, outer_image, outer_second)
    return solution_field.reshape(right_side.shape), residual.reshape(right_side.shape)


def solution(mesh):
    return jax.shard_map(
        per_device,
        mesh=mesh,
        in_specs=(
            P(None, None, "down", "cross"),
            P("down", "cross"),
            P(None, "down", "cross"),
            P(),
        ),
        out_specs=(P(None, None, "down", "cross"), P(None, None, "down", "cross")),
        check_vma=False,
    )
```

```python
import functools
import math

import jax
import jax.numpy as jnp
import numpy as np
from jax import lax
from jax.experimental import pallas as pl
from jax.experimental.pallas import tpu as pltpu
from jax.sharding import PartitionSpec as P

CZ = 32
VARS = 4
DEG = 3
TERMS = 5
COMPS = 3
MODES = 35
FIELDS = COMPS * MODES
STIFF = FIELDS + TERMS
ROWS = 4
LANES = 128
WIDE = 64


def multi_indices(count_left, budget_left):
    if count_left == 0:
        return [()]
    return [
        (leading,) + remainder
        for leading in range(budget_left + 1)
        for remainder in multi_indices(count_left - 1, budget_left - leading)
    ]


def chaos_terms():
    picked = sorted(
        multi_indices(VARS, DEG),
        key=lambda multi_index: (sum(multi_index),)
        + tuple((-entry_value for entry_value in multi_index)),
    )
    position = {multi_index: number for number, multi_index in enumerate(picked)}
    terms = [[] for mode in picked]
    for variable in range(VARS):
        for multi_index in picked:
            raised = list(multi_index)
            raised[variable] += 1
            raised = tuple(raised)
            if raised in position:
                degree = multi_index[variable]
                here, there = position[multi_index], position[raised]
                terms[here].append((variable, degree, there))
                terms[there].append((variable, degree, here))
    values = [(n + 1) / math.sqrt((2 * n + 1) * (2 * n + 3)) for n in range(DEG)]
    return terms, values


CHAOS, CHAOS_VALUES = chaos_terms()
TABLE = 1 + VARS * DEG


def tap_slots(y_in, y_out, reach):
    z = np.arange(CZ)
    y_in, z_in = np.repeat(y_in, CZ), np.tile(z, len(y_in))
    y_out, z_out = np.repeat(y_out, CZ), np.tile(z, len(y_out))
    dy = y_in[:, None] - y_out[None, :]
    dz = z_in[:, None] - z_out[None, :]
    near = (abs(dy) <= 1) & (abs(dz) <= 1) & np.repeat(np.repeat(reach, CZ, 0), CZ, 1)
    parts = []
    for dx in (0, 1, -1):
        linear = 9 * (dx + 1) + 3 * (dy + 1) + (dz + 1)
        slot = np.minimum(linear, 26 - linear)
        parts.append(np.where(near & (linear != 13), slot, 13))
    return np.concatenate(parts, axis=1).astype(np.int32)


def chunk_slots():
    y_in = np.array([0, 1, 2, 3, 4, 5, -2, -1])
    return tap_slots(y_in, np.arange(4), np.ones((8, 4), bool))


def rim_slots():
    far = 100
    y_in = np.array([16, 17, -2 - far, -1 - far, -far, 1 - far, 14, 15])
    y_out = np.array([15, 16, -1 - far, -far])
    reach = np.ones((8, 4), bool)
    reach[4:, 0] = False
    reach[4:, 3] = False
    return tap_slots(y_in, y_out, reach)


SLOTS = np.stack([chunk_slots(), rim_slots()])


def matrix_kernel(weights_ref, slots_ref, matrix_ref):
    slots = slots_ref[0]
    full = jnp.zeros(slots.shape, jnp.float32)
    for number in range(13):
        full = jnp.where(slots == number, 0.5 * weights_ref[number], full)
    high = full.astype(jnp.bfloat16)
    low = (full - high.astype(jnp.float32)).astype(jnp.bfloat16)
    rows = slots.shape[0]
    matrix_ref[0, :rows] = high
    matrix_ref[0, rows : 2 * rows] = high
    matrix_ref[0, 2 * rows :] = low


def mix(table, load, mode, total):
    for variable, degree, other in CHAOS[mode]:
        total = total + table[1 + variable * DEG + degree] * load(other)
    return total


def window(own, after, before):
    left = lax.broadcasted_iota(jnp.int32, own[0].shape, 1) < WIDE
    high, low = [jnp.where(left, ahead, behind) for ahead, behind in zip(after, before)]
    return jnp.concatenate([own[0], high, own[1], low, own[0], high], axis=1)


def stencil(own, after, before, matrix, out):
    parts = jnp.dot(
        window(own, after, before), matrix[...], preferred_element_type=jnp.float32
    )
    shape = out.shape
    centre = parts[:, :LANES].reshape(shape)
    ahead = parts[:, LANES : 2 * LANES].reshape(shape)
    behind = parts[:, 2 * LANES :].reshape(shape)
    out[...] = centre + pltpu.roll(ahead, 7, 1) + pltpu.roll(behind, 1, 1)


def halves(value):
    value = value.reshape(value.shape[0] * 8, LANES)
    high = value.astype(jnp.bfloat16)
    return high, (value - high.astype(jnp.float32)).astype(jnp.bfloat16)


def fill(table, values):
    table[0] = values[0]
    for variable in range(VARS):
        for degree in range(DEG):
            table[1 + variable * DEG + degree] = values[1 + variable] * CHAOS_VALUES[degree]


def load_table(table):
    return [table[entry] for entry in range(TABLE)]


def grow(field, table, out):
    table = load_table(table)

    @pl.loop(0, COMPS)
    def each(comp):
        base = comp * MODES
        for mode in range(MODES):
            load = lambda other: field(base + other)
            out[base + mode] = mix(table, load, mode, table[0] * load(mode))


def apply(field, near, grown_near, coef, diag, stiff, store):
    coef, diag = load_table(coef), load_table(diag)

    def each(comp, carry):
        base = comp * MODES
        for mode in range(MODES):
            load = lambda other: field(base + other)
            close = lambda other: near[base + other]
            value = mix(diag, load, mode, (stiff + diag[0]) * load(mode))
            value = value - mix(
                coef, close, mode, coef[0] * close(mode) + grown_near[base + mode]
            )
            carry = store(base + mode, value, carry)
        return carry

    return each


def finish_chunk(start, image, near, grown_near, coef, diag, stiff, image_out, second_out, lanes, sums):
    def store(number, value, sums):
        rr, rq, qq, qz = sums
        first, here = start(number), image(number)
        image_out[number, :, lanes] = here[:ROWS]
        second_out[number, :, lanes] = value[:ROWS]
        return rr + first * first, rq + first * here, qq + here * here, qz + here * value

    return lax.fori_loop(0, COMPS, apply(image, near, grown_near, coef, diag, stiff, store), sums)


def fill_diag(table, field, near, weights_ref):
    weight_sum = sum(weights_ref[number] for number in range(13))
    fill(table, [field(FIELDS + t) * weight_sum + near[FIELDS + t] for t in range(TERMS)])


def chunk_of(ref, k):
    lanes = pl.ds(pl.multiple_of(k * LANES, LANES), LANES)
    return lambda number: ref[number, :, lanes]


def entry_of(ref):
    return lambda number: ref[number]


def inner_kernel(
    tall_ref, matrix_ref, weights_ref,
    grown_high, grown_low, outer_near, outer_grown_near,
    image, image_high, image_low, image_grown_high, image_grown_low, coef_table, diag_table,
    image_ref, second_ref, sums_ref,
    field_high, field_low, grown, near, grown_near,
):
    chunks = image.shape[0]
    for k in range(chunks):
        image[k, FIELDS] = jnp.zeros((8, LANES), jnp.float32)
    grown[FIELDS] = jnp.zeros((8, LANES), jnp.float32)
    for ref in (field_high, field_low, grown_high, grown_low):
        ref[chunks] = jnp.zeros(ref.shape[1:], jnp.bfloat16)

    def step(k):
        return lax.rem(k + 1, chunks + 1), lax.rem(k + chunks, chunks + 1)

    @pl.loop(0, chunks)
    def grow_field(k):
        field = chunk_of(tall_ref, k)
        fill(coef_table.at[k], [field(FIELDS + term) for term in range(TERMS)])
        grow(field, coef_table.at[k], grown)
        grown_high[k], grown_low[k] = halves(grown[...])
        field_high[k], field_low[k] = halves(field(slice(None)))

    @pl.loop(0, chunks)
    def first(k):
        after, before = step(k)
        field = chunk_of(tall_ref, k)
        for high, low, out in ((field_high, field_low, near), (grown_high, grown_low, grown_near)):
            stencil(*[(high[at], low[at]) for at in (k, after, before)], matrix_ref.at[0], out)
        fill_diag(diag_table.at[k], field, near, weights_ref)
        stiff = field(STIFF)
        inside = stiff > 0.0

        def store(number, value, carry):
            image[k, number] = jnp.where(inside, value, 0.0)
            return carry

        lax.fori_loop(
            0,
            COMPS,
            apply(field, near, grown_near, coef_table.at[k], diag_table.at[k], stiff, store),
            0,
        )

        @pl.when(k == 0)
        def _():
            outer_near[0] = near[...]
            outer_grown_near[0] = grown_near[...]

        @pl.when(k == chunks - 1)
        def _():
            outer_near[1] = near[...]
            outer_grown_near[1] = grown_near[...]

    @pl.loop(0, chunks)
    def grow_image(k):
        grow(entry_of(image.at[k]), coef_table.at[k], grown)
        image_grown_high[k], image_grown_low[k] = halves(grown[...])
        image_high[k], image_low[k] = halves(image[k])

    image_near = near.at[pl.ds(0, FIELDS + 1)]
    zero = jnp.zeros((8, LANES), jnp.float32)

    def second(k, sums):
        for high, low, out in (
            (image_high, image_low, image_near),
            (image_grown_high, image_grown_low, grown_near),
        ):
            stencil(*[(high[at], low[at]) for at in (k, k + 1, k - 1)], matrix_ref.at[0], out)
        field = chunk_of(tall_ref, k)
        lanes = pl.ds(pl.multiple_of((k - 1) * LANES, LANES), LANES)
        return finish_chunk(
            field, entry_of(image.at[k]), image_near, grown_near, coef_table.at[k], diag_table.at[k],
            field(STIFF), image_ref, second_ref, lanes, sums,
        )

    sums = lax.fori_loop(1, chunks - 1, second, (zero, zero, zero, zero))
    for number, value in enumerate(sums):
        sums_ref[number] = value


def outer_kernel(
    right_ref, left_ref, tall_ref, matrix_ref, weights_ref,
    grown_high, grown_low, outer_near, outer_grown_near,
    image, image_high, image_low, image_grown_high, image_grown_low, coef_table, diag_table, before_ref,
    image_ref, second_ref, sums_ref,
    edge, rim, grown, near, grown_near, rim_image, edge_image, coef, diag, edge_coef, ends,
):
    final = image.shape[0] - 1
    first_field, last_field = chunk_of(tall_ref, 0), chunk_of(tall_ref, final)
    lane = lax.broadcasted_iota(jnp.int32, (8, LANES), 1)
    zero = jnp.zeros((8, LANES), jnp.float32)
    edge[: STIFF + 1] = jnp.concatenate([right_ref[...], left_ref[...]], axis=2)
    edge[STIFF + 1] = zero
    grown[FIELDS] = zero
    rim_image[FIELDS] = zero
    for side in range(2):
        ends[side, FIELDS] = zero
    edge_image[FIELDS] = zero

    def to_rim(last, beyond, begin):
        right = pltpu.roll(jnp.where(lane >= 3 * CZ, last, beyond), CZ, last.ndim - 1)
        left = pltpu.roll(jnp.where(lane < CZ, begin, beyond), LANES - CZ, last.ndim - 1)
        return jnp.where(lane < WIDE, right, left)

    fill(edge_coef, [edge[FIELDS + term] for term in range(TERMS)])
    grow(entry_of(edge), edge_coef, grown)
    edge_parts = halves(edge[...])
    begin, last = halves(first_field(slice(None))), halves(last_field(slice(None)))
    stencil(edge_parts, begin, last, matrix_ref.at[1], near)
    stencil(
        halves(grown[...]),
        (grown_high[0], grown_low[0]),
        (grown_high[final], grown_low[final]),
        matrix_ref.at[1],
        grown_near,
    )
    left_rim, right_rim = lane >= 3 * CZ, lane < CZ

    def own_part(last, begin):
        moved = jnp.where(right_rim, pltpu.roll(last, CZ, last.ndim - 1), 0.0)
        return jnp.where(left_rim, pltpu.roll(begin, LANES - CZ, last.ndim - 1), moved)

    near[...] = near[...] + own_part(outer_near[1], outer_near[0])
    grown_near[...] = grown_near[...] + own_part(outer_grown_near[1], outer_grown_near[0])
    rim[...] = to_rim(last_field(slice(None)), edge[...], first_field(slice(None)))
    fill(coef, [rim[FIELDS + term] for term in range(TERMS)])
    fill_diag(diag, entry_of(rim), near, weights_ref)
    stiff = rim[STIFF]
    inside = stiff > 0.0

    def store(number, value, carry):
        rim_image[number] = jnp.where(inside, value, 0.0)
        return carry

    lax.fori_loop(0, COMPS, apply(entry_of(rim), near, grown_near, coef, diag, stiff, store), 0)
    grow(entry_of(rim_image), coef, grown)

    def from_rim(value):
        return pltpu.roll(value, CZ, value.ndim - 1), pltpu.roll(value, LANES - CZ, value.ndim - 1)

    def placed(begin, last, value):
        to_left, to_right = from_rim(value)
        return (
            jnp.where(lane < CZ, to_left, begin),
            jnp.where(lane >= 3 * CZ, to_right, last),
            jnp.where(lane < WIDE, to_right, to_left),
        )

    ends[0], ends[1], edge_image[...] = placed(image[0], image[final], rim_image[...])
    image_parts = [halves(ends[0]), halves(ends[1]), halves(edge_image[...])]

    def joined(ref_high, ref_low, k):
        return (ref_high[k].astype(jnp.float32) + ref_low[k].astype(jnp.float32)).reshape(
            grown.shape
        )

    grown_parts = [
        halves(value)
        for value in placed(
            joined(image_grown_high, image_grown_low, 0),
            joined(image_grown_high, image_grown_low, final),
            grown[...],
        )
    ]
    for entry in range(TABLE):
        to_left, to_right = from_rim(diag[entry])
        edge_coef[entry] = jnp.where(lane < CZ, to_left, diag_table[0, entry])
        coef[entry] = jnp.where(lane >= 3 * CZ, to_right, diag_table[final, entry])
    image_near = near.at[pl.ds(0, FIELDS + 1)]
    sums = tuple(before_ref[number] for number in range(4))
    for side, k, table, field in ((0, 0, edge_coef, first_field), (1, final, coef, last_field)):
        for (begin, last, beyond), high, low, out in (
            (image_parts, image_high, image_low, image_near),
            (grown_parts, image_grown_high, image_grown_low, grown_near),
        ):
            if side == 0:
                chunk = (begin, (high[1], low[1]), beyond)
            else:
                chunk = (last, beyond, (high[final - 1], low[final - 1]))
            stencil(*chunk, matrix_ref.at[0], out)
        sums = finish_chunk(
            field, entry_of(ends.at[side]), image_near, grown_near, coef_table.at[k], table,
            field(STIFF), image_ref, second_ref, pl.ds(side * LANES, LANES), sums,
        )
    inner = lax.broadcasted_iota(jnp.int32, (8, LANES), 0) < ROWS
    column = lax.broadcasted_iota(jnp.int32, sums_ref.shape, 1)
    row = jnp.zeros(sums_ref.shape, jnp.float32)
    for number, value in enumerate(sums):
        row = jnp.where(column == number, jnp.sum(jnp.where(inner, value, 0.0)), row)
    sums_ref[...] = row


def finish_kernel(sums_ref, start_ref, *refs):
    *parts, field_ref, residual_ref = refs
    total = jnp.sum(sums_ref[...], axis=0, keepdims=True)
    lane = lax.broadcasted_iota(jnp.int32, total.shape, 1)
    rr, rq, qq, qz = [
        jnp.sum(jnp.where(lane == number, total, 0.0), axis=1, keepdims=True)[None]
        for number in range(4)
    ]
    step = rr / rq
    fresh = rr - 2.0 * step * rq + step * step * qq
    grow = 1.0 + fresh / rr
    curvature = grow * grow * rq - 2.0 * grow * step * qq + step * step * qz
    later = fresh / curvature
    both = step + later * grow
    cross = later * step
    inner, outer = parts[:2], parts[2:]
    columns = start_ref.shape[2]
    for (image_ref, second_ref), source, at, width in (
        (outer, 0, 0, LANES),
        (inner, 0, LANES, columns - 2 * LANES),
        (outer, LANES, columns - LANES, LANES),
    ):
        there, here = pl.ds(source, width), pl.ds(at, width)
        start, image, second = start_ref[:, :, here], image_ref[:, :, there], second_ref[:, :, there]
        field_ref[:, :, here] = both * start - cross * image
        residual_ref[:, :, here] = start - both * image + cross * second


def shift(value, axis, by):
    size = lax.axis_size(axis)
    return lax.ppermute(value, axis, [(i, i + by) for i in range(size) if 0 <= i + by < size])


def swap(value, axis, begin):
    size = lax.axis_size(axis)
    pairs = [(i, i + 1) for i in range(begin, size - 1, 2)]
    return lax.ppermute(value, axis, pairs + [(j, i) for i, j in pairs])


def per_device(right_side, stiffness, coefficients, stencil_weights):
    columns = right_side.shape[3]
    chunks = columns // LANES
    devices = lax.axis_size("down") * lax.axis_size("cross")
    own = right_side.reshape(FIELDS, ROWS, columns)
    extra = jnp.concatenate([coefficients, stiffness[None]], axis=0)
    spare = jnp.zeros((1, ROWS, columns), jnp.float32)
    all_fields = jnp.concatenate([own, extra, spare], axis=0)
    even = lax.axis_index("down") % 2 == 0
    head, tail = all_fields[: STIFF + 1, :2], all_fields[: STIFF + 1, ROWS - 2 :]
    one = swap(jnp.where(even, tail, head), "down", 0)
    other = swap(jnp.where(even, head, tail), "down", 1)
    upper, lower = jnp.where(even, one, other), jnp.where(even, other, one)
    beyond = jnp.concatenate([upper, lower], axis=1)
    beyond = jnp.concatenate([beyond, spare], axis=0)
    tall = jnp.concatenate([all_fields, beyond], axis=1)
    right = shift(tall[: STIFF + 1, :, :WIDE], "cross", -1)
    left = shift(tall[: STIFF + 1, :, columns - WIDE :], "cross", 1)
    vmem = pl.BlockSpec(memory_space=pltpu.VMEM)
    smem = pl.BlockSpec(memory_space=pltpu.SMEM)
    f32, bf16 = jnp.float32, jnp.bfloat16
    params = pltpu.CompilerParams(vmem_limit_bytes=32 * 1024 * 1024)
    matrices = pl.pallas_call(
        matrix_kernel,
        grid=(2,),
        out_shape=jax.ShapeDtypeStruct((2, 3 * SLOTS.shape[1], SLOTS.shape[2]), bf16),
        in_specs=[smem, pl.BlockSpec((1,) + SLOTS.shape[1:], lambda i: (i, 0, 0))],
        out_specs=pl.BlockSpec((1, 3 * SLOTS.shape[1], SLOTS.shape[2]), lambda i: (i, 0, 0)),
        name="matrix",
    )(stencil_weights, jnp.asarray(SLOTS))
    shape = jax.ShapeDtypeStruct
    count, wider = FIELDS + 1, STIFF + 2
    tiles = lambda number: (number, 8, LANES)
    rows = lambda number: (number * 8, LANES)
    half = (FIELDS, ROWS, columns // 2)
    *kept, image, second, sums = pl.pallas_call(
        inner_kernel,
        out_shape=(
            shape((chunks + 1,) + rows(count), bf16),
            shape((chunks + 1,) + rows(count), bf16),
            shape((2,) + tiles(wider), f32),
            shape((2,) + tiles(count), f32),
            shape((chunks,) + tiles(count), f32),
            shape((chunks,) + rows(count), bf16),
            shape((chunks,) + rows(count), bf16),
            shape((chunks,) + rows(count), bf16),
            shape((chunks,) + rows(count), bf16),
            shape((chunks,) + tiles(TABLE), f32),
            shape((chunks,) + tiles(TABLE), f32),
            shape(half, f32),
            shape(half, f32),
            shape(tiles(4), f32),
        ),
        in_specs=[vmem] * 2 + [smem],
        out_specs=(vmem,) * 14,
        scratch_shapes=[
            pltpu.VMEM((chunks + 1,) + rows(wider), bf16),
            pltpu.VMEM((chunks + 1,) + rows(wider), bf16),
            pltpu.VMEM(tiles(count), f32),
            pltpu.VMEM(tiles(wider), f32),
            pltpu.VMEM(tiles(count), f32),
        ],
        compiler_params=params,
        cost_estimate=pl.CostEstimate(flops=10**10, bytes_accessed=0, transcendentals=0),
        name="inner",
    )(tall, matrices, stencil_weights)
    outer_image, outer_second, sums = pl.pallas_call(
        outer_kernel,
        out_shape=(shape(half, f32), shape(half, f32), shape((devices, LANES), f32)),
        in_specs=[vmem] * 4 + [smem] + [vmem] * 12,
        out_specs=(vmem,) * 3,
        scratch_shapes=[
            pltpu.VMEM(tiles(wider), f32),
            pltpu.VMEM(tiles(wider), f32),
            pltpu.VMEM(tiles(count), f32),
            pltpu.VMEM(tiles(wider), f32),
            pltpu.VMEM(tiles(count), f32),
            pltpu.VMEM(tiles(count), f32),
            pltpu.VMEM(tiles(count), f32),
            pltpu.VMEM(tiles(TABLE), f32),
            pltpu.VMEM(tiles(TABLE), f32),
            pltpu.VMEM(tiles(TABLE), f32),
            pltpu.VMEM((2,) + tiles(count), f32),
        ],
        compiler_params=params,
        name="outer",
    )(right, left, tall, matrices, stencil_weights, *kept, sums)
    sums = lax.all_to_all(sums, ("down", "cross"), 0, 0, tiled=True)
    solution_field, residual = pl.pallas_call(
        finish_kernel,
        out_shape=(shape(own.shape, f32), shape(own.shape, f32)),
        in_specs=[vmem] * 6,
        out_specs=(vmem, vmem),
        compiler_params=params,
        name="finish",
    )(sums, own, image, second, outer_image, outer_second)
    return solution_field.reshape(right_side.shape), residual.reshape(right_side.shape)


def solution(mesh):
    return jax.shard_map(
        per_device,
        mesh=mesh,
        in_specs=(
            P(None, None, "down", "cross"),
            P("down", "cross"),
            P(None, "down", "cross"),
            P(),
        ),
        out_specs=(P(None, None, "down", "cross"), P(None, None, "down", "cross")),
        check_vma=False,
    )
```

```python
import functools
import math

import jax
import jax.numpy as jnp
import numpy as np
from jax import lax
from jax.experimental import pallas as pl
from jax.experimental.pallas import tpu as pltpu
from jax.sharding import PartitionSpec as P

CZ = 32
VARS = 4
DEG = 3
TERMS = 5
COMPS = 3
MODES = 35
FIELDS = COMPS * MODES
STIFF = FIELDS + TERMS
ROWS = 4
LANES = 128
WIDE = 64


def multi_indices(count_left, budget_left):
    if count_left == 0:
        return [()]
    return [
        (leading,) + remainder
        for leading in range(budget_left + 1)
        for remainder in multi_indices(count_left - 1, budget_left - leading)
    ]


def chaos_terms():
    picked = sorted(
        multi_indices(VARS, DEG),
        key=lambda multi_index: (sum(multi_index),)
        + tuple((-entry_value for entry_value in multi_index)),
    )
    position = {multi_index: number for number, multi_index in enumerate(picked)}
    terms = [[] for mode in picked]
    for variable in range(VARS):
        for multi_index in picked:
            raised = list(multi_index)
            raised[variable] += 1
            raised = tuple(raised)
            if raised in position:
                degree = multi_index[variable]
                here, there = position[multi_index], position[raised]
                terms[here].append((variable, degree, there))
                terms[there].append((variable, degree, here))
    values = [(n + 1) / math.sqrt((2 * n + 1) * (2 * n + 3)) for n in range(DEG)]
    return terms, values


CHAOS, CHAOS_VALUES = chaos_terms()
TABLE = 1 + VARS * DEG


def tap_slots(y_in, y_out, reach):
    z = np.arange(CZ)
    y_in, z_in = np.repeat(y_in, CZ), np.tile(z, len(y_in))
    y_out, z_out = np.repeat(y_out, CZ), np.tile(z, len(y_out))
    dy = y_in[:, None] - y_out[None, :]
    dz = z_in[:, None] - z_out[None, :]
    near = (abs(dy) <= 1) & (abs(dz) <= 1) & np.repeat(np.repeat(reach, CZ, 0), CZ, 1)
    parts = []
    for dx in (0, 1, -1):
        linear = 9 * (dx + 1) + 3 * (dy + 1) + (dz + 1)
        slot = np.minimum(linear, 26 - linear)
        parts.append(np.where(near & (linear != 13), slot, 13))
    return np.concatenate(parts, axis=1).astype(np.int32)


def chunk_slots():
    y_in = np.array([0, 1, 2, 3, 4, 5, -2, -1])
    return tap_slots(y_in, np.arange(4), np.ones((8, 4), bool))


def rim_slots():
    far = 100
    y_in = np.array([16, 17, -2 - far, -1 - far, -far, 1 - far, 14, 15])
    y_out = np.array([15, 16, -1 - far, -far])
    reach = np.ones((8, 4), bool)
    reach[4:, 0] = False
    reach[4:, 3] = False
    return tap_slots(y_in, y_out, reach)


SLOTS = np.stack([chunk_slots(), rim_slots()])


def matrix_kernel(weights_ref, slots_ref, matrix_ref):
    slots = slots_ref[0]
    full = jnp.zeros(slots.shape, jnp.float32)
    for number in range(13):
        full = jnp.where(slots == number, 0.5 * weights_ref[number], full)
    high = full.astype(jnp.bfloat16)
    low = (full - high.astype(jnp.float32)).astype(jnp.bfloat16)
    rows = slots.shape[0]
    matrix_ref[0, :rows] = high
    matrix_ref[0, rows : 2 * rows] = high
    matrix_ref[0, 2 * rows :] = low


def mix(table, load, mode, total):
    for variable, degree, other in CHAOS[mode]:
        total = total + table[1 + variable * DEG + degree] * load(other)
    return total


def window(own, after, before):
    left = lax.broadcasted_iota(jnp.int32, own[0].shape, 1) < WIDE
    high, low = [jnp.where(left, ahead, behind) for ahead, behind in zip(after, before)]
    return jnp.concatenate([own[0], high, own[1], low, own[0], high], axis=1)


def stencil(own, after, before, matrix, out):
    parts = jnp.dot(
        window(own, after, before), matrix[...], preferred_element_type=jnp.float32
    )
    shape = out.shape
    centre = parts[:, :LANES].reshape(shape)
    ahead = parts[:, LANES : 2 * LANES].reshape(shape)
    behind = parts[:, 2 * LANES :].reshape(shape)
    out[...] = centre + pltpu.roll(ahead, 7, 1) + pltpu.roll(behind, 1, 1)


def halves(value):
    value = value.reshape(value.shape[0] * 8, LANES)
    high = value.astype(jnp.bfloat16)
    return high, (value - high.astype(jnp.float32)).astype(jnp.bfloat16)


def paired_mixes(first, second, lead):
    left = lax.broadcasted_iota(jnp.int32, (8, LANES), 1) < WIDE
    turned, other = pltpu.roll(first, 4, 1), pltpu.roll(second, 4, 1)
    return (
        jnp.where(left, jnp.where(lead, turned, other), jnp.where(lead, 0.0, turned)),
        jnp.where(left, jnp.where(lead, other, 0.0), jnp.where(lead, turned, other)),
    )


def paired_stencil(pairs, lead, matrix, store):
    mixes = paired_mixes(pairs[0], pairs[1], lead)
    for number, (pair, beside) in enumerate(zip(pairs, mixes)):
        own, near = halves(pair), halves(beside)
        lines = jnp.concatenate([own[0], near[0], own[1], near[1], own[0], near[0]], axis=1)
        parts = jnp.dot(lines, matrix[...], preferred_element_type=jnp.float32)
        parts = [
            parts[:, n * LANES : (n + 1) * LANES].reshape(pair.shape) for n in range(3)
        ]
        for chunk, mask, turns in ((2 * number, lead, (0, 7, 1)), (2 * number + 1, ~lead, (4, 3, 5))):
            terms = [
                pltpu.roll(value, turn, 1) if turn else value
                for value, turn in zip([jnp.where(mask, part, 0.0) for part in parts], turns)
            ]
            store(chunk, terms[0] + terms[1] + terms[2])


def fill(table, values):
    table[0] = values[0]
    for variable in range(VARS):
        for degree in range(DEG):
            table[1 + variable * DEG + degree] = values[1 + variable] * CHAOS_VALUES[degree]


def load_table(table):
    return [table[entry] for entry in range(TABLE)]


def grow(field, table, out):
    table = load_table(table)

    @pl.loop(0, COMPS)
    def each(comp):
        base = comp * MODES
        for mode in range(MODES):
            load = lambda other: field(base + other)
            out[base + mode] = mix(table, load, mode, table[0] * load(mode))


def apply(field, near, grown_near, coef, diag, stiff, store):
    coef, diag = load_table(coef), load_table(diag)

    def each(comp, carry):
        base = comp * MODES
        for mode in range(MODES):
            load = lambda other: field(base + other)
            close = lambda other: near[base + other]
            value = mix(diag, load, mode, (stiff + diag[0]) * load(mode))
            value = value - mix(
                coef, close, mode, coef[0] * close(mode) + grown_near[base + mode]
            )
            carry = store(base + mode, value, carry)
        return carry

    return each


def finish_chunk(start, image, near, grown_near, coef, diag, stiff, image_out, second_out, lanes, sums):
    def store(number, value, sums):
        rr, rq, qq, qz = sums
        first, here = start(number), image(number)
        image_out[number, :, lanes] = here[:ROWS]
        second_out[number, :, lanes] = value[:ROWS]
        return rr + first * first, rq + first * here, qq + here * here, qz + here * value

    return lax.fori_loop(0, COMPS, apply(image, near, grown_near, coef, diag, stiff, store), sums)


def fill_diag(table, field, near, weights_ref):
    weight_sum = sum(weights_ref[number] for number in range(13))
    fill(table, [field(FIELDS + t) * weight_sum + near[FIELDS + t] for t in range(TERMS)])


def chunk_of(ref, k):
    lanes = pl.ds(pl.multiple_of(k * LANES, LANES), LANES)
    return lambda number: ref[number, :, lanes]


def entry_of(ref):
    return lambda number: ref[number]


def grow_pairs(pairs, grown):
    for number in range(2):
        field = entry_of(pairs.at[number])
        table = [field(FIELDS + term) for term in range(TERMS)]
        table = [table[0]] + [
            table[1 + variable] * CHAOS_VALUES[degree]
            for variable in range(VARS)
            for degree in range(DEG)
        ]
        grow(field, table, grown.at[number])
        grown[number, FIELDS] = jnp.zeros((8, LANES), jnp.float32)


def start_kernel(own_ref, extra_ref, matrix_ref, near_ref, grown_near_ref, grown_ref, pairs):
    for number in range(2):
        for side in range(2):
            lanes, rows = pl.ds((2 * number + side) * LANES, LANES), pl.ds(side * ROWS, ROWS)
            pairs[number, :FIELDS, rows, :] = own_ref[:, :, lanes]
            pairs[number, FIELDS : STIFF + 1, rows, :] = extra_ref[:, :, lanes]
        pairs[number, STIFF + 1] = jnp.zeros((8, LANES), jnp.float32)
    grow_pairs(pairs, grown_ref)
    lead = lax.broadcasted_iota(jnp.int32, (8, LANES), 0) < ROWS
    for ref, out in ((pairs, near_ref), (grown_ref, grown_near_ref)):

        def store(chunk, value):
            out[chunk] = value

        paired_stencil([ref[0], ref[1]], lead, matrix_ref.at[0], store)


def inner_kernel(
    tall_ref, matrix_ref, weights_ref, own_near, own_grown_near,
    halo_grown, outer_near, outer_grown_near,
    image, image_high, image_low, image_grown_high, image_grown_low, coef_table, diag_table,
    image_ref, second_ref, sums_ref,
    pairs, grown, near, grown_near,
):
    chunks = image.shape[0]
    final = chunks - 1
    for k in range(chunks):
        image[k, FIELDS] = jnp.zeros((8, LANES), jnp.float32)
    grown[FIELDS] = jnp.zeros((8, LANES), jnp.float32)
    lead = lax.broadcasted_iota(jnp.int32, (8, LANES), 0) >= ROWS
    for number in range(2):
        one, other = [tall_ref[:, :, pl.ds((2 * number + n) * LANES, LANES)] for n in range(2)]
        pairs[number] = jnp.where(lead, one, pltpu.roll(other, ROWS, 1))
    grow_pairs(pairs, halo_grown)
    for ref, before, out in ((pairs, own_near, near), (halo_grown, own_grown_near, grown_near)):

        def store(chunk, value):
            out[chunk] = before[chunk] + value

        paired_stencil([ref[0], ref[1]], lead, matrix_ref.at[0], store)
    for side, k in enumerate((0, final)):
        outer_near[side] = near[k]
        outer_grown_near[side] = grown_near[k]

    @pl.loop(0, chunks)
    def first(k):
        field = chunk_of(tall_ref, k)
        fill(coef_table.at[k], [field(FIELDS + term) for term in range(TERMS)])
        fill_diag(diag_table.at[k], field, near.at[k], weights_ref)
        stiff = field(STIFF)
        inside = stiff > 0.0

        def store(number, value, carry):
            image[k, number] = jnp.where(inside, value, 0.0)
            return carry

        lax.fori_loop(
            0,
            COMPS,
            apply(
                field, near.at[k], grown_near.at[k], coef_table.at[k], diag_table.at[k], stiff, store
            ),
            0,
        )

    @pl.loop(0, chunks)
    def grow_image(k):
        grow(entry_of(image.at[k]), coef_table.at[k], grown)
        image_grown_high[k], image_grown_low[k] = halves(grown[...])
        image_high[k], image_low[k] = halves(image[k])

    image_near, image_grown_near = near.at[0, pl.ds(0, FIELDS + 1)], grown_near.at[0]
    zero = jnp.zeros((8, LANES), jnp.float32)

    def second(k, sums):
        for high, low, out in (
            (image_high, image_low, image_near),
            (image_grown_high, image_grown_low, image_grown_near),
        ):
            stencil(*[(high[at], low[at]) for at in (k, k + 1, k - 1)], matrix_ref.at[0], out)
        field = chunk_of(tall_ref, k)
        lanes = pl.ds(pl.multiple_of((k - 1) * LANES, LANES), LANES)
        return finish_chunk(
            field, entry_of(image.at[k]), image_near, image_grown_near, coef_table.at[k], diag_table.at[k],
            field(STIFF), image_ref, second_ref, lanes, sums,
        )

    sums = lax.fori_loop(1, chunks - 1, second, (zero, zero, zero, zero))
    for number, value in enumerate(sums):
        sums_ref[number] = value


def outer_kernel(
    edge, tall_ref, matrix_ref, weights_ref,
    own_grown, halo_grown, outer_near, outer_grown_near,
    image, image_high, image_low, image_grown_high, image_grown_low, coef_table, diag_table, before_ref,
    image_ref, second_ref, sums_ref,
    rim, grown, near, grown_near, rim_image, edge_image, coef, diag, edge_coef, ends,
):
    final = image.shape[0] - 1
    first_field, last_field = chunk_of(tall_ref, 0), chunk_of(tall_ref, final)
    lane = lax.broadcasted_iota(jnp.int32, (8, LANES), 1)
    zero = jnp.zeros((8, LANES), jnp.float32)
    grown[FIELDS] = zero
    rim_image[FIELDS] = zero
    for side in range(2):
        ends[side, FIELDS] = zero
    edge_image[FIELDS] = zero

    def to_rim(last, beyond, begin):
        right = pltpu.roll(jnp.where(lane >= 3 * CZ, last, beyond), CZ, last.ndim - 1)
        left = pltpu.roll(jnp.where(lane < CZ, begin, beyond), LANES - CZ, last.ndim - 1)
        return jnp.where(lane < WIDE, right, left)

    fill(edge_coef, [edge[FIELDS + term] for term in range(TERMS)])
    grow(entry_of(edge), edge_coef, grown)
    top = lax.broadcasted_iota(jnp.int32, (8, LANES), 0) < ROWS
    edge_parts = halves(edge[...])
    begin, last = halves(first_field(slice(None))), halves(last_field(slice(None)))
    stencil(edge_parts, begin, last, matrix_ref.at[1], near)
    stencil(
        halves(grown[...]),
        halves(jnp.where(top, own_grown[0], halo_grown[0])),
        halves(pltpu.roll(jnp.where(top, halo_grown[1], own_grown[1]), ROWS, 1)),
        matrix_ref.at[1],
        grown_near,
    )
    left_rim, right_rim = lane >= 3 * CZ, lane < CZ

    def own_part(last, begin):
        moved = jnp.where(right_rim, pltpu.roll(last, CZ, last.ndim - 1), 0.0)
        return jnp.where(left_rim, pltpu.roll(begin, LANES - CZ, last.ndim - 1), moved)

    near[...] = near[...] + own_part(outer_near[1], outer_near[0])
    grown_near[...] = grown_near[...] + own_part(outer_grown_near[1], outer_grown_near[0])
    rim[...] = to_rim(last_field(slice(None)), edge[...], first_field(slice(None)))
    fill(coef, [rim[FIELDS + term] for term in range(TERMS)])
    fill_diag(diag, entry_of(rim), near, weights_ref)
    stiff = rim[STIFF]
    inside = stiff > 0.0

    def store(number, value, carry):
        rim_image[number] = jnp.where(inside, value, 0.0)
        return carry

    lax.fori_loop(0, COMPS, apply(entry_of(rim), near, grown_near, coef, diag, stiff, store), 0)
    grow(entry_of(rim_image), coef, grown)

    def from_rim(value):
        return pltpu.roll(value, CZ, value.ndim - 1), pltpu.roll(value, LANES - CZ, value.ndim - 1)

    def placed(begin, last, value):
        to_left, to_right = from_rim(value)
        return (
            jnp.where(lane < CZ, to_left, begin),
            jnp.where(lane >= 3 * CZ, to_right, last),
            jnp.where(lane < WIDE, to_right, to_left),
        )

    ends[0], ends[1], edge_image[...] = placed(image[0], image[final], rim_image[...])
    image_parts = [halves(ends[0]), halves(ends[1]), halves(edge_image[...])]

    def joined(ref_high, ref_low, k):
        return (ref_high[k].astype(jnp.float32) + ref_low[k].astype(jnp.float32)).reshape(
            grown.shape
        )

    grown_parts = [
        halves(value)
        for value in placed(
            joined(image_grown_high, image_grown_low, 0),
            joined(image_grown_high, image_grown_low, final),
            grown[...],
        )
    ]
    for entry in range(TABLE):
        to_left, to_right = from_rim(diag[entry])
        edge_coef[entry] = jnp.where(lane < CZ, to_left, diag_table[0, entry])
        coef[entry] = jnp.where(lane >= 3 * CZ, to_right, diag_table[final, entry])
    image_near = near.at[pl.ds(0, FIELDS + 1)]
    sums = tuple(before_ref[number] for number in range(4))
    for side, k, table, field in ((0, 0, edge_coef, first_field), (1, final, coef, last_field)):
        for (begin, last, beyond), high, low, out in (
            (image_parts, image_high, image_low, image_near),
            (grown_parts, image_grown_high, image_grown_low, grown_near),
        ):
            if side == 0:
                chunk = (begin, (high[1], low[1]), beyond)
            else:
                chunk = (last, beyond, (high[final - 1], low[final - 1]))
            stencil(*chunk, matrix_ref.at[0], out)
        sums = finish_chunk(
            field, entry_of(ends.at[side]), image_near, grown_near, coef_table.at[k], table,
            field(STIFF), image_ref, second_ref, pl.ds(side * LANES, LANES), sums,
        )
    inner = lax.broadcasted_iota(jnp.int32, (8, LANES), 0) < ROWS
    column = lax.broadcasted_iota(jnp.int32, sums_ref.shape, 1)
    row = jnp.zeros(sums_ref.shape, jnp.float32)
    for number, value in enumerate(sums):
        row = jnp.where(column == number, jnp.sum(jnp.where(inner, value, 0.0)), row)
    sums_ref[...] = row


def finish_kernel(sums_ref, start_ref, *refs):
    *parts, field_ref, residual_ref = refs
    total = jnp.sum(sums_ref[...], axis=0, keepdims=True)
    lane = lax.broadcasted_iota(jnp.int32, total.shape, 1)
    rr, rq, qq, qz = [
        jnp.sum(jnp.where(lane == number, total, 0.0), axis=1, keepdims=True)[None]
        for number in range(4)
    ]
    step = rr / rq
    fresh = rr - 2.0 * step * rq + step * step * qq
    grow = 1.0 + fresh / rr
    curvature = grow * grow * rq - 2.0 * grow * step * qq + step * step * qz
    later = fresh / curvature
    both = step + later * grow
    cross = later * step
    inner, outer = parts[:2], parts[2:]
    columns = start_ref.shape[2]
    for (image_ref, second_ref), source, at, width in (
        (outer, 0, 0, LANES),
        (inner, 0, LANES, columns - 2 * LANES),
        (outer, LANES, columns - LANES, LANES),
    ):
        there, here = pl.ds(source, width), pl.ds(at, width)
        start, image, second = start_ref[:, :, here], image_ref[:, :, there], second_ref[:, :, there]
        field_ref[:, :, here] = both * start - cross * image
        residual_ref[:, :, here] = start - both * image + cross * second


def shift(value, axis, by):
    size = lax.axis_size(axis)
    return lax.ppermute(value, axis, [(i, i + by) for i in range(size) if 0 <= i + by < size])


def swap(value, axis, begin):
    size = lax.axis_size(axis)
    pairs = [(i, i + 1) for i in range(begin, size - 1, 2)]
    return lax.ppermute(value, axis, pairs + [(j, i) for i, j in pairs])


def per_device(right_side, stiffness, coefficients, stencil_weights):
    columns = right_side.shape[3]
    chunks = columns // LANES
    devices = lax.axis_size("down") * lax.axis_size("cross")
    own = right_side.reshape(FIELDS, ROWS, columns)
    extra = jnp.concatenate([coefficients, stiffness[None]], axis=0)
    spare = jnp.zeros((1, ROWS, columns), jnp.float32)
    all_fields = jnp.concatenate([own, extra, spare], axis=0)
    even = lax.axis_index("down") % 2 == 0
    head, tail = all_fields[: STIFF + 1, :2], all_fields[: STIFF + 1, ROWS - 2 :]
    one = swap(jnp.where(even, tail, head), "down", 0)
    other = swap(jnp.where(even, head, tail), "down", 1)
    upper, lower = jnp.where(even, one, other), jnp.where(even, other, one)
    beyond = jnp.concatenate([upper, lower], axis=1)
    beyond = jnp.concatenate([beyond, spare], axis=0)
    tall = jnp.concatenate([all_fields, beyond], axis=1)
    even = lax.axis_index("cross") % 2 == 0
    head, tail = tall[: STIFF + 1, :, :WIDE], tall[: STIFF + 1, :, columns - WIDE :]
    one = swap(jnp.where(even, tail, head), "cross", 0)
    other = swap(jnp.where(even, head, tail), "cross", 1)
    right, left = jnp.where(even, one, other), jnp.where(even, other, one)
    edge = jnp.concatenate([right, left], axis=2)
    edge = jnp.concatenate([edge, jnp.zeros((1,) + edge.shape[1:], jnp.float32)], axis=0)
    vmem = pl.BlockSpec(memory_space=pltpu.VMEM)
    smem = pl.BlockSpec(memory_space=pltpu.SMEM)
    f32, bf16 = jnp.float32, jnp.bfloat16
    params = pltpu.CompilerParams(vmem_limit_bytes=32 * 1024 * 1024)
    matrices = pl.pallas_call(
        matrix_kernel,
        grid=(2,),
        out_shape=jax.ShapeDtypeStruct((2, 3 * SLOTS.shape[1], SLOTS.shape[2]), bf16),
        in_specs=[smem, pl.BlockSpec((1,) + SLOTS.shape[1:], lambda i: (i, 0, 0))],
        out_specs=pl.BlockSpec((1, 3 * SLOTS.shape[1], SLOTS.shape[2]), lambda i: (i, 0, 0)),
        name="matrix",
    )(stencil_weights, jnp.asarray(SLOTS))
    shape = jax.ShapeDtypeStruct
    count, wider = FIELDS + 1, STIFF + 2
    tiles = lambda number: (number, 8, LANES)
    rows = lambda number: (number * 8, LANES)
    half = (FIELDS, ROWS, columns // 2)
    own_near, own_grown_near, own_grown = pl.pallas_call(
        start_kernel,
        out_shape=(
            shape((chunks,) + tiles(wider), f32),
            shape((chunks,) + tiles(count), f32),
            shape((2,) + tiles(count), f32),
        ),
        in_specs=[vmem] * 3,
        out_specs=(vmem,) * 3,
        scratch_shapes=[pltpu.VMEM((2,) + tiles(wider), f32)],
        compiler_params=params,
        cost_estimate=pl.CostEstimate(flops=5 * 10**9, bytes_accessed=0, transcendentals=0),
        name="start",
    )(own, extra, matrices)
    halo_grown, *kept, image, second, sums = pl.pallas_call(
        inner_kernel,
        out_shape=(
            shape((2,) + tiles(count), f32),
            shape((2,) + tiles(wider), f32),
            shape((2,) + tiles(count), f32),
            shape((chunks,) + tiles(count), f32),
            shape((chunks,) + rows(count), bf16),
            shape((chunks,) + rows(count), bf16),
            shape((chunks,) + rows(count), bf16),
            shape((chunks,) + rows(count), bf16),
            shape((chunks,) + tiles(TABLE), f32),
            shape((chunks,) + tiles(TABLE), f32),
            shape(half, f32),
            shape(half, f32),
            shape(tiles(4), f32),
        ),
        in_specs=[vmem] * 2 + [smem] + [vmem] * 2,
        out_specs=(vmem,) * 13,
        scratch_shapes=[
            pltpu.VMEM((2,) + tiles(wider), f32),
            pltpu.VMEM(tiles(count), f32),
            pltpu.VMEM((chunks,) + tiles(wider), f32),
            pltpu.VMEM((chunks,) + tiles(count), f32),
        ],
        compiler_params=params,
        cost_estimate=pl.CostEstimate(flops=10**10, bytes_accessed=0, transcendentals=0),
        name="inner",
    )(tall, matrices, stencil_weights, own_near, own_grown_near)
    outer_image, outer_second, sums = pl.pallas_call(
        outer_kernel,
        out_shape=(shape(half, f32), shape(half, f32), shape((devices, LANES), f32)),
        in_specs=[vmem] * 3 + [smem] + [vmem] * 12,
        out_specs=(vmem,) * 3,
        scratch_shapes=[
            pltpu.VMEM(tiles(wider), f32),
            pltpu.VMEM(tiles(count), f32),
            pltpu.VMEM(tiles(wider), f32),
            pltpu.VMEM(tiles(count), f32),
            pltpu.VMEM(tiles(count), f32),
            pltpu.VMEM(tiles(count), f32),
            pltpu.VMEM(tiles(TABLE), f32),
            pltpu.VMEM(tiles(TABLE), f32),
            pltpu.VMEM(tiles(TABLE), f32),
            pltpu.VMEM((2,) + tiles(count), f32),
        ],
        compiler_params=params,
        name="outer",
    )(edge, tall, matrices, stencil_weights, own_grown, halo_grown, *kept, sums)
    sums = lax.all_to_all(sums, ("down", "cross"), 0, 0, tiled=True)
    solution_field, residual = pl.pallas_call(
        finish_kernel,
        out_shape=(shape(own.shape, f32), shape(own.shape, f32)),
        in_specs=[vmem] * 6,
        out_specs=(vmem, vmem),
        compiler_params=params,
        name="finish",
    )(sums, own, image, second, outer_image, outer_second)
    return solution_field.reshape(right_side.shape), residual.reshape(right_side.shape)


def solution(mesh):
    return jax.shard_map(
        per_device,
        mesh=mesh,
        in_specs=(
            P(None, None, "down", "cross"),
            P("down", "cross"),
            P(None, "down", "cross"),
            P(),
        ),
        out_specs=(P(None, None, "down", "cross"), P(None, None, "down", "cross")),
        check_vma=False,
    )
```

```python
import functools
import math

import jax
import jax.numpy as jnp
import numpy as np
from jax import lax
from jax.experimental import pallas as pl
from jax.experimental.pallas import tpu as pltpu
from jax.sharding import PartitionSpec as P

CZ = 32
VARS = 4
DEG = 3
TERMS = 5
COMPS = 3
MODES = 35
FIELDS = COMPS * MODES
STIFF = FIELDS + TERMS
ROWS = 4
LANES = 128
WIDE = 64


def multi_indices(count_left, budget_left):
    if count_left == 0:
        return [()]
    return [
        (leading,) + remainder
        for leading in range(budget_left + 1)
        for remainder in multi_indices(count_left - 1, budget_left - leading)
    ]


def chaos_terms():
    picked = sorted(
        multi_indices(VARS, DEG),
        key=lambda multi_index: (sum(multi_index),)
        + tuple((-entry_value for entry_value in multi_index)),
    )
    position = {multi_index: number for number, multi_index in enumerate(picked)}
    terms = [[] for mode in picked]
    for variable in range(VARS):
        for multi_index in picked:
            raised = list(multi_index)
            raised[variable] += 1
            raised = tuple(raised)
            if raised in position:
                degree = multi_index[variable]
                here, there = position[multi_index], position[raised]
                terms[here].append((variable, degree, there))
                terms[there].append((variable, degree, here))
    values = [(n + 1) / math.sqrt((2 * n + 1) * (2 * n + 3)) for n in range(DEG)]
    return terms, values


CHAOS, CHAOS_VALUES = chaos_terms()
TABLE = 1 + VARS * DEG


def tap_slots(y_in, y_out, reach):
    z = np.arange(CZ)
    y_in, z_in = np.repeat(y_in, CZ), np.tile(z, len(y_in))
    y_out, z_out = np.repeat(y_out, CZ), np.tile(z, len(y_out))
    dy = y_in[:, None] - y_out[None, :]
    dz = z_in[:, None] - z_out[None, :]
    near = (abs(dy) <= 1) & (abs(dz) <= 1) & np.repeat(np.repeat(reach, CZ, 0), CZ, 1)
    parts = []
    for dx in (0, 1, -1):
        linear = 9 * (dx + 1) + 3 * (dy + 1) + (dz + 1)
        slot = np.minimum(linear, 26 - linear)
        parts.append(np.where(near & (linear != 13), slot, 13))
    return np.concatenate(parts, axis=1).astype(np.int32)


def chunk_slots():
    y_in = np.array([0, 1, 2, 3, 4, 5, -2, -1])
    return tap_slots(y_in, np.arange(4), np.ones((8, 4), bool))


def rim_slots():
    far = 100
    y_in = np.array([16, 17, -2 - far, -1 - far, -far, 1 - far, 14, 15])
    y_out = np.array([15, 16, -1 - far, -far])
    reach = np.ones((8, 4), bool)
    reach[4:, 0] = False
    reach[4:, 3] = False
    return tap_slots(y_in, y_out, reach)


SLOTS = np.stack([chunk_slots(), rim_slots()])


def matrix_kernel(weights_ref, slots_ref, matrix_ref):
    slots = slots_ref[0]
    full = jnp.zeros(slots.shape, jnp.float32)
    for number in range(13):
        full = jnp.where(slots == number, 0.5 * weights_ref[number], full)
    high = full.astype(jnp.bfloat16)
    low = (full - high.astype(jnp.float32)).astype(jnp.bfloat16)
    rows = slots.shape[0]
    matrix_ref[0, :rows] = high
    matrix_ref[0, rows : 2 * rows] = high
    matrix_ref[0, 2 * rows :] = low


def mix(table, load, mode, total):
    for variable, degree, other in CHAOS[mode]:
        total = total + table[1 + variable * DEG + degree] * load(other)
    return total


PAIRS = ((0, 3), (1, 2))
OUTER, INNER = 0, 1


def tile_row():
    return lax.broadcasted_iota(jnp.int32, (8, LANES), 0)


def tile_lane():
    return lax.broadcasted_iota(jnp.int32, (8, LANES), 1)


def beside_outer(inner, lead, ahead=0.0, behind=0.0):
    left = tile_lane() < WIDE
    return jnp.where(left, jnp.where(lead, inner, ahead), jnp.where(lead, behind, inner))


def beside_inner(outer, inner, lead):
    left = tile_lane() < WIDE
    turned = pltpu.roll(inner, ROWS, 1)
    return jnp.where(left, jnp.where(lead, turned, outer), jnp.where(lead, outer, turned))


def halves(value):
    value = value.reshape(value.shape[0] * 8, LANES)
    high = value.astype(jnp.bfloat16)
    return high, (value - high.astype(jnp.float32)).astype(jnp.bfloat16)


def stencil(own, beside, matrix):
    (high, low), (near_high, near_low) = halves(own), halves(beside)
    lines = jnp.concatenate([high, near_high, low, near_low, high, near_high], axis=1)
    parts = jnp.dot(lines, matrix, preferred_element_type=jnp.float32)
    return [
        parts[:, at : at + LANES].reshape(own.shape) for at in range(0, parts.shape[1], LANES)
    ]


def turned_parts(parts):
    return pltpu.roll(parts[-2], 7, 1), pltpu.roll(parts[-1], 1, 1)


def same_rows(parts):
    ahead, behind = turned_parts(parts)
    row = tile_row() % ROWS
    return parts[0] + jnp.where(row == ROWS - 1, 0.0, ahead) + jnp.where(row == 0, 0.0, behind)


def other_rows(parts):
    ahead, behind = turned_parts(parts)
    row = tile_row() % ROWS
    return jnp.where(row == ROWS - 1, ahead, jnp.where(row == 0, behind, 0.0))


def entry_of(ref):
    return lambda number: ref[number]


def coef_values(field):
    values = [field(FIELDS + term) for term in range(TERMS)]
    return spread_values(values)


def spread_values(values):
    return [values[0]] + [
        values[1 + variable] * CHAOS_VALUES[degree]
        for variable in range(VARS)
        for degree in range(DEG)
    ]


def diag_values(field, near, weights_ref):
    weight_sum = sum(weights_ref[number] for number in range(13))
    return spread_values(
        [field(FIELDS + term) * weight_sum + near(FIELDS + term) for term in range(TERMS)]
    )


def grow(field, table, out):
    @pl.loop(0, COMPS)
    def each(comp):
        base = comp * MODES
        for mode in range(MODES):
            load = lambda other: field(base + other)
            out[base + mode] = mix(table, load, mode, table[0] * load(mode))

    out[FIELDS] = jnp.zeros((8, LANES), jnp.float32)


def apply(field, near, grown_near, coef, diag, stiff, store, carry=0):
    def each(comp, carry):
        base = comp * MODES
        for mode in range(MODES):
            load = lambda other: field(base + other)
            close = lambda other: near(base + other)
            value = mix(diag, load, mode, (stiff + diag[0]) * load(mode))
            value = value - mix(
                coef, close, mode, coef[0] * close(mode) + grown_near(base + mode)
            )
            carry = store(base + mode, value, carry)
        return carry

    return lax.fori_loop(0, COMPS, each, carry)


def masked_store(out, inside):
    def store(number, value, carry):
        out[number] = jnp.where(inside, value, 0.0)
        return carry

    return store


def second_store(start, image, out):
    def store(number, value, sums):
        rr, rq, qq, qz = sums
        first, here = start(number), image(number)
        out[number] = value
        return rr + first * first, rq + first * here, qq + here * here, qz + here * value

    return store


def second_near(own, own_beside, halo, halo_beside, matrix_ref):
    own_parts = stencil(own, own_beside, matrix_ref[0])
    halo_parts = stencil(halo, halo_beside, matrix_ref[0, :, LANES:])
    return same_rows(own_parts) + other_rows(halo_parts)


def start_kernel(
    own_ref, extra_ref, matrix_ref, pairs, grown, near, halo_near, grown_near, halo_grown_near
):
    for number, chunks in enumerate(PAIRS):
        for side, chunk in enumerate(chunks):
            lanes, rows = pl.ds(chunk * LANES, LANES), pl.ds(side * ROWS, ROWS)
            pairs[number, :FIELDS, rows, :] = own_ref[:, :, lanes]
            pairs[number, FIELDS : STIFF + 1, rows, :] = extra_ref[:, :, lanes]
        pairs[number, STIFF + 1] = jnp.zeros((8, LANES), jnp.float32)
        field = entry_of(pairs.at[number])
        grow(field, coef_values(field), grown.at[number])
    lead = tile_row() < ROWS
    for ref, out, halo_out in ((pairs, near, halo_near), (grown, grown_near, halo_grown_near)):
        outer, inner = ref[OUTER], ref[INNER]
        for number, own, beside in (
            (OUTER, outer, beside_outer(inner, lead)),
            (INNER, inner, beside_inner(outer, inner, lead)),
        ):
            parts = stencil(own, beside, matrix_ref[0])
            out[number] = same_rows(parts)
            halo_out[number] = other_rows(parts)


def inner_kernel(
    beyond_ref, pairs, matrix_ref, weights_ref,
    before_near, before_halo_near, before_grown_near, before_halo_grown_near,
    halo, halo_grown, near, halo_near, grown_near, halo_grown_near,
    image, halo_image, image_grown, halo_image_grown, diag, second_ref, sums_ref,
):
    for number, (first, second) in enumerate(PAIRS):
        halo[number, :, ROWS:, :] = beyond_ref[:, :, pl.ds(first * LANES, LANES)]
        halo[number, :, :ROWS, :] = beyond_ref[:, :, pl.ds(second * LANES, LANES)]
        field = entry_of(halo.at[number])
        grow(field, coef_values(field), halo_grown.at[number])
    lead = tile_row() >= ROWS
    for ref, before, before_halo, out, halo_out in (
        (halo, before_near, before_halo_near, near, halo_near),
        (halo_grown, before_grown_near, before_halo_grown_near, grown_near, halo_grown_near),
    ):
        outer, inner = ref[OUTER], ref[INNER]
        for number, own, beside in (
            (OUTER, outer, beside_outer(inner, lead)),
            (INNER, inner, beside_inner(outer, inner, lead)),
        ):
            parts = stencil(own, beside, matrix_ref[0])
            halo_out[number] = before_halo[number] + same_rows(parts)
            out[number] = before[number] + other_rows(parts)

    for ref, close, grown_close, out, out_grown in (
        (pairs, near, grown_near, image, image_grown),
        (halo, halo_near, halo_grown_near, halo_image, halo_image_grown),
    ):

        @pl.loop(0, len(PAIRS))
        def each(number):
            field, around = entry_of(ref.at[number]), entry_of(close.at[number])
            coef = coef_values(field)
            values = diag_values(field, around, weights_ref)
            if ref is pairs:
                for entry, value in enumerate(values):
                    diag[number, entry] = value
            stiff = field(STIFF)
            target = out.at[number]
            apply(
                field, around, entry_of(grown_close.at[number]), coef, values, stiff,
                masked_store(target, stiff > 0.0),
            )
            target[FIELDS] = jnp.zeros((8, LANES), jnp.float32)
            grow(entry_of(target), coef, out_grown.at[number])

    own_lead = tile_row() < ROWS
    image_near, image_grown_near = near.at[INNER, pl.ds(0, FIELDS + 1)], grown_near.at[INNER]
    for own, far, out in (
        (image, halo_image, image_near),
        (image_grown, halo_image_grown, image_grown_near),
    ):
        out[...] = second_near(
            own[INNER],
            beside_inner(own[OUTER], own[INNER], own_lead),
            far[INNER],
            beside_inner(far[OUTER], far[INNER], lead),
            matrix_ref,
        )
    field, here = entry_of(pairs.at[INNER]), entry_of(image.at[INNER])
    zero = jnp.zeros((8, LANES), jnp.float32)
    sums = apply(
        here, entry_of(image_near), entry_of(image_grown_near), coef_values(field),
        [diag[INNER, entry] for entry in range(TABLE)], field(STIFF),
        second_store(field, here, second_ref), (zero, zero, zero, zero),
    )
    for number, value in enumerate(sums):
        sums_ref[number] = value


def outer_kernel(
    edge, pairs, halo, matrix_ref, weights_ref, own_grown, halo_grown,
    near, halo_near, grown_near, halo_grown_near,
    image, halo_image, image_grown, halo_image_grown, diag, before_ref,
    image_ref, second_ref, sums_ref,
    rim, grown, rim_near, rim_grown_near, rim_image,
):
    lane, top = tile_lane(), tile_row() < ROWS
    bottom = ~top
    left = lane < WIDE

    def first_chunk(own, far):
        return jnp.where(top, own, far)

    def last_chunk(own, far):
        return pltpu.roll(jnp.where(top, far, own), ROWS, own.ndim - 2)

    def to_rim(last, beyond, begin):
        right = pltpu.roll(jnp.where(lane >= 3 * CZ, last, beyond), CZ, 2)
        return jnp.where(
            left, right, pltpu.roll(jnp.where(lane < CZ, begin, beyond), LANES - CZ, 2)
        )

    def rim_stencil(around, own, far, own_near, far_near):
        beside = jnp.where(left, first_chunk(own, far), last_chunk(own, far))
        parts = stencil(around, beside, matrix_ref[1])
        ahead, behind = turned_parts(parts)
        begin = first_chunk(own_near, far_near)
        last = last_chunk(own_near, far_near)
        return parts[0] + ahead + behind + to_rim(last, jnp.zeros_like(last), begin)

    field = entry_of(edge)
    grow(field, coef_values(field), grown)
    rim_near[...] = rim_stencil(
        edge[...], pairs[OUTER], halo[OUTER], near[OUTER], halo_near[OUTER]
    )
    rim_grown_near[...] = rim_stencil(
        grown[...], own_grown[OUTER], halo_grown[OUTER], grown_near[OUTER], halo_grown_near[OUTER]
    )
    rim[...] = to_rim(
        last_chunk(pairs[OUTER], halo[OUTER]), edge[...], first_chunk(pairs[OUTER], halo[OUTER])
    )
    field, around = entry_of(rim), entry_of(rim_near)
    coef, rim_diag = coef_values(field), diag_values(field, around, weights_ref)
    stiff = field(STIFF)
    apply(
        field, around, entry_of(rim_grown_near), coef, rim_diag, stiff,
        masked_store(rim_image, stiff > 0.0),
    )
    rim_image[FIELDS] = jnp.zeros((8, LANES), jnp.float32)
    grow(entry_of(rim_image), coef, grown)

    def from_rim(value):
        last = pltpu.roll(value, LANES - CZ, value.ndim - 1)
        return pltpu.roll(value, CZ, value.ndim - 1), pltpu.roll(last, ROWS, value.ndim - 2)

    def placed(lead, begin, last, value):
        value = jnp.where(lead & (lane < CZ), begin, value)
        return jnp.where(~lead & (lane >= 3 * CZ), last, value)

    image_near, image_grown_near = rim_near.at[pl.ds(0, FIELDS + 1)], rim_grown_near
    for value, own, far, out, keep in (
        (rim_image, image, halo_image, image_near, True),
        (grown, image_grown, halo_image_grown, image_grown_near, False),
    ):
        begin, last = from_rim(value[...])
        here = placed(top, begin, last, own[OUTER])
        if keep:
            image_ref[...] = here
        out[...] = second_near(
            here,
            beside_outer(own[INNER], top, last, begin),
            placed(bottom, begin, last, far[OUTER]),
            beside_outer(far[INNER], bottom, last, begin),
            matrix_ref,
        )
    values = []
    for entry in range(TABLE):
        begin, last = from_rim(rim_diag[entry])
        values.append(placed(top, begin, last, diag[OUTER, entry]))
    field, here = entry_of(pairs.at[OUTER]), entry_of(image_ref)
    sums = apply(
        here, entry_of(image_near), entry_of(image_grown_near), coef_values(field), values,
        field(STIFF), second_store(field, here, second_ref),
        tuple(before_ref[number] for number in range(4)),
    )
    column = lax.broadcasted_iota(jnp.int32, sums_ref.shape, 1)
    row = jnp.zeros(sums_ref.shape, jnp.float32)
    for number, value in enumerate(sums):
        row = jnp.where(column == number, jnp.sum(value), row)
    sums_ref[...] = row


FINISH_STEPS = 5


def finish_kernel(
    sums_ref, pairs, images, inner_second, outer_image, outer_second, field_ref, residual_ref
):
    total = jnp.sum(sums_ref[...], axis=0, keepdims=True)
    lane = lax.broadcasted_iota(jnp.int32, total.shape, 1)
    rr, rq, qq, qz = [
        jnp.sum(jnp.where(lane == number, total, 0.0), axis=1, keepdims=True)[None]
        for number in range(4)
    ]
    step = rr / rq
    fresh = rr - 2.0 * step * rq + step * step * qq
    larger = 1.0 + fresh / rr
    curvature = larger * larger * rq - 2.0 * larger * step * qq + step * step * qz
    later = fresh / curvature
    both = step + later * larger
    cross = later * step
    here = pl.ds(pl.program_id(0) * field_ref.shape[0], field_ref.shape[0])
    for number, image_ref, second_ref in (
        (OUTER, outer_image, outer_second),
        (INNER, images.at[INNER], inner_second),
    ):
        start, image, second = pairs[number, here], image_ref[here], second_ref[here]
        field = both * start - cross * image
        residual = start - both * image + cross * second
        for side, chunk in enumerate(PAIRS[number]):
            lanes, rows = pl.ds(chunk * LANES, LANES), slice(side * ROWS, (side + 1) * ROWS)
            field_ref[:, :, lanes] = field[:, rows]
            residual_ref[:, :, lanes] = residual[:, rows]


def swap(value, axis, begin):
    size = lax.axis_size(axis)
    pairs = [(i, i + 1) for i in range(begin, size - 1, 2)]
    return lax.ppermute(value, axis, pairs + [(j, i) for i, j in pairs])


def per_device(right_side, stiffness, coefficients, stencil_weights):
    columns = right_side.shape[3]
    devices = lax.axis_size("down") * lax.axis_size("cross")
    own = right_side.reshape(FIELDS, ROWS, columns)
    extra = jnp.concatenate([coefficients, stiffness[None]], axis=0)
    all_fields = jnp.concatenate([own, extra], axis=0)
    even = lax.axis_index("down") % 2 == 0
    head, tail = all_fields[:, :2], all_fields[:, ROWS - 2 :]
    one = swap(jnp.where(even, tail, head), "down", 0)
    other = swap(jnp.where(even, head, tail), "down", 1)
    upper, lower = jnp.where(even, one, other), jnp.where(even, other, one)
    beyond = jnp.concatenate([upper, lower], axis=1)
    even = lax.axis_index("cross") % 2 == 0
    tall = jnp.concatenate([all_fields, beyond], axis=1)
    head, tail = tall[:, :, :WIDE], tall[:, :, columns - WIDE :]
    one = swap(jnp.where(even, tail, head), "cross", 0)
    other = swap(jnp.where(even, head, tail), "cross", 1)
    right, left = jnp.where(even, one, other), jnp.where(even, other, one)
    edge = jnp.concatenate([right, left], axis=2)
    edge = jnp.concatenate([edge, jnp.zeros((1,) + edge.shape[1:], jnp.float32)], axis=0)
    beyond = jnp.concatenate([beyond, jnp.zeros((1, ROWS, columns), jnp.float32)], axis=0)
    vmem = pl.BlockSpec(memory_space=pltpu.VMEM)
    smem = pl.BlockSpec(memory_space=pltpu.SMEM)
    f32, bf16 = jnp.float32, jnp.bfloat16
    params = pltpu.CompilerParams(vmem_limit_bytes=32 * 1024 * 1024)
    matrices = pl.pallas_call(
        matrix_kernel,
        grid=(2,),
        out_shape=jax.ShapeDtypeStruct((2, 3 * SLOTS.shape[1], SLOTS.shape[2]), bf16),
        in_specs=[smem, pl.BlockSpec((1,) + SLOTS.shape[1:], lambda i: (i, 0, 0))],
        out_specs=pl.BlockSpec((1, 3 * SLOTS.shape[1], SLOTS.shape[2]), lambda i: (i, 0, 0)),
        name="matrix",
    )(stencil_weights, jnp.asarray(SLOTS))
    count, wider = FIELDS + 1, STIFF + 2
    one_of = lambda number: jax.ShapeDtypeStruct((number, 8, LANES), f32)
    pair_of = lambda number: jax.ShapeDtypeStruct((2, number, 8, LANES), f32)
    pairs, own_grown, *nears = pl.pallas_call(
        start_kernel,
        out_shape=(
            pair_of(wider), pair_of(count),
            pair_of(wider), pair_of(wider), pair_of(count), pair_of(count),
        ),
        in_specs=[vmem] * 3,
        out_specs=(vmem,) * 6,
        compiler_params=params,
        cost_estimate=pl.CostEstimate(flops=5 * 10**9, bytes_accessed=0, transcendentals=0),
        name="start",
    )(own, extra, matrices)
    halo, halo_grown, *kept, inner_second, sums = pl.pallas_call(
        inner_kernel,
        out_shape=(
            pair_of(wider), pair_of(count),
            pair_of(wider), pair_of(wider), pair_of(count), pair_of(count),
            pair_of(count), pair_of(count), pair_of(count), pair_of(count),
            pair_of(TABLE), one_of(FIELDS), one_of(4),
        ),
        in_specs=[vmem] * 3 + [smem] + [vmem] * 4,
        out_specs=(vmem,) * 13,
        compiler_params=params,
        cost_estimate=pl.CostEstimate(flops=10**10, bytes_accessed=0, transcendentals=0),
        name="inner",
    )(beyond, pairs, matrices, stencil_weights, *nears)
    images = kept[4]
    outer_image, outer_second, sums = pl.pallas_call(
        outer_kernel,
        out_shape=(one_of(count), one_of(FIELDS), jax.ShapeDtypeStruct((devices, LANES), f32)),
        in_specs=[vmem] * 4 + [smem] + [vmem] * 12,
        out_specs=(vmem,) * 3,
        scratch_shapes=[
            pltpu.VMEM((number, 8, LANES), f32) for number in (wider, count, wider, count, count)
        ],
        compiler_params=params,
        name="outer",
    )(edge, pairs, halo, matrices, stencil_weights, own_grown, halo_grown, *kept, sums)
    sums = lax.all_to_all(sums, ("down", "cross"), 0, 0, tiled=True)
    block = pl.BlockSpec((FIELDS // FINISH_STEPS, ROWS, columns), lambda i: (i, 0, 0))
    solution_field, residual = pl.pallas_call(
        finish_kernel,
        grid=(FINISH_STEPS,),
        out_shape=(jax.ShapeDtypeStruct(own.shape, f32), jax.ShapeDtypeStruct(own.shape, f32)),
        in_specs=[vmem] * 6,
        out_specs=(block, block),
        compiler_params=params,
        name="finish",
    )(sums, pairs, images, inner_second, outer_image, outer_second)
    return solution_field.reshape(right_side.shape), residual.reshape(right_side.shape)


def solution(mesh):
    return jax.shard_map(
        per_device,
        mesh=mesh,
        in_specs=(
            P(None, None, "down", "cross"),
            P("down", "cross"),
            P(None, "down", "cross"),
            P(),
        ),
        out_specs=(P(None, None, "down", "cross"), P(None, None, "down", "cross")),
        check_vma=False,
    )
```

```python
import functools
import math

import jax
import jax.numpy as jnp
import numpy as np
from jax import lax
from jax.experimental import pallas as pl
from jax.experimental.pallas import tpu as pltpu
from jax.sharding import PartitionSpec as P

CZ = 32
VARS = 4
DEG = 3
TERMS = 5
COMPS = 3
MODES = 35
FIELDS = COMPS * MODES
STIFF = FIELDS + TERMS
ROWS = 4
LANES = 128
WIDE = 64


def multi_indices(count_left, budget_left):
    if count_left == 0:
        return [()]
    return [
        (leading,) + remainder
        for leading in range(budget_left + 1)
        for remainder in multi_indices(count_left - 1, budget_left - leading)
    ]


def chaos_terms():
    picked = sorted(
        multi_indices(VARS, DEG),
        key=lambda multi_index: (sum(multi_index),)
        + tuple((-entry_value for entry_value in multi_index)),
    )
    position = {multi_index: number for number, multi_index in enumerate(picked)}
    terms = [[] for mode in picked]
    for variable in range(VARS):
        for multi_index in picked:
            raised = list(multi_index)
            raised[variable] += 1
            raised = tuple(raised)
            if raised in position:
                degree = multi_index[variable]
                here, there = position[multi_index], position[raised]
                terms[here].append((variable, degree, there))
                terms[there].append((variable, degree, here))
    values = [(n + 1) / math.sqrt((2 * n + 1) * (2 * n + 3)) for n in range(DEG)]
    return terms, values


CHAOS, CHAOS_VALUES = chaos_terms()
TABLE = 1 + VARS * DEG


def tap_slots(y_in, y_out, reach):
    z = np.arange(CZ)
    y_in, z_in = np.repeat(y_in, CZ), np.tile(z, len(y_in))
    y_out, z_out = np.repeat(y_out, CZ), np.tile(z, len(y_out))
    dy = y_in[:, None] - y_out[None, :]
    dz = z_in[:, None] - z_out[None, :]
    near = (abs(dy) <= 1) & (abs(dz) <= 1) & np.repeat(np.repeat(reach, CZ, 0), CZ, 1)
    parts = []
    for dx in (0, 1, -1):
        linear = 9 * (dx + 1) + 3 * (dy + 1) + (dz + 1)
        slot = np.minimum(linear, 26 - linear)
        parts.append(np.where(near & (linear != 13), slot, 13))
    return np.concatenate(parts, axis=1).astype(np.int32)


def chunk_slots():
    y_in = np.array([0, 1, 2, 3, 4, 5, -2, -1])
    return tap_slots(y_in, np.arange(4), np.ones((8, 4), bool))


def rim_slots():
    far = 100
    y_in = np.array([16, 17, -2 - far, -1 - far, -far, 1 - far, 14, 15])
    y_out = np.array([15, 16, -1 - far, -far])
    reach = np.ones((8, 4), bool)
    reach[4:, 0] = False
    reach[4:, 3] = False
    return tap_slots(y_in, y_out, reach)


SLOTS = np.stack([chunk_slots(), rim_slots()])


def matrix_kernel(weights_ref, slots_ref, matrix_ref):
    slots = slots_ref[0]
    full = jnp.zeros(slots.shape, jnp.float32)
    for number in range(13):
        full = jnp.where(slots == number, 0.5 * weights_ref[number], full)
    high = full.astype(jnp.bfloat16)
    low = (full - high.astype(jnp.float32)).astype(jnp.bfloat16)
    rows = slots.shape[0]
    matrix_ref[0, :rows] = high
    matrix_ref[0, rows : 2 * rows] = high
    matrix_ref[0, 2 * rows :] = low


def mix(table, load, mode, total):
    for variable, degree, other in CHAOS[mode]:
        total = total + table[1 + variable * DEG + degree] * load(other)
    return total


PAIRS = ((0, 3), (1, 2))
OUTER, INNER = 0, 1


def tile_row():
    return lax.broadcasted_iota(jnp.int32, (8, LANES), 0)


def tile_lane():
    return lax.broadcasted_iota(jnp.int32, (8, LANES), 1)


def beside_outer(inner, lead, ahead=0.0, behind=0.0):
    left = tile_lane() < WIDE
    return jnp.where(left, jnp.where(lead, inner, ahead), jnp.where(lead, behind, inner))


def beside_inner(outer, inner, lead):
    left = tile_lane() < WIDE
    turned = pltpu.roll(inner, ROWS, 1)
    return jnp.where(left, jnp.where(lead, turned, outer), jnp.where(lead, outer, turned))


def halves(value):
    value = value.reshape(value.shape[0] * 8, LANES)
    high = value.astype(jnp.bfloat16)
    return high, (value - high.astype(jnp.float32)).astype(jnp.bfloat16)


def stencil(own, beside, matrix):
    (high, low), (near_high, near_low) = halves(own), halves(beside)
    lines = jnp.concatenate([high, near_high, low, near_low, high, near_high], axis=1)
    parts = jnp.dot(lines, matrix, preferred_element_type=jnp.float32)
    return [
        parts[:, at : at + LANES].reshape(own.shape) for at in range(0, parts.shape[1], LANES)
    ]


def turned_parts(parts):
    return pltpu.roll(parts[-2], 7, 1), pltpu.roll(parts[-1], 1, 1)


def same_rows(parts):
    ahead, behind = turned_parts(parts)
    row = tile_row() % ROWS
    return parts[0] + jnp.where(row == ROWS - 1, 0.0, ahead) + jnp.where(row == 0, 0.0, behind)


def other_rows(parts):
    ahead, behind = turned_parts(parts)
    row = tile_row() % ROWS
    return jnp.where(row == ROWS - 1, ahead, jnp.where(row == 0, behind, 0.0))


def entry_of(ref):
    return lambda number: ref[number]


def coef_values(field):
    values = [field(FIELDS + term) for term in range(TERMS)]
    return spread_values(values)


def spread_values(values):
    return [values[0]] + [
        values[1 + variable] * CHAOS_VALUES[degree]
        for variable in range(VARS)
        for degree in range(DEG)
    ]


def diag_values(field, near, weights_ref):
    weight_sum = sum(weights_ref[number] for number in range(13))
    return spread_values(
        [field(FIELDS + term) * weight_sum + near(FIELDS + term) for term in range(TERMS)]
    )


def grow(field, table, out):
    @pl.loop(0, COMPS)
    def each(comp):
        base = comp * MODES
        for mode in range(MODES):
            load = lambda other: field(base + other)
            out[base + mode] = mix(table, load, mode, table[0] * load(mode))

    out[FIELDS] = jnp.zeros((8, LANES), jnp.float32)


def apply(field, near, grown_near, coef, diag, stiff, store, carry=0):
    def each(comp, carry):
        base = comp * MODES
        for mode in range(MODES):
            load = lambda other: field(base + other)
            close = lambda other: near(base + other)
            value = mix(diag, load, mode, (stiff + diag[0]) * load(mode))
            value = value - mix(
                coef, close, mode, coef[0] * close(mode) + grown_near(base + mode)
            )
            carry = store(base + mode, value, carry)
        return carry

    return lax.fori_loop(0, COMPS, each, carry)


def masked_store(out, inside):
    def store(number, value, carry):
        out[number] = jnp.where(inside, value, 0.0)
        return carry

    return store


def second_store(start, image, out):
    def store(number, value, sums):
        rr, rq, qq, qz = sums
        first, here = start(number), image(number)
        out[number] = value
        return rr + first * first, rq + first * here, qq + here * here, qz + here * value

    return store


def second_near(own, own_beside, halo, halo_beside, matrix_ref):
    own_parts = stencil(own, own_beside, matrix_ref[0])
    halo_parts = stencil(halo, halo_beside, matrix_ref[0, :, LANES:])
    return same_rows(own_parts) + other_rows(halo_parts)


def start_kernel(
    own_ref, extra_ref, matrix_ref, pairs, grown, near, halo_near, grown_near, halo_grown_near
):
    for number, chunks in enumerate(PAIRS):
        for side, chunk in enumerate(chunks):
            lanes, rows = pl.ds(chunk * LANES, LANES), pl.ds(side * ROWS, ROWS)
            pairs[number, :FIELDS, rows, :] = own_ref[:, :, lanes]
            pairs[number, FIELDS : STIFF + 1, rows, :] = extra_ref[:, :, lanes]
        pairs[number, STIFF + 1] = jnp.zeros((8, LANES), jnp.float32)
        field = entry_of(pairs.at[number])
        grow(field, coef_values(field), grown.at[number])
    lead = tile_row() < ROWS
    for ref, out, halo_out in ((pairs, near, halo_near), (grown, grown_near, halo_grown_near)):
        outer, inner = ref[OUTER], ref[INNER]
        for number, own, beside in (
            (OUTER, outer, beside_outer(inner, lead)),
            (INNER, inner, beside_inner(outer, inner, lead)),
        ):
            parts = stencil(own, beside, matrix_ref[0])
            out[number] = same_rows(parts)
            halo_out[number] = other_rows(parts)


def join_kernel(flags_ref, one_ref, other_ref, own_ref, extra_ref, beyond_ref, first_ref, second_ref, ends):
    even_down, even_cross = flags_ref[0] == 1, flags_ref[1] == 1
    upper = jnp.where(even_down, one_ref[...], other_ref[...])
    lower = jnp.where(even_down, other_ref[...], one_ref[...])
    fields = pl.ds(0, STIFF + 1)
    beyond_ref[fields, :2] = upper
    beyond_ref[fields, 2:] = lower
    beyond_ref[STIFF + 1] = jnp.zeros(beyond_ref.shape[1:], jnp.float32)
    for side, chunk in enumerate(PAIRS[OUTER]):
        lanes = pl.ds(chunk * LANES, LANES)
        ends[side, :FIELDS, :ROWS] = own_ref[:, :, lanes]
        ends[side, FIELDS : STIFF + 1, :ROWS] = extra_ref[:, :, lanes]
        ends[side, fields, ROWS:] = beyond_ref[fields, :, lanes]
        ends[side, STIFF + 1] = jnp.zeros((8, LANES), jnp.float32)
    half = first_ref.shape[0]
    left = tile_lane() < WIDE
    head = jnp.where(left, ends[0, :half], pltpu.roll(ends[0, half:], WIDE, 2))
    tail = jnp.where(left, pltpu.roll(ends[1, :half], WIDE, 2), ends[1, half:])
    first_ref[...] = jnp.where(even_cross, tail, head)
    second_ref[...] = jnp.where(even_cross, head, tail)


def inner_kernel(
    beyond_ref, pairs, matrix_ref, weights_ref,
    before_near, before_halo_near, before_grown_near, before_halo_grown_near,
    halo, halo_grown, near, halo_near, grown_near, halo_grown_near,
    image, halo_image, image_grown, halo_image_grown, diag, second_ref, sums_ref,
):
    for number, (first, second) in enumerate(PAIRS):
        halo[number, :, ROWS:, :] = beyond_ref[:, :, pl.ds(first * LANES, LANES)]
        halo[number, :, :ROWS, :] = beyond_ref[:, :, pl.ds(second * LANES, LANES)]
        field = entry_of(halo.at[number])
        grow(field, coef_values(field), halo_grown.at[number])
    lead = tile_row() >= ROWS
    for ref, before, before_halo, out, halo_out in (
        (halo, before_near, before_halo_near, near, halo_near),
        (halo_grown, before_grown_near, before_halo_grown_near, grown_near, halo_grown_near),
    ):
        outer, inner = ref[OUTER], ref[INNER]
        for number, own, beside in (
            (OUTER, outer, beside_outer(inner, lead)),
            (INNER, inner, beside_inner(outer, inner, lead)),
        ):
            parts = stencil(own, beside, matrix_ref[0])
            halo_out[number] = before_halo[number] + same_rows(parts)
            out[number] = before[number] + other_rows(parts)

    for ref, close, grown_close, out, out_grown in (
        (pairs, near, grown_near, image, image_grown),
        (halo, halo_near, halo_grown_near, halo_image, halo_image_grown),
    ):

        @pl.loop(0, len(PAIRS))
        def each(number):
            field, around = entry_of(ref.at[number]), entry_of(close.at[number])
            coef = coef_values(field)
            values = diag_values(field, around, weights_ref)
            if ref is pairs:
                for entry, value in enumerate(values):
                    diag[number, entry] = value
            stiff = field(STIFF)
            target = out.at[number]
            apply(
                field, around, entry_of(grown_close.at[number]), coef, values, stiff,
                masked_store(target, stiff > 0.0),
            )
            target[FIELDS] = jnp.zeros((8, LANES), jnp.float32)
            grow(entry_of(target), coef, out_grown.at[number])

    own_lead = tile_row() < ROWS
    image_near, image_grown_near = near.at[INNER, pl.ds(0, FIELDS + 1)], grown_near.at[INNER]
    for own, far, out in (
        (image, halo_image, image_near),
        (image_grown, halo_image_grown, image_grown_near),
    ):
        out[...] = second_near(
            own[INNER],
            beside_inner(own[OUTER], own[INNER], own_lead),
            far[INNER],
            beside_inner(far[OUTER], far[INNER], lead),
            matrix_ref,
        )
    field, here = entry_of(pairs.at[INNER]), entry_of(image.at[INNER])
    zero = jnp.zeros((8, LANES), jnp.float32)
    sums = apply(
        here, entry_of(image_near), entry_of(image_grown_near), coef_values(field),
        [diag[INNER, entry] for entry in range(TABLE)], field(STIFF),
        second_store(field, here, second_ref), (zero, zero, zero, zero),
    )
    for number, value in enumerate(sums):
        sums_ref[number] = value


def outer_kernel(
    flags_ref, one_ref, other_ref, pairs, halo, matrix_ref, weights_ref, own_grown, halo_grown,
    near, halo_near, grown_near, halo_grown_near,
    image, halo_image, image_grown, halo_image_grown, diag, before_ref,
    image_ref, second_ref, sums_ref,
    edge, rim, grown, rim_near, rim_grown_near, rim_image,
):
    lane, top = tile_lane(), tile_row() < ROWS
    bottom = ~top
    left = lane < WIDE

    def first_chunk(own, far):
        return jnp.where(top, own, far)

    def last_chunk(own, far):
        return pltpu.roll(jnp.where(top, far, own), ROWS, own.ndim - 2)

    def to_rim(last, beyond, begin):
        right = pltpu.roll(jnp.where(lane >= 3 * CZ, last, beyond), CZ, 2)
        return jnp.where(
            left, right, pltpu.roll(jnp.where(lane < CZ, begin, beyond), LANES - CZ, 2)
        )

    def rim_stencil(around, own, far, own_near, far_near):
        beside = jnp.where(left, first_chunk(own, far), last_chunk(own, far))
        parts = stencil(around, beside, matrix_ref[1])
        ahead, behind = turned_parts(parts)
        begin = first_chunk(own_near, far_near)
        last = last_chunk(own_near, far_near)
        return parts[0] + ahead + behind + to_rim(last, jnp.zeros_like(last), begin)

    even_cross = flags_ref[1] == 1
    right = jnp.where(even_cross, one_ref[...], other_ref[...])
    before = jnp.where(even_cross, other_ref[...], one_ref[...])
    half = one_ref.shape[0]
    edge[:half] = jnp.where(left, right, pltpu.roll(before, WIDE, 2))
    edge[half:] = jnp.where(left, pltpu.roll(right, WIDE, 2), before)
    field = entry_of(edge)
    grow(field, coef_values(field), grown)
    rim_near[...] = rim_stencil(
        edge[...], pairs[OUTER], halo[OUTER], near[OUTER], halo_near[OUTER]
    )
    rim_grown_near[...] = rim_stencil(
        grown[...], own_grown[OUTER], halo_grown[OUTER], grown_near[OUTER], halo_grown_near[OUTER]
    )
    rim[...] = to_rim(
        last_chunk(pairs[OUTER], halo[OUTER]), edge[...], first_chunk(pairs[OUTER], halo[OUTER])
    )
    field, around = entry_of(rim), entry_of(rim_near)
    coef, rim_diag = coef_values(field), diag_values(field, around, weights_ref)
    stiff = field(STIFF)
    apply(
        field, around, entry_of(rim_grown_near), coef, rim_diag, stiff,
        masked_store(rim_image, stiff > 0.0),
    )
    rim_image[FIELDS] = jnp.zeros((8, LANES), jnp.float32)
    grow(entry_of(rim_image), coef, grown)

    def from_rim(value):
        last = pltpu.roll(value, LANES - CZ, value.ndim - 1)
        return pltpu.roll(value, CZ, value.ndim - 1), pltpu.roll(last, ROWS, value.ndim - 2)

    def placed(lead, begin, last, value):
        value = jnp.where(lead & (lane < CZ), begin, value)
        return jnp.where(~lead & (lane >= 3 * CZ), last, value)

    image_near, image_grown_near = rim_near.at[pl.ds(0, FIELDS + 1)], rim_grown_near
    for value, own, far, out, keep in (
        (rim_image, image, halo_image, image_near, True),
        (grown, image_grown, halo_image_grown, image_grown_near, False),
    ):
        begin, last = from_rim(value[...])
        here = placed(top, begin, last, own[OUTER])
        if keep:
            image_ref[...] = here
        out[...] = second_near(
            here,
            beside_outer(own[INNER], top, last, begin),
            placed(bottom, begin, last, far[OUTER]),
            beside_outer(far[INNER], bottom, last, begin),
            matrix_ref,
        )
    values = []
    for entry in range(TABLE):
        begin, last = from_rim(rim_diag[entry])
        values.append(placed(top, begin, last, diag[OUTER, entry]))
    field, here = entry_of(pairs.at[OUTER]), entry_of(image_ref)
    sums = apply(
        here, entry_of(image_near), entry_of(image_grown_near), coef_values(field), values,
        field(STIFF), second_store(field, here, second_ref),
        tuple(before_ref[number] for number in range(4)),
    )
    column = lax.broadcasted_iota(jnp.int32, sums_ref.shape, 1)
    row = jnp.zeros(sums_ref.shape, jnp.float32)
    for number, value in enumerate(sums):
        row = jnp.where(column == number, jnp.sum(value), row)
    sums_ref[...] = row


FINISH_STEPS = 3


def finish_kernel(
    sums_ref, pairs, images, inner_second, outer_image, outer_second,
    field_out, residual_out, field_ref, residual_ref, sems,
):
    total = jnp.sum(sums_ref[...], axis=0, keepdims=True)
    lane = lax.broadcasted_iota(jnp.int32, total.shape, 1)
    rr, rq, qq, qz = [
        jnp.sum(jnp.where(lane == number, total, 0.0), axis=1, keepdims=True)[None]
        for number in range(4)
    ]
    step = rr / rq
    fresh = rr - 2.0 * step * rq + step * step * qq
    larger = 1.0 + fresh / rr
    curvature = larger * larger * rq - 2.0 * larger * step * qq + step * step * qz
    later = fresh / curvature
    both = step + later * larger
    cross = later * step
    count = FIELDS // FINISH_STEPS
    copies = []
    for at in range(FINISH_STEPS):
        here = pl.ds(at * count, count)
        for number, image_ref, second_ref in (
            (OUTER, outer_image, outer_second),
            (INNER, images.at[INNER], inner_second),
        ):
            start, image, second = pairs[number, here], image_ref[here], second_ref[here]
            field = both * start - cross * image
            residual = start - both * image + cross * second
            for side, chunk in enumerate(PAIRS[number]):
                lanes, rows = pl.ds(chunk * LANES, LANES), slice(side * ROWS, (side + 1) * ROWS)
                field_ref[here, :, lanes] = field[:, rows]
                residual_ref[here, :, lanes] = residual[:, rows]
        for number, (ref, out) in enumerate(((field_ref, field_out), (residual_ref, residual_out))):
            copy = pltpu.make_async_copy(ref.at[here], out.at[here], sems.at[at, number])
            copy.start()
            copies.append(copy)
    for copy in copies:
        copy.wait()


def swap(value, axis, begin):
    size = lax.axis_size(axis)
    pairs = [(i, i + 1) for i in range(begin, size - 1, 2)]
    return lax.ppermute(value, axis, pairs + [(j, i) for i, j in pairs])


def per_device(right_side, stiffness, coefficients, stencil_weights):
    columns = right_side.shape[3]
    devices = lax.axis_size("down") * lax.axis_size("cross")
    own = right_side.reshape(FIELDS, ROWS, columns)
    extra = jnp.concatenate([coefficients, stiffness[None]], axis=0)
    even = lax.axis_index("down") % 2 == 0
    flags = jnp.stack([even, lax.axis_index("cross") % 2 == 0]).astype(jnp.int32)

    def rows_for(lower):
        parts = [jnp.where(lower, x[:, ROWS - 2 :], x[:, :2]) for x in (own, extra)]
        return jnp.concatenate(parts, axis=0)

    one = swap(rows_for(even), "down", 0)
    other = swap(rows_for(~even), "down", 1)
    vmem = pl.BlockSpec(memory_space=pltpu.VMEM)
    smem = pl.BlockSpec(memory_space=pltpu.SMEM)
    f32, bf16 = jnp.float32, jnp.bfloat16
    params = pltpu.CompilerParams(vmem_limit_bytes=32 * 1024 * 1024)
    matrices = pl.pallas_call(
        matrix_kernel,
        grid=(2,),
        out_shape=jax.ShapeDtypeStruct((2, 3 * SLOTS.shape[1], SLOTS.shape[2]), bf16),
        in_specs=[smem, pl.BlockSpec((1,) + SLOTS.shape[1:], lambda i: (i, 0, 0))],
        out_specs=pl.BlockSpec((1, 3 * SLOTS.shape[1], SLOTS.shape[2]), lambda i: (i, 0, 0)),
        name="matrix",
    )(stencil_weights, jnp.asarray(SLOTS))
    count, wider = FIELDS + 1, STIFF + 2
    one_of = lambda number: jax.ShapeDtypeStruct((number, 8, LANES), f32)
    pair_of = lambda number: jax.ShapeDtypeStruct((2, number, 8, LANES), f32)
    pairs, own_grown, *nears = pl.pallas_call(
        start_kernel,
        out_shape=(
            pair_of(wider), pair_of(count),
            pair_of(wider), pair_of(wider), pair_of(count), pair_of(count),
        ),
        in_specs=[vmem] * 3,
        out_specs=(vmem,) * 6,
        compiler_params=params,
        cost_estimate=pl.CostEstimate(flops=5 * 10**9, bytes_accessed=0, transcendentals=0),
        name="start",
    )(own, extra, matrices)
    half = jax.ShapeDtypeStruct((wider // 2, 8, LANES), f32)
    beyond, first, second = pl.pallas_call(
        join_kernel,
        out_shape=(jax.ShapeDtypeStruct((wider, ROWS, columns), f32), half, half),
        in_specs=[smem] + [vmem] * 4,
        out_specs=(vmem,) * 3,
        scratch_shapes=[pltpu.VMEM((2, wider, 8, LANES), f32)],
        compiler_params=params,
        name="join",
    )(flags, one, other, own, extra)
    first, second = swap(first, "cross", 0), swap(second, "cross", 1)
    halo, halo_grown, *kept, inner_second, sums = pl.pallas_call(
        inner_kernel,
        out_shape=(
            pair_of(wider), pair_of(count),
            pair_of(wider), pair_of(wider), pair_of(count), pair_of(count),
            pair_of(count), pair_of(count), pair_of(count), pair_of(count),
            pair_of(TABLE), one_of(FIELDS), one_of(4),
        ),
        in_specs=[vmem] * 3 + [smem] + [vmem] * 4,
        out_specs=(vmem,) * 13,
        compiler_params=params,
        cost_estimate=pl.CostEstimate(flops=10**10, bytes_accessed=0, transcendentals=0),
        name="inner",
    )(beyond, pairs, matrices, stencil_weights, *nears)
    images = kept[4]
    outer_image, outer_second, sums = pl.pallas_call(
        outer_kernel,
        out_shape=(one_of(count), one_of(FIELDS), jax.ShapeDtypeStruct((devices, LANES), f32)),
        in_specs=[smem] + [vmem] * 5 + [smem] + [vmem] * 12,
        out_specs=(vmem,) * 3,
        scratch_shapes=[
            pltpu.VMEM((number, 8, LANES), f32)
            for number in (wider, wider, count, wider, count, count)
        ],
        compiler_params=params,
        name="outer",
    )(flags, first, second, pairs, halo, matrices, stencil_weights, own_grown, halo_grown, *kept, sums)
    sums = lax.all_to_all(sums, ("down", "cross"), 0, 0, tiled=True)
    anywhere = pl.BlockSpec(memory_space=pl.ANY)
    solution_field, residual = pl.pallas_call(
        finish_kernel,
        out_shape=(jax.ShapeDtypeStruct(own.shape, f32), jax.ShapeDtypeStruct(own.shape, f32)),
        in_specs=[vmem] * 6,
        out_specs=(anywhere, anywhere),
        scratch_shapes=[
            pltpu.VMEM(own.shape, f32),
            pltpu.VMEM(own.shape, f32),
            pltpu.SemaphoreType.DMA((FINISH_STEPS, 2)),
        ],
        compiler_params=params,
        name="finish",
    )(sums, pairs, images, inner_second, outer_image, outer_second)
    return solution_field.reshape(right_side.shape), residual.reshape(right_side.shape)


def solution(mesh):
    return jax.shard_map(
        per_device,
        mesh=mesh,
        in_specs=(
            P(None, None, "down", "cross"),
            P("down", "cross"),
            P(None, "down", "cross"),
            P(),
        ),
        out_specs=(P(None, None, "down", "cross"), P(None, None, "down", "cross")),
        check_vma=False,
    )
```

```python
import functools
import math

import jax
import jax.numpy as jnp
import numpy as np
from jax import lax
from jax.experimental import pallas as pl
from jax.experimental.pallas import tpu as pltpu
from jax.sharding import PartitionSpec as P

CZ = 32
VARS = 4
DEG = 3
TERMS = 5
COMPS = 3
MODES = 35
FIELDS = COMPS * MODES
STIFF = FIELDS + TERMS
ROWS = 4
LANES = 128
WIDE = 64


def multi_indices(count_left, budget_left):
    if count_left == 0:
        return [()]
    return [
        (leading,) + remainder
        for leading in range(budget_left + 1)
        for remainder in multi_indices(count_left - 1, budget_left - leading)
    ]


def chaos_terms():
    picked = sorted(
        multi_indices(VARS, DEG),
        key=lambda multi_index: (sum(multi_index),)
        + tuple((-entry_value for entry_value in multi_index)),
    )
    position = {multi_index: number for number, multi_index in enumerate(picked)}
    terms = [[] for mode in picked]
    for variable in range(VARS):
        for multi_index in picked:
            raised = list(multi_index)
            raised[variable] += 1
            raised = tuple(raised)
            if raised in position:
                degree = multi_index[variable]
                here, there = position[multi_index], position[raised]
                terms[here].append((variable, degree, there))
                terms[there].append((variable, degree, here))
    values = [(n + 1) / math.sqrt((2 * n + 1) * (2 * n + 3)) for n in range(DEG)]
    return terms, values


CHAOS, CHAOS_VALUES = chaos_terms()
TABLE = 1 + VARS * DEG


def tap_slots(y_in, y_out, reach):
    z = np.arange(CZ)
    y_in, z_in = np.repeat(y_in, CZ), np.tile(z, len(y_in))
    y_out, z_out = np.repeat(y_out, CZ), np.tile(z, len(y_out))
    dy = y_in[:, None] - y_out[None, :]
    dz = z_in[:, None] - z_out[None, :]
    near = (abs(dy) <= 1) & (abs(dz) <= 1) & np.repeat(np.repeat(reach, CZ, 0), CZ, 1)
    parts = []
    for dx in (0, 1, -1):
        linear = 9 * (dx + 1) + 3 * (dy + 1) + (dz + 1)
        slot = np.minimum(linear, 26 - linear)
        parts.append(np.where(near & (linear != 13), slot, 13))
    return np.concatenate(parts, axis=1).astype(np.int32)


def chunk_slots():
    y_in = np.array([0, 1, 2, 3, 4, 5, -2, -1])
    return tap_slots(y_in, np.arange(4), np.ones((8, 4), bool))


def rim_slots():
    far = 100
    y_in = np.array([16, 17, -2 - far, -1 - far, -far, 1 - far, 14, 15])
    y_out = np.array([15, 16, -1 - far, -far])
    reach = np.ones((8, 4), bool)
    reach[4:, 0] = False
    reach[4:, 3] = False
    return tap_slots(y_in, y_out, reach)


SLOTS = np.stack([chunk_slots(), rim_slots()])


def matrix_kernel(weights_ref, slots_ref, matrix_ref):
    slots = slots_ref[0]
    full = jnp.zeros(slots.shape, jnp.float32)
    for number in range(13):
        full = jnp.where(slots == number, 0.5 * weights_ref[number], full)
    high = full.astype(jnp.bfloat16)
    low = (full - high.astype(jnp.float32)).astype(jnp.bfloat16)
    rows = slots.shape[0]
    matrix_ref[0, :rows] = high
    matrix_ref[0, rows : 2 * rows] = high
    matrix_ref[0, 2 * rows :] = low


def mix(table, load, mode, total):
    for variable, degree, other in CHAOS[mode]:
        total = total + table[1 + variable * DEG + degree] * load(other)
    return total


PAIRS = ((0, 3), (1, 2))
OUTER, INNER = 0, 1


def tile_row():
    return lax.broadcasted_iota(jnp.int32, (8, LANES), 0)


def tile_lane():
    return lax.broadcasted_iota(jnp.int32, (8, LANES), 1)


def beside_outer(inner, lead, ahead=0.0, behind=0.0):
    left = tile_lane() < WIDE
    return jnp.where(left, jnp.where(lead, inner, ahead), jnp.where(lead, behind, inner))


def beside_inner(outer, inner, lead):
    left = tile_lane() < WIDE
    turned = pltpu.roll(inner, ROWS, 1)
    return jnp.where(left, jnp.where(lead, turned, outer), jnp.where(lead, outer, turned))


def halves(value):
    value = value.reshape(value.shape[0] * 8, LANES)
    high = value.astype(jnp.bfloat16)
    return high, (value - high.astype(jnp.float32)).astype(jnp.bfloat16)


def stencil(own, beside, matrix):
    (high, low), (near_high, near_low) = halves(own), halves(beside)
    lines = jnp.concatenate([high, near_high, low, near_low, high, near_high], axis=1)
    parts = jnp.dot(lines, matrix, preferred_element_type=jnp.float32)
    return [
        parts[:, at : at + LANES].reshape(own.shape) for at in range(0, parts.shape[1], LANES)
    ]


def turned_parts(parts):
    return pltpu.roll(parts[-2], 7, 1), pltpu.roll(parts[-1], 1, 1)


def same_rows(parts):
    ahead, behind = turned_parts(parts)
    row = tile_row() % ROWS
    return parts[0] + jnp.where(row == ROWS - 1, 0.0, ahead) + jnp.where(row == 0, 0.0, behind)


def other_rows(parts):
    ahead, behind = turned_parts(parts)
    row = tile_row() % ROWS
    return jnp.where(row == ROWS - 1, ahead, jnp.where(row == 0, behind, 0.0))


def entry_of(ref):
    return lambda number: ref[number]


def coef_values(field):
    values = [field(FIELDS + term) for term in range(TERMS)]
    return spread_values(values)


def spread_values(values):
    return [values[0]] + [
        values[1 + variable] * CHAOS_VALUES[degree]
        for variable in range(VARS)
        for degree in range(DEG)
    ]


def diag_values(field, near, weights_ref):
    weight_sum = sum(weights_ref[number] for number in range(13))
    return spread_values(
        [field(FIELDS + term) * weight_sum + near(FIELDS + term) for term in range(TERMS)]
    )


def grow(field, table, out):
    for comp in range(COMPS):
        base = comp * MODES
        for mode in range(MODES):
            load = lambda other: field(base + other)
            out[base + mode] = mix(table, load, mode, table[0] * load(mode))

    out[FIELDS] = jnp.zeros((8, LANES), jnp.float32)


def apply(field, near, grown_near, coef, diag, stiff, store, carry=0):
    def each(comp, carry):
        base = comp * MODES
        for mode in range(MODES):
            load = lambda other: field(base + other)
            close = lambda other: near(base + other)
            value = mix(diag, load, mode, (stiff + diag[0]) * load(mode))
            value = value - mix(
                coef, close, mode, coef[0] * close(mode) + grown_near(base + mode)
            )
            carry = store(base + mode, value, carry)
        return carry

    for comp in range(COMPS):
        carry = each(comp, carry)
    return carry


def masked_store(out, inside):
    def store(number, value, carry):
        out[number] = jnp.where(inside, value, 0.0)
        return carry

    return store


def second_store(start, image, out):
    def store(number, value, sums):
        rr, rq, qq, qz = sums
        first, here = start(number), image(number)
        out[number] = value
        return rr + first * first, rq + first * here, qq + here * here, qz + here * value

    return store


def second_near(own, own_beside, halo, halo_beside, matrix_ref):
    own_parts = stencil(own, own_beside, matrix_ref[0])
    halo_parts = stencil(halo, halo_beside, matrix_ref[0, :, LANES:])
    return same_rows(own_parts) + other_rows(halo_parts)


def start_kernel(
    own_ref, extra_ref, matrix_ref, pairs, grown, near, halo_near, grown_near, halo_grown_near
):
    for number, chunks in enumerate(PAIRS):
        for side, chunk in enumerate(chunks):
            lanes, rows = pl.ds(chunk * LANES, LANES), pl.ds(side * ROWS, ROWS)
            pairs[number, :FIELDS, rows, :] = own_ref[:, :, lanes]
            pairs[number, FIELDS : STIFF + 1, rows, :] = extra_ref[:, :, lanes]
        pairs[number, STIFF + 1] = jnp.zeros((8, LANES), jnp.float32)
        field = entry_of(pairs.at[number])
        grow(field, coef_values(field), grown.at[number])
    lead = tile_row() < ROWS
    for ref, out, halo_out in ((pairs, near, halo_near), (grown, grown_near, halo_grown_near)):
        outer, inner = ref[OUTER], ref[INNER]
        for number, own, beside in (
            (OUTER, outer, beside_outer(inner, lead)),
            (INNER, inner, beside_inner(outer, inner, lead)),
        ):
            parts = stencil(own, beside, matrix_ref[0])
            out[number] = same_rows(parts)
            halo_out[number] = other_rows(parts)


def join_kernel(flags_ref, one_ref, other_ref, own_ref, extra_ref, beyond_ref, first_ref, second_ref, ends):
    even_down, even_cross = flags_ref[0] == 1, flags_ref[1] == 1
    upper = jnp.where(even_down, one_ref[...], other_ref[...])
    lower = jnp.where(even_down, other_ref[...], one_ref[...])
    fields = pl.ds(0, STIFF + 1)
    beyond_ref[fields, :2] = upper
    beyond_ref[fields, 2:] = lower
    beyond_ref[STIFF + 1] = jnp.zeros(beyond_ref.shape[1:], jnp.float32)
    for side, chunk in enumerate(PAIRS[OUTER]):
        lanes = pl.ds(chunk * LANES, LANES)
        ends[side, :FIELDS, :ROWS] = own_ref[:, :, lanes]
        ends[side, FIELDS : STIFF + 1, :ROWS] = extra_ref[:, :, lanes]
        ends[side, fields, ROWS:] = beyond_ref[fields, :, lanes]
        ends[side, STIFF + 1] = jnp.zeros((8, LANES), jnp.float32)
    half = first_ref.shape[0]
    left = tile_lane() < WIDE
    head = jnp.where(left, ends[0, :half], pltpu.roll(ends[0, half:], WIDE, 2))
    tail = jnp.where(left, pltpu.roll(ends[1, :half], WIDE, 2), ends[1, half:])
    first_ref[...] = jnp.where(even_cross, tail, head)
    second_ref[...] = jnp.where(even_cross, head, tail)


def inner_kernel(
    beyond_ref, pairs, matrix_ref, weights_ref,
    before_near, before_halo_near, before_grown_near, before_halo_grown_near,
    halo, halo_grown, near, halo_near, grown_near, halo_grown_near,
    image, halo_image, image_grown, halo_image_grown, diag, second_ref, sums_ref,
):
    for number, (first, second) in enumerate(PAIRS):
        halo[number, :, ROWS:, :] = beyond_ref[:, :, pl.ds(first * LANES, LANES)]
        halo[number, :, :ROWS, :] = beyond_ref[:, :, pl.ds(second * LANES, LANES)]
        field = entry_of(halo.at[number])
        grow(field, coef_values(field), halo_grown.at[number])
    lead = tile_row() >= ROWS
    for ref, before, before_halo, out, halo_out in (
        (halo, before_near, before_halo_near, near, halo_near),
        (halo_grown, before_grown_near, before_halo_grown_near, grown_near, halo_grown_near),
    ):
        outer, inner = ref[OUTER], ref[INNER]
        for number, own, beside in (
            (OUTER, outer, beside_outer(inner, lead)),
            (INNER, inner, beside_inner(outer, inner, lead)),
        ):
            parts = stencil(own, beside, matrix_ref[0])
            halo_out[number] = before_halo[number] + same_rows(parts)
            out[number] = before[number] + other_rows(parts)

    for ref, close, grown_close, out, out_grown in (
        (pairs, near, grown_near, image, image_grown),
        (halo, halo_near, halo_grown_near, halo_image, halo_image_grown),
    ):

        for number in range(len(PAIRS)):
            field, around = entry_of(ref.at[number]), entry_of(close.at[number])
            coef = coef_values(field)
            values = diag_values(field, around, weights_ref)
            if ref is pairs:
                for entry, value in enumerate(values):
                    diag[number, entry] = value
            stiff = field(STIFF)
            target = out.at[number]
            apply(
                field, around, entry_of(grown_close.at[number]), coef, values, stiff,
                masked_store(target, stiff > 0.0),
            )
            target[FIELDS] = jnp.zeros((8, LANES), jnp.float32)
            grow(entry_of(target), coef, out_grown.at[number])

    own_lead = tile_row() < ROWS
    image_near, image_grown_near = near.at[INNER, pl.ds(0, FIELDS + 1)], grown_near.at[INNER]
    for own, far, out in (
        (image, halo_image, image_near),
        (image_grown, halo_image_grown, image_grown_near),
    ):
        out[...] = second_near(
            own[INNER],
            beside_inner(own[OUTER], own[INNER], own_lead),
            far[INNER],
            beside_inner(far[OUTER], far[INNER], lead),
            matrix_ref,
        )
    field, here = entry_of(pairs.at[INNER]), entry_of(image.at[INNER])
    zero = jnp.zeros((8, LANES), jnp.float32)
    sums = apply(
        here, entry_of(image_near), entry_of(image_grown_near), coef_values(field),
        [diag[INNER, entry] for entry in range(TABLE)], field(STIFF),
        second_store(field, here, second_ref), (zero, zero, zero, zero),
    )
    for number, value in enumerate(sums):
        sums_ref[number] = value


def outer_kernel(
    flags_ref, one_ref, other_ref, pairs, halo, matrix_ref, weights_ref, own_grown, halo_grown,
    near, halo_near, grown_near, halo_grown_near,
    image, halo_image, image_grown, halo_image_grown, diag, before_ref,
    image_ref, second_ref, sums_ref,
    edge, rim, grown, rim_near, rim_grown_near, rim_image,
):
    lane, top = tile_lane(), tile_row() < ROWS
    bottom = ~top
    left = lane < WIDE

    def first_chunk(own, far):
        return jnp.where(top, own, far)

    def last_chunk(own, far):
        return pltpu.roll(jnp.where(top, far, own), ROWS, own.ndim - 2)

    def to_rim(last, beyond, begin):
        right = pltpu.roll(jnp.where(lane >= 3 * CZ, last, beyond), CZ, 2)
        return jnp.where(
            left, right, pltpu.roll(jnp.where(lane < CZ, begin, beyond), LANES - CZ, 2)
        )

    def rim_stencil(around, own, far, own_near, far_near):
        beside = jnp.where(left, first_chunk(own, far), last_chunk(own, far))
        parts = stencil(around, beside, matrix_ref[1])
        ahead, behind = turned_parts(parts)
        begin = first_chunk(own_near, far_near)
        last = last_chunk(own_near, far_near)
        return parts[0] + ahead + behind + to_rim(last, jnp.zeros_like(last), begin)

    even_cross = flags_ref[1] == 1
    right = jnp.where(even_cross, one_ref[...], other_ref[...])
    before = jnp.where(even_cross, other_ref[...], one_ref[...])
    half = one_ref.shape[0]
    edge[:half] = jnp.where(left, right, pltpu.roll(before, WIDE, 2))
    edge[half:] = jnp.where(left, pltpu.roll(right, WIDE, 2), before)
    field = entry_of(edge)
    grow(field, coef_values(field), grown)
    rim_near[...] = rim_stencil(
        edge[...], pairs[OUTER], halo[OUTER], near[OUTER], halo_near[OUTER]
    )
    rim_grown_near[...] = rim_stencil(
        grown[...], own_grown[OUTER], halo_grown[OUTER], grown_near[OUTER], halo_grown_near[OUTER]
    )
    rim[...] = to_rim(
        last_chunk(pairs[OUTER], halo[OUTER]), edge[...], first_chunk(pairs[OUTER], halo[OUTER])
    )
    field, around = entry_of(rim), entry_of(rim_near)
    coef, rim_diag = coef_values(field), diag_values(field, around, weights_ref)
    stiff = field(STIFF)
    apply(
        field, around, entry_of(rim_grown_near), coef, rim_diag, stiff,
        masked_store(rim_image, stiff > 0.0),
    )
    rim_image[FIELDS] = jnp.zeros((8, LANES), jnp.float32)
    grow(entry_of(rim_image), coef, grown)

    def from_rim(value):
        last = pltpu.roll(value, LANES - CZ, value.ndim - 1)
        return pltpu.roll(value, CZ, value.ndim - 1), pltpu.roll(last, ROWS, value.ndim - 2)

    def placed(lead, begin, last, value):
        value = jnp.where(lead & (lane < CZ), begin, value)
        return jnp.where(~lead & (lane >= 3 * CZ), last, value)

    image_near, image_grown_near = rim_near.at[pl.ds(0, FIELDS + 1)], rim_grown_near
    for value, own, far, out, keep in (
        (rim_image, image, halo_image, image_near, True),
        (grown, image_grown, halo_image_grown, image_grown_near, False),
    ):
        begin, last = from_rim(value[...])
        here = placed(top, begin, last, own[OUTER])
        if keep:
            image_ref[...] = here
        out[...] = second_near(
            here,
            beside_outer(own[INNER], top, last, begin),
            placed(bottom, begin, last, far[OUTER]),
            beside_outer(far[INNER], bottom, last, begin),
            matrix_ref,
        )
    values = []
    for entry in range(TABLE):
        begin, last = from_rim(rim_diag[entry])
        values.append(placed(top, begin, last, diag[OUTER, entry]))
    field, here = entry_of(pairs.at[OUTER]), entry_of(image_ref)
    sums = apply(
        here, entry_of(image_near), entry_of(image_grown_near), coef_values(field), values,
        field(STIFF), second_store(field, here, second_ref),
        tuple(before_ref[number] for number in range(4)),
    )
    column = lax.broadcasted_iota(jnp.int32, sums_ref.shape, 1)
    row = jnp.zeros(sums_ref.shape, jnp.float32)
    for number, value in enumerate(sums):
        row = jnp.where(column == number, jnp.sum(value), row)
    sums_ref[...] = row


FINISH_STEPS = 3


def finish_kernel(
    sums_ref, pairs, images, inner_second, outer_image, outer_second,
    field_out, residual_out, field_ref, residual_ref, sems,
):
    total = jnp.sum(sums_ref[...], axis=0, keepdims=True)
    lane = lax.broadcasted_iota(jnp.int32, total.shape, 1)
    rr, rq, qq, qz = [
        jnp.sum(jnp.where(lane == number, total, 0.0), axis=1, keepdims=True)[None]
        for number in range(4)
    ]
    step = rr / rq
    fresh = rr - 2.0 * step * rq + step * step * qq
    larger = 1.0 + fresh / rr
    curvature = larger * larger * rq - 2.0 * larger * step * qq + step * step * qz
    later = fresh / curvature
    both = step + later * larger
    cross = later * step
    count = FIELDS // FINISH_STEPS
    copies = []
    for at in range(FINISH_STEPS):
        here = pl.ds(at * count, count)
        for number, image_ref, second_ref in (
            (OUTER, outer_image, outer_second),
            (INNER, images.at[INNER], inner_second),
        ):
            start, image, second = pairs[number, here], image_ref[here], second_ref[here]
            field = both * start - cross * image
            residual = start - both * image + cross * second
            for side, chunk in enumerate(PAIRS[number]):
                lanes, rows = pl.ds(chunk * LANES, LANES), slice(side * ROWS, (side + 1) * ROWS)
                field_ref[here, :, lanes] = field[:, rows]
                residual_ref[here, :, lanes] = residual[:, rows]
        for number, (ref, out) in enumerate(((field_ref, field_out), (residual_ref, residual_out))):
            copy = pltpu.make_async_copy(ref.at[here], out.at[here], sems.at[at, number])
            copy.start()
            copies.append(copy)
    for copy in copies:
        copy.wait()


def swap(value, axis, begin):
    size = lax.axis_size(axis)
    pairs = [(i, i + 1) for i in range(begin, size - 1, 2)]
    return lax.ppermute(value, axis, pairs + [(j, i) for i, j in pairs])


def per_device(right_side, stiffness, coefficients, stencil_weights):
    columns = right_side.shape[3]
    devices = lax.axis_size("down") * lax.axis_size("cross")
    own = right_side.reshape(FIELDS, ROWS, columns)
    extra = jnp.concatenate([coefficients, stiffness[None]], axis=0)
    even = lax.axis_index("down") % 2 == 0
    flags = jnp.stack([even, lax.axis_index("cross") % 2 == 0]).astype(jnp.int32)

    def rows_for(lower, arrays):
        parts = [jnp.where(lower, x[:, ROWS - 2 :], x[:, :2]) for x in arrays]
        return jnp.concatenate(parts, axis=0)

    sent = rows_for(~even, (own, extra))
    other = swap(sent, "down", 1)
    here, there, _ = lax.optimization_barrier((own, extra, sent))
    one = swap(rows_for(even, (here, there)), "down", 0)
    vmem = pl.BlockSpec(memory_space=pltpu.VMEM)
    smem = pl.BlockSpec(memory_space=pltpu.SMEM)
    f32, bf16 = jnp.float32, jnp.bfloat16
    params = pltpu.CompilerParams(vmem_limit_bytes=32 * 1024 * 1024)
    matrices = pl.pallas_call(
        matrix_kernel,
        grid=(2,),
        out_shape=jax.ShapeDtypeStruct((2, 3 * SLOTS.shape[1], SLOTS.shape[2]), bf16),
        in_specs=[smem, pl.BlockSpec((1,) + SLOTS.shape[1:], lambda i: (i, 0, 0))],
        out_specs=pl.BlockSpec((1, 3 * SLOTS.shape[1], SLOTS.shape[2]), lambda i: (i, 0, 0)),
        name="matrix",
    )(stencil_weights, jnp.asarray(SLOTS))
    count, wider = FIELDS + 1, STIFF + 2
    one_of = lambda number: jax.ShapeDtypeStruct((number, 8, LANES), f32)
    pair_of = lambda number: jax.ShapeDtypeStruct((2, number, 8, LANES), f32)
    pairs, own_grown, *nears = pl.pallas_call(
        start_kernel,
        out_shape=(
            pair_of(wider), pair_of(count),
            pair_of(wider), pair_of(wider), pair_of(count), pair_of(count),
        ),
        in_specs=[vmem] * 3,
        out_specs=(vmem,) * 6,
        compiler_params=params,
        cost_estimate=pl.CostEstimate(flops=5 * 10**9, bytes_accessed=0, transcendentals=0),
        name="start",
    )(own, extra, matrices)
    half = jax.ShapeDtypeStruct((wider // 2, 8, LANES), f32)
    beyond, first, second = pl.pallas_call(
        join_kernel,
        out_shape=(jax.ShapeDtypeStruct((wider, ROWS, columns), f32), half, half),
        in_specs=[smem] + [vmem] * 4,
        out_specs=(vmem,) * 3,
        scratch_shapes=[pltpu.VMEM((2, wider, 8, LANES), f32)],
        compiler_params=params,
        name="join",
    )(flags, one, other, own, extra)
    first, second = swap(first, "cross", 0), swap(second, "cross", 1)
    halo, halo_grown, *kept, inner_second, sums = pl.pallas_call(
        inner_kernel,
        out_shape=(
            pair_of(wider), pair_of(count),
            pair_of(wider), pair_of(wider), pair_of(count), pair_of(count),
            pair_of(count), pair_of(count), pair_of(count), pair_of(count),
            pair_of(TABLE), one_of(FIELDS), one_of(4),
        ),
        in_specs=[vmem] * 3 + [smem] + [vmem] * 4,
        out_specs=(vmem,) * 13,
        compiler_params=params,
        cost_estimate=pl.CostEstimate(flops=10**10, bytes_accessed=0, transcendentals=0),
        name="inner",
    )(beyond, pairs, matrices, stencil_weights, *nears)
    images = kept[4]
    outer_image, outer_second, sums = pl.pallas_call(
        outer_kernel,
        out_shape=(one_of(count), one_of(FIELDS), jax.ShapeDtypeStruct((devices, LANES), f32)),
        in_specs=[smem] + [vmem] * 5 + [smem] + [vmem] * 12,
        out_specs=(vmem,) * 3,
        scratch_shapes=[
            pltpu.VMEM((number, 8, LANES), f32)
            for number in (wider, wider, count, wider, count, count)
        ],
        compiler_params=params,
        name="outer",
    )(flags, first, second, pairs, halo, matrices, stencil_weights, own_grown, halo_grown, *kept, sums)
    sums = lax.all_to_all(sums, ("down", "cross"), 0, 0, tiled=True)
    anywhere = pl.BlockSpec(memory_space=pl.ANY)
    solution_field, residual = pl.pallas_call(
        finish_kernel,
        out_shape=(jax.ShapeDtypeStruct(own.shape, f32), jax.ShapeDtypeStruct(own.shape, f32)),
        in_specs=[vmem] * 6,
        out_specs=(anywhere, anywhere),
        scratch_shapes=[
            pltpu.VMEM(own.shape, f32),
            pltpu.VMEM(own.shape, f32),
            pltpu.SemaphoreType.DMA((FINISH_STEPS, 2)),
        ],
        compiler_params=params,
        name="finish",
    )(sums, pairs, images, inner_second, outer_image, outer_second)
    return solution_field.reshape(right_side.shape), residual.reshape(right_side.shape)


def solution(mesh):
    return jax.shard_map(
        per_device,
        mesh=mesh,
        in_specs=(
            P(None, None, "down", "cross"),
            P("down", "cross"),
            P(None, "down", "cross"),
            P(),
        ),
        out_specs=(P(None, None, "down", "cross"), P(None, None, "down", "cross")),
        check_vma=False,
    )
```

```python
import functools
import math

import jax
import jax.numpy as jnp
import numpy as np
from jax import lax
from jax.experimental import pallas as pl
from jax.experimental.pallas import tpu as pltpu
from jax.sharding import PartitionSpec as P

CZ = 32
VARS = 4
DEG = 3
TERMS = 5
COMPS = 3
MODES = 35
FIELDS = COMPS * MODES
STIFF = FIELDS + TERMS
ROWS = 4
LANES = 128
WIDE = 64


def multi_indices(count_left, budget_left):
    if count_left == 0:
        return [()]
    return [
        (leading,) + remainder
        for leading in range(budget_left + 1)
        for remainder in multi_indices(count_left - 1, budget_left - leading)
    ]


def chaos_terms():
    picked = sorted(
        multi_indices(VARS, DEG),
        key=lambda multi_index: (sum(multi_index),)
        + tuple((-entry_value for entry_value in multi_index)),
    )
    position = {multi_index: number for number, multi_index in enumerate(picked)}
    terms = [[] for mode in picked]
    for variable in range(VARS):
        for multi_index in picked:
            raised = list(multi_index)
            raised[variable] += 1
            raised = tuple(raised)
            if raised in position:
                degree = multi_index[variable]
                here, there = position[multi_index], position[raised]
                terms[here].append((variable, degree, there))
                terms[there].append((variable, degree, here))
    values = [(n + 1) / math.sqrt((2 * n + 1) * (2 * n + 3)) for n in range(DEG)]
    return terms, values


CHAOS, CHAOS_VALUES = chaos_terms()
TABLE = 1 + VARS * DEG


def tap_slots(y_in, y_out, reach):
    z = np.arange(CZ)
    y_in, z_in = np.repeat(y_in, CZ), np.tile(z, len(y_in))
    y_out, z_out = np.repeat(y_out, CZ), np.tile(z, len(y_out))
    dy = y_in[:, None] - y_out[None, :]
    dz = z_in[:, None] - z_out[None, :]
    near = (abs(dy) <= 1) & (abs(dz) <= 1) & np.repeat(np.repeat(reach, CZ, 0), CZ, 1)
    parts = []
    for dx in (0, 1, -1):
        linear = 9 * (dx + 1) + 3 * (dy + 1) + (dz + 1)
        slot = np.minimum(linear, 26 - linear)
        parts.append(np.where(near & (linear != 13), slot, 13))
    return np.concatenate(parts, axis=1).astype(np.int32)


def chunk_slots():
    y_in = np.array([0, 1, 2, 3, 4, 5, -2, -1])
    return tap_slots(y_in, np.arange(4), np.ones((8, 4), bool))


def rim_slots():
    far = 100
    y_in = np.array([16, 17, -2 - far, -1 - far, -far, 1 - far, 14, 15])
    y_out = np.array([15, 16, -1 - far, -far])
    reach = np.ones((8, 4), bool)
    reach[4:, 0] = False
    reach[4:, 3] = False
    return tap_slots(y_in, y_out, reach)


SLOTS = np.stack([chunk_slots(), rim_slots()])


def matrix_kernel(weights_ref, slots_ref, matrix_ref):
    slots = slots_ref[0]
    full = jnp.zeros(slots.shape, jnp.float32)
    for number in range(13):
        full = jnp.where(slots == number, 0.5 * weights_ref[number], full)
    high = full.astype(jnp.bfloat16)
    low = (full - high.astype(jnp.float32)).astype(jnp.bfloat16)
    rows = slots.shape[0]
    matrix_ref[0, :rows] = high
    matrix_ref[0, rows : 2 * rows] = high
    matrix_ref[0, 2 * rows :] = low


def mix(table, load, mode, total):
    for variable, degree, other in CHAOS[mode]:
        total = total + table[1 + variable * DEG + degree] * load(other)
    return total


PAIRS = ((0, 3), (1, 2))
OUTER, INNER = 0, 1


def tile_row():
    return lax.broadcasted_iota(jnp.int32, (8, LANES), 0)


def tile_lane():
    return lax.broadcasted_iota(jnp.int32, (8, LANES), 1)


def beside_outer(inner, lead, ahead=0.0, behind=0.0):
    left = tile_lane() < WIDE
    return jnp.where(left, jnp.where(lead, inner, ahead), jnp.where(lead, behind, inner))


def beside_inner(outer, inner, lead):
    left = tile_lane() < WIDE
    turned = pltpu.roll(inner, ROWS, 1)
    return jnp.where(left, jnp.where(lead, turned, outer), jnp.where(lead, outer, turned))


def halves(value):
    value = value.reshape(value.shape[0] * 8, LANES)
    high = value.astype(jnp.bfloat16)
    return high, (value - high.astype(jnp.float32)).astype(jnp.bfloat16)


def stencil(own, beside, matrix):
    (high, low), (near_high, near_low) = halves(own), halves(beside)
    lines = jnp.concatenate([high, near_high, low, near_low, high, near_high], axis=1)
    parts = jnp.dot(lines, matrix, preferred_element_type=jnp.float32)
    return [
        parts[:, at : at + LANES].reshape(own.shape) for at in range(0, parts.shape[1], LANES)
    ]


def turned_parts(parts):
    return pltpu.roll(parts[-2], 7, 1), pltpu.roll(parts[-1], 1, 1)


def same_rows(parts):
    ahead, behind = turned_parts(parts)
    row = tile_row() % ROWS
    return parts[0] + jnp.where(row == ROWS - 1, 0.0, ahead) + jnp.where(row == 0, 0.0, behind)


def other_rows(parts):
    ahead, behind = turned_parts(parts)
    row = tile_row() % ROWS
    return jnp.where(row == ROWS - 1, ahead, jnp.where(row == 0, behind, 0.0))


def entry_of(ref):
    return lambda number: ref[number]


def coef_values(field):
    values = [field(FIELDS + term) for term in range(TERMS)]
    return spread_values(values)


def spread_values(values):
    return [values[0]] + [
        values[1 + variable] * CHAOS_VALUES[degree]
        for variable in range(VARS)
        for degree in range(DEG)
    ]


def diag_values(field, near, weights_ref):
    weight_sum = sum(weights_ref[number] for number in range(13))
    return spread_values(
        [field(FIELDS + term) * weight_sum + near(FIELDS + term) for term in range(TERMS)]
    )


def grow(field, table, out):
    for comp in range(COMPS):
        base = comp * MODES
        for mode in range(MODES):
            load = lambda other: field(base + other)
            out[base + mode] = mix(table, load, mode, table[0] * load(mode))

    out[FIELDS] = jnp.zeros((8, LANES), jnp.float32)


def apply(field, near, grown_near, coef, diag, stiff, store, carry=0):
    def each(comp, carry):
        base = comp * MODES
        for mode in range(MODES):
            load = lambda other: field(base + other)
            close = lambda other: near(base + other)
            value = mix(diag, load, mode, (stiff + diag[0]) * load(mode))
            value = value - mix(
                coef, close, mode, coef[0] * close(mode) + grown_near(base + mode)
            )
            carry = store(base + mode, value, carry)
        return carry

    for comp in range(COMPS):
        carry = each(comp, carry)
    return carry


def masked_store(out, inside):
    def store(number, value, carry):
        out[number] = jnp.where(inside, value, 0.0)
        return carry

    return store


def second_store(start, image, out):
    def store(number, value, sums):
        rr, rq, qq, qz = sums
        first, here = start(number), image(number)
        out[number] = value
        return rr + first * first, rq + first * here, qq + here * here, qz + here * value

    return store


def second_near(own, own_beside, halo, halo_beside, matrix_ref):
    own_parts = stencil(own, own_beside, matrix_ref[0])
    halo_parts = stencil(halo, halo_beside, matrix_ref[0, :, LANES:])
    return same_rows(own_parts) + other_rows(halo_parts)


def start_kernel(
    own_ref, extra_ref, matrix_ref, pairs, grown, near, halo_near, grown_near, halo_grown_near
):
    for number, chunks in enumerate(PAIRS):
        for side, chunk in enumerate(chunks):
            lanes, rows = pl.ds(chunk * LANES, LANES), pl.ds(side * ROWS, ROWS)
            pairs[number, :FIELDS, rows, :] = own_ref[:, :, lanes]
            pairs[number, FIELDS : STIFF + 1, rows, :] = extra_ref[:, :, lanes]
        pairs[number, STIFF + 1] = jnp.zeros((8, LANES), jnp.float32)
        field = entry_of(pairs.at[number])
        grow(field, coef_values(field), grown.at[number])
    lead = tile_row() < ROWS
    for ref, out, halo_out in ((pairs, near, halo_near), (grown, grown_near, halo_grown_near)):
        outer, inner = ref[OUTER], ref[INNER]
        for number, own, beside in (
            (OUTER, outer, beside_outer(inner, lead)),
            (INNER, inner, beside_inner(outer, inner, lead)),
        ):
            parts = stencil(own, beside, matrix_ref[0])
            out[number] = same_rows(parts)
            halo_out[number] = other_rows(parts)


def join_kernel(flags_ref, one_ref, other_ref, pairs, beyond_ref, first_ref, second_ref, ends):
    even_down, even_cross = flags_ref[0] == 1, flags_ref[1] == 1
    upper = jnp.where(even_down, one_ref[...], other_ref[...])
    lower = jnp.where(even_down, other_ref[...], one_ref[...])
    fields = pl.ds(0, STIFF + 1)
    beyond_ref[fields, :2] = upper
    beyond_ref[fields, 2:] = lower
    beyond_ref[STIFF + 1] = jnp.zeros(beyond_ref.shape[1:], jnp.float32)
    for side, chunk in enumerate(PAIRS[OUTER]):
        ends[side, :, ROWS:] = beyond_ref[:, :, pl.ds(chunk * LANES, LANES)]
    top = tile_row() < ROWS
    outer = pairs[OUTER]
    ends[0] = jnp.where(top, outer, ends[0])
    ends[1] = jnp.where(top, pltpu.roll(outer, ROWS, 1), ends[1])
    half = first_ref.shape[0]
    left = tile_lane() < WIDE
    head = jnp.where(left, ends[0, :half], pltpu.roll(ends[0, half:], WIDE, 2))
    tail = jnp.where(left, pltpu.roll(ends[1, :half], WIDE, 2), ends[1, half:])
    first_ref[...] = jnp.where(even_cross, tail, head)
    second_ref[...] = jnp.where(even_cross, head, tail)


def inner_kernel(
    beyond_ref, pairs, matrix_ref, weights_ref,
    before_near, before_halo_near, before_grown_near, before_halo_grown_near,
    halo, halo_grown, near, halo_near, grown_near, halo_grown_near,
    image, halo_image, image_grown, halo_image_grown, diag, second_ref, sums_ref,
):
    for number, (first, second) in enumerate(PAIRS):
        halo[number, :, ROWS:, :] = beyond_ref[:, :, pl.ds(first * LANES, LANES)]
        halo[number, :, :ROWS, :] = beyond_ref[:, :, pl.ds(second * LANES, LANES)]
        field = entry_of(halo.at[number])
        grow(field, coef_values(field), halo_grown.at[number])
    lead = tile_row() >= ROWS
    for ref, before, before_halo, out, halo_out in (
        (halo, before_near, before_halo_near, near, halo_near),
        (halo_grown, before_grown_near, before_halo_grown_near, grown_near, halo_grown_near),
    ):
        outer, inner = ref[OUTER], ref[INNER]
        for number, own, beside in (
            (OUTER, outer, beside_outer(inner, lead)),
            (INNER, inner, beside_inner(outer, inner, lead)),
        ):
            parts = stencil(own, beside, matrix_ref[0])
            halo_out[number] = before_halo[number] + same_rows(parts)
            out[number] = before[number] + other_rows(parts)

    for ref, close, grown_close, out, out_grown in (
        (pairs, near, grown_near, image, image_grown),
        (halo, halo_near, halo_grown_near, halo_image, halo_image_grown),
    ):

        for number in range(len(PAIRS)):
            field, around = entry_of(ref.at[number]), entry_of(close.at[number])
            coef = coef_values(field)
            values = diag_values(field, around, weights_ref)
            if ref is pairs:
                for entry, value in enumerate(values):
                    diag[number, entry] = value
            stiff = field(STIFF)
            target = out.at[number]
            apply(
                field, around, entry_of(grown_close.at[number]), coef, values, stiff,
                masked_store(target, stiff > 0.0),
            )
            target[FIELDS] = jnp.zeros((8, LANES), jnp.float32)
            grow(entry_of(target), coef, out_grown.at[number])

    own_lead = tile_row() < ROWS
    image_near, image_grown_near = near.at[INNER, pl.ds(0, FIELDS + 1)], grown_near.at[INNER]
    for own, far, out in (
        (image, halo_image, image_near),
        (image_grown, halo_image_grown, image_grown_near),
    ):
        out[...] = second_near(
            own[INNER],
            beside_inner(own[OUTER], own[INNER], own_lead),
            far[INNER],
            beside_inner(far[OUTER], far[INNER], lead),
            matrix_ref,
        )
    field, here = entry_of(pairs.at[INNER]), entry_of(image.at[INNER])
    zero = jnp.zeros((8, LANES), jnp.float32)
    sums = apply(
        here, entry_of(image_near), entry_of(image_grown_near), coef_values(field),
        [diag[INNER, entry] for entry in range(TABLE)], field(STIFF),
        second_store(field, here, second_ref), (zero, zero, zero, zero),
    )
    for number, value in enumerate(sums):
        sums_ref[number] = value


def outer_kernel(
    flags_ref, one_ref, other_ref, pairs, halo, matrix_ref, weights_ref, own_grown, halo_grown,
    near, halo_near, grown_near, halo_grown_near,
    image, halo_image, image_grown, halo_image_grown, diag, before_ref,
    image_ref, second_ref, sums_ref,
    edge, rim, grown, rim_near, rim_grown_near, rim_image,
):
    lane, top = tile_lane(), tile_row() < ROWS
    bottom = ~top
    left = lane < WIDE

    def first_chunk(own, far):
        return jnp.where(top, own, far)

    def last_chunk(own, far):
        return pltpu.roll(jnp.where(top, far, own), ROWS, own.ndim - 2)

    def to_rim(last, beyond, begin):
        right = pltpu.roll(jnp.where(lane >= 3 * CZ, last, beyond), CZ, 2)
        return jnp.where(
            left, right, pltpu.roll(jnp.where(lane < CZ, begin, beyond), LANES - CZ, 2)
        )

    def rim_stencil(around, own, far, own_near, far_near):
        beside = jnp.where(left, first_chunk(own, far), last_chunk(own, far))
        parts = stencil(around, beside, matrix_ref[1])
        ahead, behind = turned_parts(parts)
        begin = first_chunk(own_near, far_near)
        last = last_chunk(own_near, far_near)
        return parts[0] + ahead + behind + to_rim(last, jnp.zeros_like(last), begin)

    even_cross = flags_ref[1] == 1
    right = jnp.where(even_cross, one_ref[...], other_ref[...])
    before = jnp.where(even_cross, other_ref[...], one_ref[...])
    half = one_ref.shape[0]
    edge[:half] = jnp.where(left, right, pltpu.roll(before, WIDE, 2))
    edge[half:] = jnp.where(left, pltpu.roll(right, WIDE, 2), before)
    field = entry_of(edge)
    grow(field, coef_values(field), grown)
    rim_near[...] = rim_stencil(
        edge[...], pairs[OUTER], halo[OUTER], near[OUTER], halo_near[OUTER]
    )
    rim_grown_near[...] = rim_stencil(
        grown[...], own_grown[OUTER], halo_grown[OUTER], grown_near[OUTER], halo_grown_near[OUTER]
    )
    rim[...] = to_rim(
        last_chunk(pairs[OUTER], halo[OUTER]), edge[...], first_chunk(pairs[OUTER], halo[OUTER])
    )
    field, around = entry_of(rim), entry_of(rim_near)
    coef, rim_diag = coef_values(field), diag_values(field, around, weights_ref)
    stiff = field(STIFF)
    apply(
        field, around, entry_of(rim_grown_near), coef, rim_diag, stiff,
        masked_store(rim_image, stiff > 0.0),
    )
    rim_image[FIELDS] = jnp.zeros((8, LANES), jnp.float32)
    grow(entry_of(rim_image), coef, grown)

    def from_rim(value):
        last = pltpu.roll(value, LANES - CZ, value.ndim - 1)
        return pltpu.roll(value, CZ, value.ndim - 1), pltpu.roll(last, ROWS, value.ndim - 2)

    def placed(lead, begin, last, value):
        value = jnp.where(lead & (lane < CZ), begin, value)
        return jnp.where(~lead & (lane >= 3 * CZ), last, value)

    image_near, image_grown_near = rim_near.at[pl.ds(0, FIELDS + 1)], rim_grown_near
    for value, own, far, out, keep in (
        (rim_image, image, halo_image, image_near, True),
        (grown, image_grown, halo_image_grown, image_grown_near, False),
    ):
        begin, last = from_rim(value[...])
        here = placed(top, begin, last, own[OUTER])
        if keep:
            image_ref[...] = here
        out[...] = second_near(
            here,
            beside_outer(own[INNER], top, last, begin),
            placed(bottom, begin, last, far[OUTER]),
            beside_outer(far[INNER], bottom, last, begin),
            matrix_ref,
        )
    values = []
    for entry in range(TABLE):
        begin, last = from_rim(rim_diag[entry])
        values.append(placed(top, begin, last, diag[OUTER, entry]))
    field, here = entry_of(pairs.at[OUTER]), entry_of(image_ref)
    sums = apply(
        here, entry_of(image_near), entry_of(image_grown_near), coef_values(field), values,
        field(STIFF), second_store(field, here, second_ref),
        tuple(before_ref[number] for number in range(4)),
    )
    column = lax.broadcasted_iota(jnp.int32, sums_ref.shape, 1)
    row = jnp.zeros(sums_ref.shape, jnp.float32)
    for number, value in enumerate(sums):
        row = jnp.where(column == number, jnp.sum(value), row)
    sums_ref[...] = row


FINISH_STEPS = 7


def finish_kernel(
    sums_ref, pairs, images, inner_second, outer_image, outer_second,
    field_out, residual_out, field_ref, residual_ref, sems,
):
    total = jnp.sum(sums_ref[...], axis=0, keepdims=True)
    lane = lax.broadcasted_iota(jnp.int32, total.shape, 1)
    rr, rq, qq, qz = [
        jnp.sum(jnp.where(lane == number, total, 0.0), axis=1, keepdims=True)[None]
        for number in range(4)
    ]
    step = rr / rq
    fresh = rr - 2.0 * step * rq + step * step * qq
    larger = 1.0 + fresh / rr
    curvature = larger * larger * rq - 2.0 * larger * step * qq + step * step * qz
    later = fresh / curvature
    both = step + later * larger
    cross = later * step
    count = FIELDS // FINISH_STEPS
    copies = []
    for at in range(FINISH_STEPS):
        here = pl.ds(at * count, count)
        for number, image_ref, second_ref in (
            (OUTER, outer_image, outer_second),
            (INNER, images.at[INNER], inner_second),
        ):
            start, image, second = pairs[number, here], image_ref[here], second_ref[here]
            field = both * start - cross * image
            residual = start - both * image + cross * second
            for side, chunk in enumerate(PAIRS[number]):
                lanes, rows = pl.ds(chunk * LANES, LANES), slice(side * ROWS, (side + 1) * ROWS)
                field_ref[here, :, lanes] = field[:, rows]
                residual_ref[here, :, lanes] = residual[:, rows]
        for number, (ref, out) in enumerate(((field_ref, field_out), (residual_ref, residual_out))):
            copy = pltpu.make_async_copy(ref.at[here], out.at[here], sems.at[at, number])
            copy.start()
            copies.append(copy)
    for copy in copies:
        copy.wait()


def swap(value, axis, begin):
    size = lax.axis_size(axis)
    pairs = [(i, i + 1) for i in range(begin, size - 1, 2)]
    return lax.ppermute(value, axis, pairs + [(j, i) for i, j in pairs])


def per_device(right_side, stiffness, coefficients, stencil_weights):
    columns = right_side.shape[3]
    devices = lax.axis_size("down") * lax.axis_size("cross")
    own = right_side.reshape(FIELDS, ROWS, columns)
    extra = jnp.concatenate([coefficients, stiffness[None]], axis=0)
    even = lax.axis_index("down") % 2 == 0
    flags = jnp.stack([even, lax.axis_index("cross") % 2 == 0]).astype(jnp.int32)

    def rows_for(lower, arrays):
        parts = [jnp.where(lower, x[:, ROWS - 2 :], x[:, :2]) for x in arrays]
        return jnp.concatenate(parts, axis=0)

    sent = rows_for(~even, (own, extra))
    other = swap(sent, "down", 1)
    here, there, _ = lax.optimization_barrier((own, extra, sent))
    one = swap(rows_for(even, (here, there)), "down", 0)
    vmem = pl.BlockSpec(memory_space=pltpu.VMEM)
    smem = pl.BlockSpec(memory_space=pltpu.SMEM)
    f32, bf16 = jnp.float32, jnp.bfloat16
    params = pltpu.CompilerParams(vmem_limit_bytes=32 * 1024 * 1024)
    matrices = pl.pallas_call(
        matrix_kernel,
        grid=(2,),
        out_shape=jax.ShapeDtypeStruct((2, 3 * SLOTS.shape[1], SLOTS.shape[2]), bf16),
        in_specs=[smem, pl.BlockSpec((1,) + SLOTS.shape[1:], lambda i: (i, 0, 0))],
        out_specs=pl.BlockSpec((1, 3 * SLOTS.shape[1], SLOTS.shape[2]), lambda i: (i, 0, 0)),
        name="matrix",
    )(stencil_weights, jnp.asarray(SLOTS))
    count, wider = FIELDS + 1, STIFF + 2
    one_of = lambda number: jax.ShapeDtypeStruct((number, 8, LANES), f32)
    pair_of = lambda number: jax.ShapeDtypeStruct((2, number, 8, LANES), f32)
    pairs, own_grown, *nears = pl.pallas_call(
        start_kernel,
        out_shape=(
            pair_of(wider), pair_of(count),
            pair_of(wider), pair_of(wider), pair_of(count), pair_of(count),
        ),
        in_specs=[vmem] * 3,
        out_specs=(vmem,) * 6,
        compiler_params=params,
        cost_estimate=pl.CostEstimate(flops=5 * 10**9, bytes_accessed=0, transcendentals=0),
        name="start",
    )(own, extra, matrices)
    half = jax.ShapeDtypeStruct((wider // 2, 8, LANES), f32)
    beyond, first, second = pl.pallas_call(
        join_kernel,
        out_shape=(jax.ShapeDtypeStruct((wider, ROWS, columns), f32), half, half),
        in_specs=[smem] + [vmem] * 3,
        out_specs=(vmem,) * 3,
        scratch_shapes=[pltpu.VMEM((2, wider, 8, LANES), f32)],
        compiler_params=params,
        name="join",
    )(flags, one, other, pairs)
    first, second = swap(first, "cross", 0), swap(second, "cross", 1)
    halo, halo_grown, *kept, inner_second, sums = pl.pallas_call(
        inner_kernel,
        out_shape=(
            pair_of(wider), pair_of(count),
            pair_of(wider), pair_of(wider), pair_of(count), pair_of(count),
            pair_of(count), pair_of(count), pair_of(count), pair_of(count),
            pair_of(TABLE), one_of(FIELDS), one_of(4),
        ),
        in_specs=[vmem] * 3 + [smem] + [vmem] * 4,
        out_specs=(vmem,) * 13,
        compiler_params=params,
        cost_estimate=pl.CostEstimate(flops=10**10, bytes_accessed=0, transcendentals=0),
        name="inner",
    )(beyond, pairs, matrices, stencil_weights, *nears)
    images = kept[4]
    outer_image, outer_second, sums = pl.pallas_call(
        outer_kernel,
        out_shape=(one_of(count), one_of(FIELDS), jax.ShapeDtypeStruct((devices, LANES), f32)),
        in_specs=[smem] + [vmem] * 5 + [smem] + [vmem] * 12,
        out_specs=(vmem,) * 3,
        scratch_shapes=[
            pltpu.VMEM((number, 8, LANES), f32)
            for number in (wider, wider, count, wider, count, count)
        ],
        compiler_params=params,
        name="outer",
    )(flags, first, second, pairs, halo, matrices, stencil_weights, own_grown, halo_grown, *kept, sums)
    sums = lax.all_to_all(sums, ("down", "cross"), 0, 0, tiled=True)
    anywhere = pl.BlockSpec(memory_space=pl.ANY)
    solution_field, residual = pl.pallas_call(
        finish_kernel,
        out_shape=(jax.ShapeDtypeStruct(own.shape, f32), jax.ShapeDtypeStruct(own.shape, f32)),
        in_specs=[vmem] * 6,
        out_specs=(anywhere, anywhere),
        scratch_shapes=[
            pltpu.VMEM(own.shape, f32),
            pltpu.VMEM(own.shape, f32),
            pltpu.SemaphoreType.DMA((FINISH_STEPS, 2)),
        ],
        compiler_params=params,
        name="finish",
    )(sums, pairs, images, inner_second, outer_image, outer_second)
    return solution_field.reshape(right_side.shape), residual.reshape(right_side.shape)


def solution(mesh):
    return jax.shard_map(
        per_device,
        mesh=mesh,
        in_specs=(
            P(None, None, "down", "cross"),
            P("down", "cross"),
            P(None, "down", "cross"),
            P(),
        ),
        out_specs=(P(None, None, "down", "cross"), P(None, None, "down", "cross")),
        check_vma=False,
    )
```
